32 devices in a mesh: dp: 8 (over z, x), fsdp: 4 (over y, core).
Axes of the slice: x: 2, y: 2, z: 4, core: 2. Of those that a mesh axis runs over, the one named last changes fastest.
Arguments:
- tokens: bfloat16 [32, 2048, 512], P(('dp', 'fsdp')), may hold values from -6 to 6
- cotangent: bfloat16 [32, 2048, 512], P(('dp', 'fsdp')), may hold values from -6 to 6
- known_genes: int32 [32, 2048], P(('dp', 'fsdp')), may hold values 0 or 1
- cell_kind: int32 [32], P(('dp', 'fsdp')), may hold values from 0 to 1, as said below
- gene_counts: int32 [32, 4], P(('dp', 'fsdp')), may hold values from 0 to 2048, as said below
- study_index: int32 [32, 4], P(('dp', 'fsdp')), may hold values from 0 to 7, as said below
- qkv_weight: float32 [512, 1536], P('fsdp'), may hold values from -0.25 to 0.25
- qkv_first: float32 [512, 1536], P('fsdp'), may hold values from -1536 to 1536
- qkv_second: float32 [512, 1536], P('fsdp'), may hold values from 65536 to 262144
- proj_weight: float32 [512, 512], P('fsdp'), may hold values from -6 to 6
- proj_first: float32 [512, 512], P('fsdp'), may hold values from -128 to 128
- proj_second: float32 [512, 512], P('fsdp'), may hold values from 512 to 2048
- up_weight: float32 [512, 512], P('fsdp'), may hold values from -0.25 to 0.25
- up_first: float32 [512, 512], P('fsdp'), may hold values from -1536 to 1536
- up_second: float32 [512, 512], P('fsdp'), may hold values from 65536 to 262144
- down_weight: float32 [512, 512], P('fsdp'), may hold values from -0.25 to 0.25
- down_first: float32 [512, 512], P('fsdp'), may hold values from -768 to 768
- down_second: float32 [512, 512], P('fsdp'), may hold values from 16384 to 65536
- norm_params: float32 [4, 512], P(None, 'fsdp'), may hold values from -0.5 to 1.4, as said below
- norm_first: float32 [4, 512], P(None, 'fsdp'), may hold values from -1536 to 1536
- norm_second: float32 [4, 512], P(None, 'fsdp'), may hold values from 65536 to 262144
Outputs:
- out: bfloat16 [32, 2048, 512], P(('dp', 'fsdp'))
- input_grad: bfloat16 [32, 2048, 512], P(('dp', 'fsdp'))
- study_mean: float32 [8, 512], replicated
- study_var: float32 [8, 512], replicated
- qkv_first_new: float32 [512, 1536], P('fsdp')
- qkv_second_new: float32 [512, 1536], P('fsdp')
- qkv_weight_new: float32 [512, 1536], P('fsdp')
- qkv_weight_copy: bfloat16 [512, 1536], P('fsdp')
- proj_first_new: float32 [512, 512], P('fsdp')
- proj_second_new: float32 [512, 512], P('fsdp')
- proj_weight_new: float32 [512, 512], P('fsdp')
- proj_weight_copy: bfloat16 [512, 512], P('fsdp')
- up_first_new: float32 [512, 512], P('fsdp')
- up_second_new: float32 [512, 512], P('fsdp')
- up_weight_new: float32 [512, 512], P('fsdp')
- up_weight_copy: bfloat16 [512, 512], P('fsdp')
- down_first_new: float32 [512, 512], P('fsdp')
- down_second_new: float32 [512, 512], P('fsdp')
- down_weight_new: float32 [512, 512], P('fsdp')
- down_weight_copy: bfloat16 [512, 512], P('fsdp')
- norm_first_new: float32 [4, 512], P(None, 'fsdp')
- norm_second_new: float32 [4, 512], P(None, 'fsdp')
- norm_params_new: float32 [4, 512], P(None, 'fsdp')
- norm_params_copy: bfloat16 [4, 512], P(None, 'fsdp')
- matrix_norms: float32 [3, 4], replicated
The draws below stay inside these ranges and needn't reach their ends.
Inputs may be any that keep to these rules, and one draw needn't show every extreme that they name: `cell_kind`: both kinds occur in every draw. `gene_counts`: slots 1 and up of a group with cell_kind 1 hold 0. A long cell has 1024 genes or more, some long cell exactly 2048; a short cell has 256 or more, some short cell exactly 512. `study_index`: every study has a used cell slot. `norm_params`: rows 0 and 2 are gains, rows 1 and 3 biases.
All inputs are finite; a program needn't handle non-finite values. No bound on the sum of `known_genes` on one device may be relied on, other than what follows from the above.
Results may differ from the reference program's by a relative error of at most 0.019.
Values may be sent and summed in bfloat16 or wider, within the bound.
No kernel may reach another device: no remote copies, remote signals or barrier semaphores. Data moves between devices by JAX's collectives and lax.ppermute only.
A program may use at most 256 MiB of HBM per device.

```python
import math
import jax
import jax.numpy as jnp
from jax import lax

D = 512
HEADS = 8
HDIM = 64
FF = 512
GROUP_LENGTH = 2048
SHORT_LENGTH = 512
STUDY_COUNT = 8
STEP = 5
CELL_GROUPS = 32


def cell_plan(key):
    group_index = jnp.arange(CELL_GROUPS, dtype=jnp.int32)
    kind_key, pick_key, long_key, short_key = jax.random.split(key, 4)
    kind_flag = (jax.random.randint(kind_key, (CELL_GROUPS,), 0, CELL_GROUPS) >= group_index).astype(jnp.int32)
    chosen = jax.random.randint(pick_key, (), 0, CELL_GROUPS // 2)
    kind_flag = jnp.where(group_index == chosen, 1, kind_flag)
    kind_flag = jnp.where(group_index == CELL_GROUPS - 1, 0, kind_flag)
    long_count = jax.random.randint(long_key, (CELL_GROUPS,), GROUP_LENGTH // 2, GROUP_LENGTH + 1)
    long_count = jnp.where(group_index == chosen, GROUP_LENGTH, long_count)
    slot_index = jnp.arange(GROUP_LENGTH // SHORT_LENGTH, dtype=jnp.int32)
    short_count = jax.random.randint(short_key, (CELL_GROUPS, GROUP_LENGTH // SHORT_LENGTH), SHORT_LENGTH // 2, SHORT_LENGTH + 1)
    short_count = jnp.where((group_index[:, None] == CELL_GROUPS - 1) & (slot_index[None, :] == 0), SHORT_LENGTH, short_count)
    gene_count = jnp.where(kind_flag[:, None] == 1, jnp.where(slot_index[None, :] == 0, long_count[:, None], 0), short_count)
    return (kind_flag.astype(jnp.int32), gene_count.astype(jnp.int32))


def draw_cell_kind(key, part):
    kind_flag, gene_count = cell_plan(key)
    return kind_flag


def draw_gene_counts(key, part):
    kind_flag, gene_count = cell_plan(key)
    return gene_count


def draw_study_index(key, part):
    key = jax.random.fold_in(key, 3)
    group_index = jnp.arange(CELL_GROUPS, dtype=jnp.int32)
    slot_index = jnp.arange(GROUP_LENGTH // SHORT_LENGTH, dtype=jnp.int32)
    study_label = jax.random.randint(key, (CELL_GROUPS, GROUP_LENGTH // SHORT_LENGTH), 0, STUDY_COUNT)
    forced_flag = (group_index[:, None] < STUDY_COUNT) & (slot_index[None, :] == 0)
    study_label = jnp.where(forced_flag, group_index[:, None] % STUDY_COUNT, study_label)
    return study_label.astype(jnp.int32)


def draw_norm_params(key, part):
    key = jax.random.fold_in(key, 5)
    gain_key, bias_key = jax.random.split(key)
    gains = jnp.clip(1.0 + 0.1 * jax.random.normal(gain_key, (2, D), jnp.float32), 0.6, 1.4)
    biases = jnp.clip(0.25 * jax.random.normal(bias_key, (2, D), jnp.float32), -0.5, 0.5)
    return jnp.stack([gains[0], biases[0], gains[1], biases[1]]).astype(jnp.float32)


def with_ends(array, stream_key, low, high):
    dims = array.shape
    place = [jax.random.randint(jax.random.fold_in(stream_key, axis), (), 0, dims[axis]) for axis in range(len(dims))]
    array = array.at[tuple(place)].set(low)
    longest = dims.index(max(dims))
    place[longest] = (place[longest] + 1) % dims[longest]
    return array.at[tuple(place)].set(high)


def block_levels(key, extent, cuts, smallest, high):
    def one(dim, shards_of):
        steps = jax.random.uniform(jax.random.fold_in(jax.random.fold_in(key, 6), dim), (shards_of,), jnp.float32, smallest / len(cuts), high / len(cuts))
        return jnp.repeat(jnp.exp(steps), extent[dim] // shards_of).reshape((-1,) + (1,) * (len(extent) - dim - 1))

    loudness = one(*cuts[0])
    for cut in cuts[1:]:
        loudness = loudness * one(*cut)
    return loudness


def scatter_about(own_key, shape, deviation, limit, cuts=(), kind=jnp.bfloat16):
    values = jax.random.normal(own_key, shape, jnp.float32) * deviation
    if len(cuts) > 0:
        values = block_levels(own_key, shape, cuts, -0.22, 0.18) * values
    return jnp.clip(values, min=-limit, max=limit).astype(kind)


def setup_inputs(seed: int = 0) -> dict:
    splits = jax.random.split(jax.random.key(seed), 22)
    tokens = scatter_about(splits[0], (CELL_GROUPS, GROUP_LENGTH, D), 1.0, 6.0, ((0, 32),))
    cotangent = scatter_about(splits[1], (CELL_GROUPS, GROUP_LENGTH, D), 1.0, 6.0, ((0, 32),))
    known_genes = with_ends((jax.random.randint(splits[2], (CELL_GROUPS, GROUP_LENGTH), 0, 2) < 1).astype(jnp.int32), jax.random.fold_in(splits[2], 1), 0, 1)
    cell_kind = draw_cell_kind(jax.random.fold_in(splits[21], 71), 0)
    gene_counts = draw_gene_counts(jax.random.fold_in(splits[21], 71), 0)
    study_index = draw_study_index(jax.random.fold_in(splits[21], 71), 0)
    qkv_weight = scatter_about(splits[6], (D, 3 * D), D ** -0.5, 0.25, ((0, 4),), jnp.float32)
    qkv_first = scatter_about(splits[7], (D, 3 * D), ((CELL_GROUPS * GROUP_LENGTH) ** 0.5), 1536.0, ((0, 4),), jnp.float32)
    qkv_second = jnp.clip(jnp.exp(math.log(262144.0) - 1.3862944 * jax.random.uniform(splits[8], (D, 3 * D), jnp.float32) ** block_levels(splits[8], (D, 3 * D), ((0, 4),), -0.2, 0.2)), 65536.0, 262144.0)
    proj_weight = scatter_about(splits[9], (D, D), (max(1, D * 4 // GROUP_LENGTH)) ** -0.5, 6.0, ((0, 4),), jnp.float32)
    proj_first = scatter_about(splits[10], (D, D), (2 * (CELL_GROUPS * GROUP_LENGTH // SHORT_LENGTH) ** 0.5), 128.0, ((0, 4),), jnp.float32)
    proj_second = jnp.clip(jnp.exp(math.log(2048.0) - 1.3862944 * jax.random.uniform(splits[11], (D, D), jnp.float32) ** block_levels(splits[11], (D, D), ((0, 4),), -0.2, 0.2)), 512.0, 2048.0)
    up_weight = scatter_about(splits[12], (D, FF), D ** -0.5, 0.25, ((0, 4),), jnp.float32)
    up_first = scatter_about(splits[13], (D, FF), ((CELL_GROUPS * GROUP_LENGTH) ** 0.5), 1536.0, ((0, 4),), jnp.float32)
    up_second = jnp.clip(jnp.exp(math.log(262144.0) - 1.3862944 * jax.random.uniform(splits[14], (D, FF), jnp.float32) ** block_levels(splits[14], (D, FF), ((0, 4),), -0.2, 0.2)), 65536.0, 262144.0)
    down_weight = scatter_about(splits[15], (FF, D), FF ** -0.5, 0.25, ((0, 4),), jnp.float32)
    down_first = scatter_about(splits[16], (FF, D), (0.5 * (CELL_GROUPS * GROUP_LENGTH) ** 0.5), 768.0, ((0, 4),), jnp.float32)
    down_second = jnp.clip(jnp.exp(math.log(65536.0) - 1.3862944 * jax.random.uniform(splits[17], (FF, D), jnp.float32) ** block_levels(splits[17], (FF, D), ((0, 4),), -0.2, 0.2)), 16384.0, 65536.0)
    norm_params = draw_norm_params(jax.random.fold_in(splits[21], 71), 0)
    norm_first = scatter_about(splits[19], (4, D), ((CELL_GROUPS * GROUP_LENGTH) ** 0.5), 1536.0, ((1, 4),), jnp.float32)
    norm_second = jnp.clip(jnp.exp(math.log(262144.0) - 1.3862944 * jax.random.uniform(splits[20], (4, D), jnp.float32) ** block_levels(splits[20], (4, D), ((1, 4),), -0.2, 0.2)), 65536.0, 262144.0)
    return {"tokens": tokens, "cotangent": cotangent, "known_genes": known_genes, "cell_kind": cell_kind, "gene_counts": gene_counts, "study_index": study_index, "qkv_weight": qkv_weight, "qkv_first": qkv_first, "qkv_second": qkv_second, "proj_weight": proj_weight, "proj_first": proj_first, "proj_second": proj_second, "up_weight": up_weight, "up_first": up_first, "up_second": up_second, "down_weight": down_weight, "down_first": down_first, "down_second": down_second, "norm_params": norm_params, "norm_first": norm_first, "norm_second": norm_second}


BETA = 0.5
ADAM_EPS = 1e-06
NORM_EPS = 1e-05
MATRIX_RATE = 0.5
VECTOR_RATE = 0.3
MATRIX_DECAY = 0.01
MASKED = -1000000000.0
HIGHEST_PREC = lax.Precision.HIGHEST

@jax.custom_vjp
def low(v):
    return lax.optimization_barrier(v.astype(jnp.bfloat16)).astype(jnp.float32)

@jax.custom_vjp
def low_back(v):
    return v

def low_keep(v):
    return (low(v), None)

def low_pass(kept, grad):
    return (grad,)

def back_keep(v):
    return (v, None)

def back_low(kept, grad):
    return (low(grad),)
low.defvjp(low_keep, low_pass)
low_back.defvjp(back_keep, back_low)

def layer_norm(inputs, gain_vec, bias_vec):
    row_mean = lax.optimization_barrier(jnp.mean(inputs, axis=-1, keepdims=True))
    centred = inputs - row_mean
    variance = lax.optimization_barrier(jnp.mean(centred * centred, axis=-1, keepdims=True))
    return centred * lax.rsqrt(variance + NORM_EPS) * gain_vec + bias_vec

def cell_layout(kind_flag, gene_count, known_flag):
    position = jnp.arange(known_flag.shape[0], dtype=jnp.int32)
    segment = position // SHORT_LENGTH
    cell_ids = jnp.where(kind_flag == 1, 0, segment).astype(jnp.int32)
    cell_start = jnp.where(kind_flag == 1, 0, segment * SHORT_LENGTH).astype(jnp.int32)
    slot_index = jnp.arange(gene_count.shape[0], dtype=jnp.int32)
    cell_limit = lax.optimization_barrier(jnp.sum(jnp.where(cell_ids[:, None] == slot_index[None, :], gene_count[None, :], 0), axis=1))
    key_ok = (position - cell_start < cell_limit) & ((known_flag == 1) | (position == cell_start))
    return (cell_ids, key_ok)

def group_forward(tokens_f, w_qkv, w_proj, w_up, w_down, norm_rows, cell_ids, key_ok):
    length = tokens_f.shape[0]
    block_rows = min(512, length)
    score_scale = HDIM ** (-0.5)
    qkv = low(low_back(jnp.dot(tokens_f, w_qkv, precision=HIGHEST_PREC)))
    queries = qkv[:, :D].reshape(length, HEADS, HDIM)
    keys = qkv[:, D:2 * D].reshape(length, HEADS, HDIM)
    values = qkv[:, 2 * D:].reshape(length, HEADS, HDIM)
    position = jnp.arange(length, dtype=jnp.int32)

    def one_block(begin_row):
        query_block = lax.dynamic_slice_in_dim(queries, begin_row, block_rows, 0)
        row_ids = lax.dynamic_slice_in_dim(position, begin_row, block_rows, 0)
        cell_block = lax.dynamic_slice_in_dim(cell_ids, begin_row, block_rows, 0)
        scores = low_back(jnp.einsum('bhd,khd->hbk', query_block, keys, precision=HIGHEST_PREC) * score_scale)
        allowed = (cell_block[:, None] == cell_ids[None, :]) & (key_ok[None, :] | (row_ids[:, None] == position[None, :]))
        scores = jnp.where(allowed[None], scores, MASKED)
        row_top = lax.optimization_barrier(jnp.max(scores, axis=-1, keepdims=True))
        raised = jnp.exp(scores - row_top)
        attn_probs = low(raised / lax.optimization_barrier(jnp.sum(raised, axis=-1, keepdims=True)))
        return jnp.einsum('hbk,khd->bhd', attn_probs, values, precision=HIGHEST_PREC).reshape(block_rows, D)
    begins = jnp.arange(length // block_rows, dtype=jnp.int32) * block_rows
    context = low(low_back(lax.map(jax.checkpoint(one_block), begins).reshape(length, D)))
    proj_out = low_back(jnp.dot(context, w_proj, precision=HIGHEST_PREC))
    middle = layer_norm(tokens_f + proj_out, norm_rows[0], norm_rows[1])
    hidden = low_back(jnp.dot(low(middle), w_up, precision=HIGHEST_PREC))
    active = low(jax.nn.gelu(hidden, approximate=False))
    branch = low_back(jnp.dot(active, w_down, precision=HIGHEST_PREC))
    return layer_norm(middle + branch, norm_rows[2], norm_rows[3])

def adam_terms(gradient, first_old, second_old):
    first_new = BETA * first_old + (1.0 - BETA) * gradient
    second_new = BETA * second_old + (1.0 - BETA) * gradient * gradient
    debias = 1.0 - BETA ** STEP
    update = first_new / debias / (jnp.sqrt(second_new / debias) + ADAM_EPS)
    return (first_new, second_new, update)

def reference(tokens, cotangent, known_genes, cell_kind, gene_counts, study_index, qkv_weight, qkv_first, qkv_second, proj_weight, proj_first, proj_second, up_weight, up_first, up_second, down_weight, down_first, down_second, norm_params, norm_first, norm_second):
    masters = (qkv_weight, proj_weight, up_weight, down_weight, norm_params)
    firsts_old = (qkv_first, proj_first, up_first, down_first, norm_first)
    seconds_old = (qkv_second, proj_second, up_second, down_second, norm_second)

    def one_group(running, group_item):
        group_tokens, group_cot, known_flag, kind_flag, gene_count = group_item
        cell_ids, key_ok = cell_layout(kind_flag, gene_count, known_flag)

        def forward(tokens_f, w_qkv, w_proj, w_up, w_down, norm_rows):
            return group_forward(tokens_f, low(w_qkv), low(w_proj), low(w_up), low(w_down), low(norm_rows), cell_ids, key_ok)
        result, pullback = jax.vjp(forward, group_tokens.astype(jnp.float32), *masters)
        pulled = pullback(group_cot.astype(jnp.float32))
        running = tuple((total_grad + new_grad for total_grad, new_grad in zip(running, pulled[1:])))
        return (running, (result.astype(jnp.bfloat16), pulled[0].astype(jnp.bfloat16)))
    zero_grads = tuple((jnp.zeros_like(weight) for weight in masters))
    totals, (out, input_grad) = lax.scan(one_group, zero_grads, (tokens, cotangent, known_genes, cell_kind, gene_counts))
    first_cells = out.reshape(out.shape[0], -1, SHORT_LENGTH, D)[:, :, 0, :].astype(jnp.float32)
    slot_index = jnp.arange(first_cells.shape[1], dtype=jnp.int32)
    used_slots = (cell_kind[:, None] == 0) | (slot_index[None, :] == 0)
    member_cell = ((study_index[:, :, None] == jnp.arange(STUDY_COUNT, dtype=jnp.int32)[None, None, :]) & used_slots[:, :, None]).astype(jnp.float32)
    study_counts = lax.optimization_barrier(jnp.sum(member_cell, axis=(0, 1)))
    study_sums = jnp.einsum('gcs,gcd->sd', member_cell, first_cells, precision=HIGHEST_PREC)
    study_squares = jnp.einsum('gcs,gcd->sd', member_cell, first_cells * first_cells, precision=HIGHEST_PREC)
    study_mean = study_sums / study_counts[:, None]
    study_var = study_squares / study_counts[:, None] - study_mean * study_mean
    results = []
    weight_norms = []
    update_norms = []
    ratios = []
    for index in range(5):
        first_new, second_new, update = adam_terms(totals[index], firsts_old[index], seconds_old[index])
        if index < 4:
            update = update + MATRIX_DECAY * masters[index]
            weight_norm = jnp.sqrt(jnp.sum(masters[index] * masters[index]))
            update_norm = jnp.sqrt(jnp.sum(update * update))
            ratio = weight_norm / update_norm
            new_weight = masters[index] - MATRIX_RATE * ratio * update
            weight_norms.append(weight_norm)
            update_norms.append(update_norm)
            ratios.append(ratio)
        else:
            new_weight = masters[index] - VECTOR_RATE * update
        results.extend([first_new, second_new, new_weight, new_weight.astype(jnp.bfloat16)])
    matrix_norms = jnp.stack([jnp.stack(weight_norms), jnp.stack(update_norms), jnp.stack(ratios)])
    return (out, input_grad, study_mean, study_var, results[0], results[1], results[2], results[3], results[4], results[5], results[6], results[7], results[8], results[9], results[10], results[11], results[12], results[13], results[14], results[15], results[16], results[17], results[18], results[19], matrix_norms)
```

```python
from functools import partial

import jax
import jax.numpy as jnp
from jax import lax
from jax.experimental import pallas as pl
from jax.experimental.pallas import tpu as pltpu
from jax.sharding import PartitionSpec as P

HEADS = 8
HDIM = 64
SHORT_LENGTH = 512
STUDY_COUNT = 8
STEP = 5
PAIR = 2 * HDIM
PAIRS = HEADS // 2
KEY_BLOCK = 256
TAIL = 128


BETA = 0.5
ADAM_EPS = 1e-06
NORM_EPS = 1e-05
MATRIX_RATE = 0.5
VECTOR_RATE = 0.3
MATRIX_DECAY = 0.01
MASKED = -1000000000.0
SAFE_SCORE = 40.0

BF = jnp.bfloat16
F32 = jnp.float32
NN = (((1,), (0,)), ((), ()))
NT = (((1,), (1,)), ((), ()))
TN = (((0,), (0,)), ((), ()))
SMEM = pl.BlockSpec(memory_space=pltpu.SMEM)
ANY = pl.BlockSpec(memory_space=pl.ANY)
VMEM_LIMIT = 60 * 2**20


def mm(left, right, dims):
    return lax.dot_general(left, right, dims, preferred_element_type=F32)


def whole(*shape):
    return pl.BlockSpec(shape, lambda *_: (0,) * len(shape))


def params():
    return pltpu.CompilerParams(vmem_limit_bytes=VMEM_LIMIT)


def cost(flops, nbytes, trans=0):
    return pl.CostEstimate(flops=int(flops), bytes_accessed=int(nbytes), transcendentals=int(trans))


def iota(shape, dim):
    return lax.broadcasted_iota(jnp.int32, shape, dim)


def prep_kernel(kind, counts, known, tokens, cot, tokens_t, cot_t, packed, slot, meta):
    cells = known.shape[1] // SHORT_LENGTH if known.shape[0] == 1 else 4
    length = tokens.shape[0]
    is_long = kind[0] == 1
    row = iota(known.shape, 0)
    col = iota(known.shape, 1)
    limit = jnp.zeros(known.shape, jnp.int32)
    for cell in range(cells):
        limit = jnp.where(row == cell, counts[cell], limit)
    limit = jnp.where(is_long, counts[0] - SHORT_LENGTH * row, limit)
    first = (col == 0) & (jnp.logical_not(is_long) | (row == 0))
    usable = (col < limit) & ((known[...] == 1) | first) & (row < cells)
    usable_f = jnp.where(usable, 1.0, 0.0)
    square = (SHORT_LENGTH, SHORT_LENGTH)
    before = jnp.where(iota(square, 0) < iota(square, 1), 1.0, 0.0).astype(BF)
    rank = mm(usable_f.astype(BF), before, NN).astype(jnp.int32)
    totals = [jnp.sum(usable_f[cell : cell + 1, :]).astype(jnp.int32) for cell in range(cells)]
    base = jnp.zeros(known.shape, jnp.int32)
    running = jnp.int32(0)
    for cell in range(cells):
        start = jnp.where(is_long, running, SHORT_LENGTH * cell)
        base = jnp.where(row == cell, start, base)
        running = running + totals[cell]
    place = jnp.where(usable, rank + base, -1)
    for cell in range(cells):
        slot[0:1, pl.ds(cell * SHORT_LENGTH, SHORT_LENGTH)] = place[cell : cell + 1, :]
    meta[0] = kind[0]
    for cell in range(cells):
        meta[1 + cell] = jnp.where(is_long, running if cell == 0 else 0, totals[cell])

    for block in range(length // KEY_BLOCK):
        rows = pl.ds(block * KEY_BLOCK, KEY_BLOCK)
        tokens_t[:, rows] = tokens[rows, :].T
        cot_t[:, rows] = cot[rows, :].T
        cell = block * KEY_BLOCK // SHORT_LENGTH
        inside = block * KEY_BLOCK - cell * SHORT_LENGTH
        needed = jnp.where(is_long, block * KEY_BLOCK < running, inside < totals[cell])

        @pl.when(needed)
        def _(block=block, rows=rows):
            hot = one_hot(slot, block * KEY_BLOCK, KEY_BLOCK)
            packed[rows, :] = mm(hot, tokens[...], NN).astype(BF)


def one_hot(slot, begin, rows):
    shape = (rows, slot.shape[1])
    hit = (iota(shape, 0) + begin) == slot[0:1, :]
    return jnp.where(hit, 1.0, 0.0).astype(BF)


def prep(kind, counts, known, tokens, cot):
    length, width = tokens.shape
    cells = length // SHORT_LENGTH
    known = jnp.pad(known.reshape(cells, SHORT_LENGTH), ((0, 8 - cells), (0, 0)))
    return pl.pallas_call(
        prep_kernel,
        in_specs=[SMEM, SMEM, whole(8, SHORT_LENGTH), whole(length, width), whole(length, width)],
        out_specs=[
            whole(width, length),
            whole(width, length),
            whole(length, width),
            whole(1, length),
            SMEM,
        ],
        out_shape=[
            jax.ShapeDtypeStruct((width, length), BF),
            jax.ShapeDtypeStruct((width, length), BF),
            jax.ShapeDtypeStruct((length, width), BF),
            jax.ShapeDtypeStruct((1, length), jnp.int32),
            jax.ShapeDtypeStruct((8,), jnp.int32),
        ],
        compiler_params=params(),
        cost_estimate=cost(3e9, 12e6),
        name="prep",
    )(kind, counts, known, tokens, cot)


def fetch_rows(pieces, mine, target, sem):
    rows = pieces[0].shape[0]
    copies = []
    for index, piece in enumerate(pieces):
        owner = jnp.bitwise_xor(mine, index)
        place = target.at[pl.ds(pl.multiple_of(owner * rows, rows), rows), :]
        copies.append(pltpu.make_async_copy(piece, place, sem.at[index]))
    for copy in copies:
        copy.start()
    for copy in copies:
        copy.wait()


def head_lanes(shape, head):
    lane = iota(shape, 1)
    return (lane >= HDIM * head) & (lane < HDIM * (head + 1))


def spare(head):
    return HDIM * (1 - head)


def key_side(block, head, begin, count):
    lane = iota(block.shape, 1) - spare(head)
    row = iota(block.shape, 0) + begin
    bias = jnp.where(row < count, 0.0, MASKED)
    extra = jnp.where(lane == 0, bias, jnp.where((lane > 0) & (lane < 4), 1.0, 0.0))
    return jnp.where(head_lanes(block.shape, head), block.astype(F32), extra).astype(BF)


def value_side(block, head):
    lane = iota(block.shape, 1) - spare(head)
    extra = jnp.where((lane > 0) & (lane < 4), 1.0, 0.0)
    return jnp.where(head_lanes(block.shape, head), block.astype(F32), extra).astype(BF)


def split_rows(shift):
    high = shift.astype(BF).astype(F32)
    rest = shift - high
    mid = rest.astype(BF).astype(F32)
    low = rest - mid
    shape = (16, shift.shape[1])
    row = iota(shape, 0)
    out = jnp.where(row == 0, 1.0, 0.0)
    out = jnp.where(row == 1, -high, out)
    out = jnp.where(row == 2, -mid, out)
    return jnp.where(row == 3, -low, out).astype(BF)


def query_side(target, head, rows, shift):
    other = spare(head)
    target[head, HDIM * head : HDIM * (head + 1), :] = rows
    target[head, other : other + 16, :] = split_rows(shift)
    target[head, other + 16 : other + HDIM, :] = jnp.zeros((HDIM - 16, rows.shape[1]), BF)


def walk(meta, length, body):
    @pl.when(meta[0] == 1)
    def _():
        cell_walk(meta[1], 0, 0, length, body)

    @pl.when(meta[0] != 1)
    def _():
        for cell in range(length // SHORT_LENGTH):
            cell_walk(meta[1 + cell], cell * SHORT_LENGTH, cell * SHORT_LENGTH, SHORT_LENGTH, body)


def cell_walk(count, slot_begin, query_begin, queries, body):
    rest = lax.rem(count, KEY_BLOCK)
    tail = (rest > 0) & (rest <= TAIL)
    full = count // KEY_BLOCK + jnp.where(rest > TAIL, 1, 0)
    end = slot_begin + count

    @pl.loop(0, full)
    def _(index):
        begin = pl.multiple_of(slot_begin + index * KEY_BLOCK, KEY_BLOCK)
        body(begin, KEY_BLOCK, query_begin, queries, end)

    @pl.when(tail)
    def _():
        begin = pl.multiple_of(slot_begin + full * KEY_BLOCK, KEY_BLOCK)
        body(begin, TAIL, query_begin, queries, end)


def forward_kernel(count, mine, meta, *refs):
    pieces = refs[:count]
    tokens_t, packed, slot = refs[count : count + 3]
    q_out, k_out, v_out, kc_out, vc_out, kct_out, context, log_total = refs[count + 3 : count + 11]
    weights, vct, side, total, shift, sem = refs[count + 11 :]
    step = pl.program_id(0)
    length = tokens_t.shape[1]

    @pl.when(step == 0)
    def _():
        fetch_rows(pieces, mine[0], weights, sem)

    columns = pl.ds(pl.multiple_of(step * 3 * PAIR, 3 * PAIR), 3 * PAIR)
    part = weights[:, columns]
    joined = mm(part, tokens_t[...], TN)
    q_out[...] = (joined[:PAIR] * HDIM**-0.5).astype(BF)
    k_out[...] = joined[PAIR : 2 * PAIR].astype(BF)
    v_out[...] = joined[2 * PAIR :].astype(BF)

    def project(begin, rows, *_):
        place = pl.ds(begin, rows)
        both = mm(packed[place, :], part[:, PAIR:], NN).astype(BF)
        kc_out[place, :] = both[:, :PAIR]
        vc_out[place, :] = both[:, PAIR:]
        kct_out[:, place] = both[:, :PAIR].T
        turned = both[:, PAIR:].T
        ones = jnp.where(iota((16, rows), 0) == 0, 1.0, 0.0).astype(BF)
        for head in range(2):
            vct[head, :HDIM, place] = turned[HDIM * head : HDIM * (head + 1)]
            vct[head, HDIM:, place] = ones

    walk(meta, length, project)

    masked = slot[...] < 0
    own = []
    for head in range(2):
        rows = slice(HDIM * head, HDIM * (head + 1))
        queries = q_out[rows, :].astype(F32)
        keys = k_out[rows, :].astype(F32)
        own.append(jnp.where(masked, jnp.sum(queries * keys, axis=0, keepdims=True), MASKED))
        top_q = jnp.max(jnp.sum(queries * queries, axis=0, keepdims=True))
        top_k = jnp.max(jnp.sum(keys * keys, axis=0, keepdims=True))
        unsafe = jnp.logical_not(top_q * top_k < SAFE_SCORE * SAFE_SCORE)
        shift[head : head + 1, :] = jnp.zeros((1, length), F32)
        query_side(side, head, q_out[rows, :], jnp.zeros((1, length), F32))

        @pl.when(unsafe)
        def _(head=head, rows=rows):
            shift[head : head + 1, :] = own[head]

            def raise_top(begin, rows, first, queries, end):
                keys = key_side(kc_out[pl.ds(begin, rows), :], head, begin, end)
                place = pl.ds(first, queries)
                scores = mm(keys, side[head, :, place], NN)
                top = jnp.max(scores, axis=0, keepdims=True)
                shift[head : head + 1, place] = jnp.maximum(shift[head : head + 1, place], top)

            walk(meta, length, raise_top)
            query_side(side, head, q_out[rows, :], shift[head : head + 1, :])

    total[...] = jnp.zeros(total.shape, F32)

    def attend(begin, rows, first, queries, end):
        slots = pl.ds(begin, rows)
        place = pl.ds(first, queries)
        for head in range(2):
            keys = key_side(kc_out[slots, :], head, begin, end)
            raised = jnp.exp(mm(keys, side[head, :, place], NN)).astype(BF)
            total[head, :, place] += mm(vct[head, :, slots], raised, NN)

    walk(meta, length, attend)

    for head in range(2):
        rows = slice(HDIM * head, HDIM * (head + 1))
        alone = jnp.exp(own[head] - shift[head : head + 1, :])
        row_total = total[head, HDIM : HDIM + 1, :] + alone
        gathered = total[head, :HDIM, :] + v_out[rows, :].astype(F32) * alone
        context[rows, :] = (gathered / row_total).astype(BF)
        log_total[pl.ds(step * 2 + head, 1), :] = shift[head : head + 1, :] + jnp.log(row_total)


def forward(mine, meta, pieces, tokens_t, packed, slot):
    width, length = tokens_t.shape
    pair_rows = pl.BlockSpec((PAIR, length), lambda step: (step, 0))
    pair_lanes = pl.BlockSpec((length, PAIR), lambda step: (0, step))
    transposed = jax.ShapeDtypeStruct((width, length), BF)
    natural = jax.ShapeDtypeStruct((length, width), BF)
    count = len(pieces)
    return pl.pallas_call(
        partial(forward_kernel, count),
        grid=(PAIRS,),
        in_specs=[SMEM, SMEM]
        + [ANY] * count
        + [whole(width, length), whole(length, width), whole(1, length)],
        out_specs=[pair_rows] * 3 + [pair_lanes] * 2 + [pair_rows] * 2 + [whole(HEADS, length)],
        out_shape=[transposed] * 3
        + [natural] * 2
        + [transposed] * 2
        + [jax.ShapeDtypeStruct((HEADS, length), F32)],
        scratch_shapes=[
            pltpu.VMEM((width, 3 * width), BF),
            pltpu.VMEM((2, HDIM + 16, length), BF),
            pltpu.VMEM((2, PAIR, length), BF),
            pltpu.VMEM((2, HDIM + 16, length), F32),
            pltpu.VMEM((8, length), F32),
            pltpu.SemaphoreType.DMA((count,)),
        ],
        compiler_params=params(),
        cost_estimate=cost(15e9, 25e6, 20e6),
        name="attend_forward",
    )(mine, meta, *pieces, tokens_t, packed, slot)


def backward_kernel(pair, meta, *refs):
    q_t, k_t, v_t, kc, vc, kct, grad_context, log_total, inner, slot, tokens_t = refs[:11]
    grad_t, grad_weight = refs[11:13]
    q_side, g_side, grad_q, grad_kv, ready = refs[13:]
    length = tokens_t.shape[1]
    for head in range(2):
        rows = slice(HDIM * head, HDIM * (head + 1))
        index = 2 * pair + head
        query_side(q_side, head, q_t[rows, :], log_total[index : index + 1, :])
        query_side(g_side, head, grad_context[rows, :], inner[index : index + 1, :])
    grad_q[...] = jnp.zeros(grad_q.shape, F32)
    grad_kv[...] = jnp.zeros(grad_kv.shape, F32)

    def pull(begin, rows, first, queries, end):
        slots = pl.ds(begin, rows)
        place = pl.ds(first, queries)
        for head in range(2):
            lanes = slice(HDIM * head, HDIM * (head + 1))
            keys = key_side(kc[slots, :], head, begin, end)
            values = value_side(vc[slots, :], head)
            probs = jnp.exp(mm(keys, q_side[head, :, place], NN))
            grad_scores = (probs * mm(values, g_side[head, :, place], NN)).astype(BF)
            grad_q[lanes, place] += mm(kct[lanes, slots], grad_scores, NN)
            ready[HDIM * head : HDIM * (head + 1), :rows] = mm(
                q_t[lanes, place], grad_scores, NT
            ).astype(BF)
            ready[PAIR + HDIM * head : PAIR + HDIM * (head + 1), :rows] = mm(
                grad_context[lanes, place], probs.astype(BF), NT
            ).astype(BF)
        hit = (iota((rows, queries), 0) + begin) == slot[0:1, place]
        spread = jnp.where(hit, 1.0, 0.0).astype(BF)
        grad_kv[:, place] += mm(ready[:, :rows], spread, NN)

    walk(meta, length, pull)

    masked = slot[...] < 0
    for head in range(2):
        rows = slice(HDIM * head, HDIM * (head + 1))
        index = 2 * pair + head
        queries = q_t[rows, :].astype(F32)
        keys = k_t[rows, :].astype(F32)
        values = v_t[rows, :].astype(F32)
        grads = grad_context[rows, :].astype(F32)
        own = jnp.sum(queries * keys, axis=0, keepdims=True)
        own = jnp.where(masked, own - log_total[index : index + 1, :], MASKED)
        alone = jnp.exp(own)
        pulled = jnp.sum(grads * values, axis=0, keepdims=True) - inner[index : index + 1, :]
        pulled = (alone * pulled).astype(BF).astype(F32)
        alone = alone.astype(BF).astype(F32)
        part = (grad_q[rows, :] + keys * pulled) * HDIM**-0.5
        grad_t[HDIM * head : HDIM * (head + 1), :] = part.astype(BF)
        part = grad_kv[rows, :] + queries * pulled
        grad_t[PAIR + HDIM * head : PAIR + HDIM * (head + 1), :] = part.astype(BF)
        part = grad_kv[PAIR + HDIM * head : PAIR + HDIM * (head + 1), :] + grads * alone
        grad_t[2 * PAIR + HDIM * head : 2 * PAIR + HDIM * (head + 1), :] = part.astype(BF)
    grad_weight[...] = mm(tokens_t[...], grad_t[...], NT).astype(BF)


def backward(pair, meta, q_t, k_t, v_t, kc, vc, kct, grad_context, log_total, inner, slot, tokens_t):
    width, length = tokens_t.shape
    pair_rows = pl.BlockSpec((PAIR, length), lambda step: (pair, 0))
    pair_lanes = pl.BlockSpec((length, PAIR), lambda step: (0, pair))
    return pl.pallas_call(
        partial(backward_kernel, pair),
        grid=(1,),
        in_specs=[SMEM]
        + [pair_rows] * 3
        + [pair_lanes] * 2
        + [pair_rows] * 2
        + [whole(HEADS, length)] * 2
        + [whole(1, length), whole(width, length)],
        out_specs=[whole(3 * PAIR, length), whole(width, 3 * PAIR)],
        out_shape=[
            jax.ShapeDtypeStruct((3 * PAIR, length), BF),
            jax.ShapeDtypeStruct((width, 3 * PAIR), BF),
        ],
        scratch_shapes=[
            pltpu.VMEM((2, PAIR, length), BF),
            pltpu.VMEM((2, PAIR, length), BF),
            pltpu.VMEM((PAIR, length), F32),
            pltpu.VMEM((2 * PAIR, length), F32),
            pltpu.VMEM((2 * PAIR, KEY_BLOCK), BF),
        ],
        compiler_params=params(),
        cost_estimate=cost(12e9, 10e6, 6e6),
        name=f"attend_backward_{pair}",
    )(meta, q_t, k_t, v_t, kc, vc, kct, grad_context, log_total, inner, slot, tokens_t)


def feature_mean(values):
    return jnp.sum(values, axis=0, keepdims=True) * (1.0 / values.shape[0])


def normalise(values):
    centred = values - feature_mean(values)
    scale = lax.rsqrt(feature_mean(centred * centred) + NORM_EPS)
    return centred * scale, scale


def pull_norm(grad, scaled, scale, gain):
    lifted = grad * gain
    return scale * (lifted - feature_mean(lifted) - scaled * feature_mean(lifted * scaled))


def lane_sums(values):
    width = 128
    out = values[:, :width]
    for begin in range(width, values.shape[1], width):
        out = out + values[:, begin : begin + width]
    return out


def dense_kernel(count, mine, *refs):
    pieces = refs[:count]
    tokens_t, context, cot_t = refs[count : count + 3]
    out, grad_context, grad_first, inner, g_proj, g_up, g_down, g_norm = refs[count + 3 : count + 11]
    weights, total, norm_total, sem = refs[count + 11 :]
    step = pl.program_id(0)
    width = tokens_t.shape[0]

    @pl.when(step == 0)
    def _():
        fetch_rows(pieces, mine[0], weights, sem)
        total[...] = jnp.zeros(total.shape, F32)
        norm_total[...] = jnp.zeros(norm_total.shape, F32)

    proj = weights[:, :width]
    up = weights[:, width : 2 * width]
    down = weights[:, 2 * width : 3 * width]
    rows = weights[:, 3 * width :].astype(F32)
    gain1, bias1, gain2, bias2 = (rows[:, index : index + 1] for index in range(4))

    context_low = context[...]
    scaled1, scale1 = normalise(tokens_t[...].astype(F32) + mm(proj, context_low, TN))
    middle = scaled1 * gain1 + bias1
    middle_low = middle.astype(BF)
    hidden = mm(up, middle_low, TN)
    cdf = 0.5 * (1.0 + lax.erf(hidden * 2.0**-0.5))
    slope = cdf + hidden * jnp.exp(hidden * hidden * -0.5) * 0.3989422804014327
    active = (hidden * cdf).astype(BF)
    scaled2, scale2 = normalise(middle + mm(down, active, TN))
    out[...] = (scaled2 * gain2 + bias2).astype(BF).T

    cot = cot_t[...].astype(F32)
    norm_total[2] += lane_sums(cot * scaled2)
    norm_total[3] += lane_sums(cot)
    grad_second = pull_norm(cot, scaled2, scale2, gain2)
    grad_low = grad_second.astype(BF)
    total[2] += mm(active, grad_low, NT)
    grad_hidden = (mm(down, grad_low, NN) * slope).astype(BF)
    total[1] += mm(middle_low, grad_hidden, NT)
    grad_middle = grad_second + mm(up, grad_hidden, NN)
    norm_total[0] += lane_sums(grad_middle * scaled1)
    norm_total[1] += lane_sums(grad_middle)
    grad_h1 = pull_norm(grad_middle, scaled1, scale1, gain1)
    grad_first[...] = grad_h1
    proj_low = grad_h1.astype(BF)
    total[0] += mm(context_low, proj_low, NT)
    pulled = mm(proj, proj_low, NN).astype(BF)
    grad_context[...] = pulled
    both = pulled.astype(F32) * context_low.astype(F32)
    for head in range(HEADS):
        part = both[HDIM * head : HDIM * (head + 1), :]
        inner[head : head + 1, :] = jnp.sum(part, axis=0, keepdims=True)

    @pl.when(step == pl.num_programs(0) - 1)
    def _():
        g_proj[...] = total[0].astype(BF)
        g_up[...] = total[1].astype(BF)
        g_down[...] = total[2].astype(BF)
        lane = iota((width, 128), 1)
        packed = jnp.zeros((width, 128), F32)
        for index in range(4):
            column = jnp.sum(norm_total[index], axis=1, keepdims=True)
            packed = jnp.where(lane == index, column, packed)
        g_norm[...] = packed


def dense(mine, pieces, tokens_t, context, cot_t):
    width, length = tokens_t.shape
    block = 512
    count = len(pieces)
    columns = pl.BlockSpec((width, block), lambda step: (0, step))
    square = jax.ShapeDtypeStruct((width, width), BF)
    return pl.pallas_call(
        partial(dense_kernel, count),
        grid=(length // block,),
        in_specs=[SMEM] + [ANY] * count + [columns] * 3,
        out_specs=[
            pl.BlockSpec((block, width), lambda step: (step, 0)),
            columns,
            columns,
            pl.BlockSpec((HEADS, block), lambda step: (0, step)),
        ]
        + [whole(width, width)] * 3
        + [whole(width, 128)],
        out_shape=[
            jax.ShapeDtypeStruct((length, width), BF),
            jax.ShapeDtypeStruct((width, length), BF),
            jax.ShapeDtypeStruct((width, length), F32),
            jax.ShapeDtypeStruct((HEADS, length), F32),
        ]
        + [square] * 3
        + [jax.ShapeDtypeStruct((width, 128), F32)],
        scratch_shapes=[
            pltpu.VMEM((width, 3 * width + 128), BF),
            pltpu.VMEM((3, width, width), F32),
            pltpu.VMEM((4, width, 128), F32),
            pltpu.SemaphoreType.DMA((count,)),
        ],
        compiler_params=params(),
        cost_estimate=cost(10e9, 20e6, 4e6),
        name="dense",
    )(mine, *pieces, tokens_t, context, cot_t)


def input_kernel(count, mine, *refs):
    pieces = refs[:count]
    grads = refs[count : count + PAIRS]
    grad_first, out = refs[count + PAIRS : count + PAIRS + 2]
    weights, sem = refs[count + PAIRS + 2 :]

    @pl.when(pl.program_id(0) == 0)
    def _():
        fetch_rows(pieces, mine[0], weights, sem)

    total = grad_first[...]
    for pair in range(PAIRS):
        total = total + mm(weights[:, 3 * PAIR * pair : 3 * PAIR * (pair + 1)], grads[pair][...], NN)
    out[...] = total.astype(BF).T


def input_side(mine, pieces, grads, grad_first):
    width, length = grad_first.shape
    block = 512
    count = len(pieces)
    return pl.pallas_call(
        partial(input_kernel, count),
        grid=(length // block,),
        in_specs=[SMEM]
        + [ANY] * count
        + [pl.BlockSpec((3 * PAIR, block), lambda step: (0, step))] * PAIRS
        + [pl.BlockSpec((width, block), lambda step: (0, step))],
        out_specs=pl.BlockSpec((block, width), lambda step: (step, 0)),
        out_shape=jax.ShapeDtypeStruct((length, width), BF),
        scratch_shapes=[pltpu.VMEM((width, 3 * width), BF), pltpu.SemaphoreType.DMA((count,))],
        compiler_params=params(),
        cost_estimate=cost(3.3e9, 14e6),
        name="input_side",
    )(mine, *pieces, *grads, grad_first)


def swap(value, axis, size, mask):
    return lax.ppermute(value, axis, [(index, index ^ mask) for index in range(size)])


def masks_of(size):
    return [1 << bit for bit in range(size.bit_length() - 1)]


def gather_pieces(piece, axis, size):
    pieces = {0: piece}
    for mask in reversed(masks_of(size)):
        for known in list(pieces):
            pieces[known ^ mask] = swap(pieces[known], axis, size, mask)
    return [pieces[index] for index in range(size)]


def halve(value, axis, size, mask, index):
    keep = lax.dynamic_index_in_dim(value, index, 0, keepdims=False)
    send = lax.dynamic_index_in_dim(value, 1 - index, 0, keepdims=False)
    got = swap(send, axis, size, mask)
    return (keep.astype(F32) + got.astype(F32)).astype(BF)


def reduce_shard(grad, fsdp, dp):
    columns = grad.shape[1]
    mine = lax.axis_index("fsdp")
    rows = grad.shape[0] // fsdp
    value = grad.reshape(fsdp, rows, columns)
    for bit, mask in enumerate(masks_of(fsdp)):
        value = value.reshape(value.shape[0] // 2, 2, rows, columns).swapaxes(0, 1)
        value = halve(value, "fsdp", fsdp, mask, (mine >> bit) & 1)
    value = value.reshape(rows, columns)
    place = lax.axis_index("dp")
    taken = []
    for bit, mask in enumerate(masks_of(dp)):
        if value.shape[0] % 32:
            got = swap(value, "dp", dp, mask)
            value = (value.astype(F32) + got.astype(F32)).astype(BF)
            continue
        half = (place >> bit) & 1
        value = halve(value.reshape(2, -1, columns), "dp", dp, mask, half)
        taken.append((mask, half))
    for mask, half in reversed(taken):
        got = swap(value, "dp", dp, mask)
        first = jnp.where(half == 0, value, got)
        second = jnp.where(half == 0, got, value)
        value = jnp.concatenate([first, second], axis=0)
    return value.astype(F32)


def total_over(value, sizes):
    for axis, size in sizes:
        for mask in masks_of(size):
            value = value + swap(value, axis, size, mask)
    return value


def adam_terms(gradient, first_old, second_old):
    first_new = BETA * first_old + (1.0 - BETA) * gradient
    second_new = BETA * second_old + (1.0 - BETA) * gradient * gradient
    debias = 1.0 - BETA**STEP
    update = first_new / debias / (jnp.sqrt(second_new / debias) + ADAM_EPS)
    return (first_new, second_new, update)


def pair_major(columns):
    rows = columns.shape[0]
    return columns.reshape(rows, 3, PAIRS, PAIR).swapaxes(1, 2).reshape(rows, -1)


def shards(
    fsdp,
    dp,
    tokens,
    cotangent,
    known_genes,
    cell_kind,
    gene_counts,
    study_index,
    qkv_weight,
    qkv_first,
    qkv_second,
    proj_weight,
    proj_first,
    proj_second,
    up_weight,
    up_first,
    up_second,
    down_weight,
    down_first,
    down_second,
    norm_params,
    norm_first,
    norm_second,
):
    masters = (qkv_weight, proj_weight, up_weight, down_weight, norm_params)
    firsts_old = (qkv_first, proj_first, up_first, down_first, norm_first)
    seconds_old = (qkv_second, proj_second, up_second, down_second, norm_second)
    _, length, width = tokens.shape
    mine = lax.axis_index("fsdp").astype(jnp.int32)
    mine_ref = mine.reshape(1)
    sizes = (("fsdp", fsdp), ("dp", dp))

    qkv_pieces = gather_pieces(pair_major(qkv_weight.astype(BF)), "fsdp", fsdp)
    norm_columns = jnp.pad(norm_params.T, ((0, 0), (0, 124)))
    rest = jnp.concatenate([proj_weight, up_weight, down_weight, norm_columns], axis=1).astype(BF)
    rest, _ = lax.optimization_barrier((rest, qkv_pieces[-1]))
    rest_pieces = gather_pieces(rest, "fsdp", fsdp)

    tokens_t, cot_t, packed, slot, meta = prep(
        cell_kind, gene_counts.reshape(-1), known_genes.reshape(-1), tokens[0], cotangent[0]
    )
    q_t, k_t, v_t, kc, vc, kct, context, log_total = forward(
        mine_ref, meta, qkv_pieces, tokens_t, packed, slot
    )
    out, grad_context, grad_first, inner, g_proj, g_up, g_down, g_norm = dense(
        mine_ref, rest_pieces, tokens_t, context, cot_t
    )

    first_cells = out.reshape(-1, SHORT_LENGTH, width)[:, 0, :].astype(F32)
    slot_index = jnp.arange(first_cells.shape[0], dtype=jnp.int32)
    used_slots = (cell_kind[0] == 0) | (slot_index == 0)
    member = (
        (study_index[0][:, None] == jnp.arange(STUDY_COUNT, dtype=jnp.int32)[None, :])
        & used_slots[:, None]
    ).astype(F32)
    counts = jnp.broadcast_to(jnp.sum(member, axis=0)[:, None], (STUDY_COUNT, width))
    sums = jnp.sum(member[:, :, None] * first_cells[:, None, :], axis=0)
    squares = jnp.sum(member[:, :, None] * (first_cells * first_cells)[:, None, :], axis=0)
    small = jnp.concatenate([counts, sums, squares, g_norm[:, :8].T], axis=0)
    small = total_over(small, sizes)
    study_mean = small[8:16] / small[:8]
    study_var = small[16:24] / small[:8] - study_mean * study_mean
    norm_share = lax.dynamic_slice_in_dim(small[24:28], mine * (width // fsdp), width // fsdp, 1)

    side_share = reduce_shard(jnp.concatenate([g_proj, g_up, g_down], axis=1), fsdp, dp)
    grads = []
    weight_shares = []
    for pair in range(PAIRS):
        grad_t, grad_weight = backward(
            pair, meta, q_t, k_t, v_t, kc, vc, kct, grad_context, log_total, inner, slot, tokens_t
        )
        grads.append(grad_t)
        weight_shares.append(reduce_shard(grad_weight, fsdp, dp))
    input_grad = input_side(mine_ref, qkv_pieces, grads, grad_first)

    qkv_share = jnp.concatenate(
        [share[:, PAIR * kind : PAIR * (kind + 1)] for kind in range(3) for share in weight_shares],
        axis=1,
    )
    shares = (
        qkv_share,
        side_share[:, :width],
        side_share[:, width : 2 * width],
        side_share[:, 2 * width :],
        norm_share,
    )
    moved = [adam_terms(shares[index], firsts_old[index], seconds_old[index]) for index in range(5)]
    updates = [moved[index][2] + MATRIX_DECAY * masters[index] for index in range(4)]
    square_terms = [jnp.sum(masters[index] * masters[index]) for index in range(4)]
    square_terms = square_terms + [jnp.sum(updates[index] * updates[index]) for index in range(4)]
    total_squares = total_over(jnp.stack(square_terms), (("fsdp", fsdp),))
    weight_norms = jnp.sqrt(total_squares[:4])
    update_norms = jnp.sqrt(total_squares[4:])
    trust = weight_norms / update_norms
    results = []
    for index in range(5):
        if index < 4:
            new_weight = masters[index] - MATRIX_RATE * trust[index] * updates[index]
        else:
            new_weight = masters[index] - VECTOR_RATE * moved[index][2]
        results.extend(
            [moved[index][0], moved[index][1], new_weight, new_weight.astype(jnp.bfloat16)]
        )
    matrix_norms = jnp.stack([weight_norms, update_norms, trust])
    return (
        out.reshape(tokens.shape),
        input_grad.reshape(tokens.shape),
        study_mean,
        study_var,
        *results,
        matrix_norms,
    )


def solution(mesh):
    whole_groups = P(("dp", "fsdp"))
    rows = P("fsdp", None)
    columns = P(None, "fsdp")
    return jax.shard_map(
        partial(shards, mesh.shape["fsdp"], mesh.shape["dp"]),
        mesh=mesh,
        in_specs=(whole_groups,) * 6 + (rows,) * 12 + (columns,) * 3,
        out_specs=(whole_groups,) * 2 + (P(), P()) + (rows,) * 16 + (columns,) * 4 + (P(),),
        check_vma=False,
    )
```

```python
from functools import partial

import jax
import jax.numpy as jnp
from jax import lax
from jax.experimental import pallas as pl
from jax.experimental.pallas import tpu as pltpu
from jax.sharding import PartitionSpec as P

HEADS = 8
HDIM = 64
SHORT_LENGTH = 512
STUDY_COUNT = 8
STEP = 5
PAIR = 2 * HDIM
PAIRS = HEADS // 2
KEY_BLOCK = 256
TAIL = 128


BETA = 0.5
ADAM_EPS = 1e-06
NORM_EPS = 1e-05
MATRIX_RATE = 0.5
VECTOR_RATE = 0.3
MATRIX_DECAY = 0.01
MASKED = -1000000000.0
SAFE_SCORE = 40.0

BF = jnp.bfloat16
F32 = jnp.float32
NN = (((1,), (0,)), ((), ()))
NT = (((1,), (1,)), ((), ()))
TN = (((0,), (0,)), ((), ()))
SMEM = pl.BlockSpec(memory_space=pltpu.SMEM)
VMEM = pl.BlockSpec(memory_space=pltpu.VMEM)


def mm(left, right, dims):
    return lax.dot_general(left, right, dims, preferred_element_type=F32)


def whole(*shape):
    return pl.BlockSpec(shape, lambda *_: (0,) * len(shape))


def params(mebibytes):
    return pltpu.CompilerParams(vmem_limit_bytes=mebibytes * 2**20)


def cost(flops, nbytes, trans=0):
    return pl.CostEstimate(flops=int(flops), bytes_accessed=int(nbytes), transcendentals=int(trans))


def iota(shape, dim):
    return lax.broadcasted_iota(jnp.int32, shape, dim)


def prep_kernel(kind, counts, known, tokens, cot, tokens_t, cot_t, packed, slot, meta):
    cells = known.shape[1] // SHORT_LENGTH if known.shape[0] == 1 else 4
    length = tokens.shape[0]
    is_long = kind[0] == 1
    row = iota(known.shape, 0)
    col = iota(known.shape, 1)
    limit = jnp.zeros(known.shape, jnp.int32)
    for cell in range(cells):
        limit = jnp.where(row == cell, counts[cell], limit)
    limit = jnp.where(is_long, counts[0] - SHORT_LENGTH * row, limit)
    first = (col == 0) & (jnp.logical_not(is_long) | (row == 0))
    usable = (col < limit) & ((known[...] == 1) | first) & (row < cells)
    usable_f = jnp.where(usable, 1.0, 0.0)
    square = (SHORT_LENGTH, SHORT_LENGTH)
    before = jnp.where(iota(square, 0) < iota(square, 1), 1.0, 0.0).astype(BF)
    rank = mm(usable_f.astype(BF), before, NN).astype(jnp.int32)
    totals = [jnp.sum(usable_f[cell : cell + 1, :]).astype(jnp.int32) for cell in range(cells)]
    base = jnp.zeros(known.shape, jnp.int32)
    running = jnp.int32(0)
    for cell in range(cells):
        start = jnp.where(is_long, running, SHORT_LENGTH * cell)
        base = jnp.where(row == cell, start, base)
        running = running + totals[cell]
    place = jnp.where(usable, rank + base, -1)
    for cell in range(cells):
        slot[0:1, pl.ds(cell * SHORT_LENGTH, SHORT_LENGTH)] = place[cell : cell + 1, :]
    meta[0] = kind[0]
    for cell in range(cells):
        meta[1 + cell] = jnp.where(is_long, running if cell == 0 else 0, totals[cell])

    for block in range(length // KEY_BLOCK):
        rows = pl.ds(block * KEY_BLOCK, KEY_BLOCK)
        tokens_t[:, rows] = tokens[rows, :].T
        cot_t[:, rows] = cot[rows, :].T
        cell = block * KEY_BLOCK // SHORT_LENGTH
        inside = block * KEY_BLOCK - cell * SHORT_LENGTH
        needed = jnp.where(is_long, block * KEY_BLOCK < running, inside < totals[cell])

        @pl.when(needed)
        def _(block=block, rows=rows):
            hot = one_hot(slot, block * KEY_BLOCK, KEY_BLOCK)
            packed[rows, :] = mm(hot, tokens[...], NN).astype(BF)


def one_hot(slot, begin, rows):
    shape = (rows, slot.shape[1])
    hit = (iota(shape, 0) + begin) == slot[0:1, :]
    return jnp.where(hit, 1.0, 0.0).astype(BF)


def prep(kind, counts, known, tokens, cot):
    length, width = tokens.shape
    cells = length // SHORT_LENGTH
    known = jnp.pad(known.reshape(cells, SHORT_LENGTH), ((0, 8 - cells), (0, 0)))
    return pl.pallas_call(
        prep_kernel,
        in_specs=[SMEM, SMEM, whole(8, SHORT_LENGTH), whole(length, width), whole(length, width)],
        out_specs=[
            whole(width, length),
            whole(width, length),
            whole(length, width),
            whole(1, length),
            SMEM,
        ],
        out_shape=[
            jax.ShapeDtypeStruct((width, length), BF),
            jax.ShapeDtypeStruct((width, length), BF),
            jax.ShapeDtypeStruct((length, width), BF),
            jax.ShapeDtypeStruct((1, length), jnp.int32),
            jax.ShapeDtypeStruct((8,), jnp.int32),
        ],
        compiler_params=params(28),
        cost_estimate=cost(3e9, 12e6),
        name="prep",
    )(kind, counts, known, tokens, cot)


def fetch_rows(pieces, mine, target):
    rows = pieces[0].shape[0]
    for index, piece in enumerate(pieces):
        owner = jnp.bitwise_xor(mine, index)
        target[pl.ds(pl.multiple_of(owner * rows, rows), rows), :] = piece[...]


def head_lanes(shape, head):
    lane = iota(shape, 1)
    return (lane >= HDIM * head) & (lane < HDIM * (head + 1))


def spare(head):
    return HDIM * (1 - head)


def key_side(block, head, begin, count):
    lane = iota(block.shape, 1) - spare(head)
    row = iota(block.shape, 0) + begin
    bias = jnp.where(row < count, 0.0, MASKED)
    extra = jnp.where(lane == 0, bias, jnp.where((lane > 0) & (lane < 4), 1.0, 0.0))
    return jnp.where(head_lanes(block.shape, head), block.astype(F32), extra).astype(BF)


def value_side(block, head):
    lane = iota(block.shape, 1) - spare(head)
    extra = jnp.where((lane > 0) & (lane < 4), 1.0, 0.0)
    return jnp.where(head_lanes(block.shape, head), block.astype(F32), extra).astype(BF)


def split_rows(shift):
    high = shift.astype(BF).astype(F32)
    rest = shift - high
    mid = rest.astype(BF).astype(F32)
    low = rest - mid
    shape = (16, shift.shape[1])
    row = iota(shape, 0)
    out = jnp.where(row == 0, 1.0, 0.0)
    out = jnp.where(row == 1, -high, out)
    out = jnp.where(row == 2, -mid, out)
    return jnp.where(row == 3, -low, out).astype(BF)


def query_side(target, head, rows, shift):
    other = spare(head)
    target[head, HDIM * head : HDIM * (head + 1), :] = rows
    target[head, other : other + 16, :] = split_rows(shift)
    target[head, other + 16 : other + HDIM, :] = jnp.zeros((HDIM - 16, rows.shape[1]), BF)


def walk(meta, length, body):
    @pl.when(meta[0] == 1)
    def _():
        cell_walk(meta[1], 0, 0, length, body)

    @pl.when(meta[0] != 1)
    def _():
        for cell in range(length // SHORT_LENGTH):
            cell_walk(meta[1 + cell], cell * SHORT_LENGTH, cell * SHORT_LENGTH, SHORT_LENGTH, body)


def cell_walk(count, slot_begin, query_begin, queries, body):
    rest = lax.rem(count, KEY_BLOCK)
    tail = (rest > 0) & (rest <= TAIL)
    full = count // KEY_BLOCK + jnp.where(rest > TAIL, 1, 0)
    end = slot_begin + count

    @pl.loop(0, full)
    def _(index):
        begin = pl.multiple_of(slot_begin + index * KEY_BLOCK, KEY_BLOCK)
        body(begin, KEY_BLOCK, query_begin, queries, end)

    @pl.when(tail)
    def _():
        begin = pl.multiple_of(slot_begin + full * KEY_BLOCK, KEY_BLOCK)
        body(begin, TAIL, query_begin, queries, end)


def forward_kernel(count, mine, meta, *refs):
    pieces = refs[:count]
    tokens_t, packed, slot = refs[count : count + 3]
    q_out, k_out, v_out, kc_out, vc_out, kct_out, context, log_total = refs[count + 3 : count + 11]
    weights, vct, side, total, shift = refs[count + 11 :]
    step = pl.program_id(0)
    length = tokens_t.shape[1]

    @pl.when(step == 0)
    def _():
        fetch_rows(pieces, mine[0], weights)

    columns = pl.ds(pl.multiple_of(step * 3 * PAIR, 3 * PAIR), 3 * PAIR)
    part = weights[:, columns]
    joined = mm(part, tokens_t[...], TN)
    q_out[...] = (joined[:PAIR] * HDIM**-0.5).astype(BF)
    k_out[...] = joined[PAIR : 2 * PAIR].astype(BF)
    v_out[...] = joined[2 * PAIR :].astype(BF)

    def project(begin, rows, *_):
        place = pl.ds(begin, rows)
        both = mm(packed[place, :], part[:, PAIR:], NN).astype(BF)
        kc_out[place, :] = both[:, :PAIR]
        vc_out[place, :] = both[:, PAIR:]
        kct_out[:, place] = both[:, :PAIR].T
        turned = both[:, PAIR:].T
        ones = jnp.where(iota((16, rows), 0) == 0, 1.0, 0.0).astype(BF)
        for head in range(2):
            vct[head, :HDIM, place] = turned[HDIM * head : HDIM * (head + 1)]
            vct[head, HDIM:, place] = ones

    walk(meta, length, project)

    masked = slot[...] < 0
    own = []
    for head in range(2):
        rows = slice(HDIM * head, HDIM * (head + 1))
        queries = q_out[rows, :].astype(F32)
        keys = k_out[rows, :].astype(F32)
        own.append(jnp.where(masked, jnp.sum(queries * keys, axis=0, keepdims=True), MASKED))
        top_q = jnp.max(jnp.sum(queries * queries, axis=0, keepdims=True))
        top_k = jnp.max(jnp.sum(keys * keys, axis=0, keepdims=True))
        unsafe = jnp.logical_not(top_q * top_k < SAFE_SCORE * SAFE_SCORE)
        shift[head : head + 1, :] = jnp.zeros((1, length), F32)
        query_side(side, head, q_out[rows, :], jnp.zeros((1, length), F32))

        @pl.when(unsafe)
        def _(head=head, rows=rows):
            shift[head : head + 1, :] = own[head]

            def raise_top(begin, rows, first, queries, end):
                keys = key_side(kc_out[pl.ds(begin, rows), :], head, begin, end)
                place = pl.ds(first, queries)
                scores = mm(keys, side[head, :, place], NN)
                top = jnp.max(scores, axis=0, keepdims=True)
                shift[head : head + 1, place] = jnp.maximum(shift[head : head + 1, place], top)

            walk(meta, length, raise_top)
            query_side(side, head, q_out[rows, :], shift[head : head + 1, :])

    total[...] = jnp.zeros(total.shape, F32)

    def attend(begin, rows, first, queries, end):
        slots = pl.ds(begin, rows)
        place = pl.ds(first, queries)
        for head in range(2):
            keys = key_side(kc_out[slots, :], head, begin, end)
            raised = jnp.exp(mm(keys, side[head, :, place], NN)).astype(BF)
            total[head, :, place] += mm(vct[head, :, slots], raised, NN)

    walk(meta, length, attend)

    for head in range(2):
        rows = slice(HDIM * head, HDIM * (head + 1))
        alone = jnp.exp(own[head] - shift[head : head + 1, :])
        row_total = total[head, HDIM : HDIM + 1, :] + alone
        gathered = total[head, :HDIM, :] + v_out[rows, :].astype(F32) * alone
        context[rows, :] = (gathered / row_total).astype(BF)
        log_total[pl.ds(step * 2 + head, 1), :] = shift[head : head + 1, :] + jnp.log(row_total)


def forward(mine, meta, pieces, tokens_t, packed, slot):
    width, length = tokens_t.shape
    pair_rows = pl.BlockSpec((PAIR, length), lambda step: (step, 0))
    pair_lanes = pl.BlockSpec((length, PAIR), lambda step: (0, step))
    transposed = jax.ShapeDtypeStruct((width, length), BF)
    natural = jax.ShapeDtypeStruct((length, width), BF)
    count = len(pieces)
    return pl.pallas_call(
        partial(forward_kernel, count),
        grid=(PAIRS,),
        in_specs=[SMEM, SMEM]
        + [VMEM] * count
        + [whole(width, length), whole(length, width), whole(1, length)],
        out_specs=[pair_rows] * 3 + [pair_lanes] * 2 + [pair_rows] * 2 + [whole(HEADS, length)],
        out_shape=[transposed] * 3
        + [natural] * 2
        + [transposed] * 2
        + [jax.ShapeDtypeStruct((HEADS, length), F32)],
        scratch_shapes=[
            pltpu.VMEM((width, 3 * width), BF),
            pltpu.VMEM((2, HDIM + 16, length), BF),
            pltpu.VMEM((2, PAIR, length), BF),
            pltpu.VMEM((2, HDIM + 16, length), F32),
            pltpu.VMEM((8, length), F32),
        ],
        compiler_params=params(36),
        cost_estimate=cost(15e9, 25e6, 20e6),
        name="attend_forward",
    )(mine, meta, *pieces, tokens_t, packed, slot)


def backward_kernel(pair, meta, *refs):
    q_t, k_t, v_t, kc, vc, kct, grad_context, log_total, inner, slot, tokens_t = refs[:11]
    grad_t, grad_weight = refs[11:13]
    q_side, g_side, grad_q, grad_kv, ready = refs[13:]
    length = tokens_t.shape[1]
    for head in range(2):
        rows = slice(HDIM * head, HDIM * (head + 1))
        index = 2 * pair + head
        query_side(q_side, head, q_t[rows, :], log_total[index : index + 1, :])
        query_side(g_side, head, grad_context[rows, :], inner[index : index + 1, :])
    grad_q[...] = jnp.zeros(grad_q.shape, F32)
    grad_kv[...] = jnp.zeros(grad_kv.shape, F32)

    def pull(begin, rows, first, queries, end):
        slots = pl.ds(begin, rows)
        place = pl.ds(first, queries)
        for head in range(2):
            lanes = slice(HDIM * head, HDIM * (head + 1))
            keys = key_side(kc[slots, :], head, begin, end)
            values = value_side(vc[slots, :], head)
            probs = jnp.exp(mm(keys, q_side[head, :, place], NN))
            grad_scores = (probs * mm(values, g_side[head, :, place], NN)).astype(BF)
            grad_q[lanes, place] += mm(kct[lanes, slots], grad_scores, NN)
            ready[HDIM * head : HDIM * (head + 1), :rows] = mm(
                q_t[lanes, place], grad_scores, NT
            ).astype(BF)
            ready[PAIR + HDIM * head : PAIR + HDIM * (head + 1), :rows] = mm(
                grad_context[lanes, place], probs.astype(BF), NT
            ).astype(BF)
        hit = (iota((rows, queries), 0) + begin) == slot[0:1, place]
        spread = jnp.where(hit, 1.0, 0.0).astype(BF)
        grad_kv[:, place] += mm(ready[:, :rows], spread, NN)

    walk(meta, length, pull)

    masked = slot[...] < 0
    for head in range(2):
        rows = slice(HDIM * head, HDIM * (head + 1))
        index = 2 * pair + head
        queries = q_t[rows, :].astype(F32)
        keys = k_t[rows, :].astype(F32)
        values = v_t[rows, :].astype(F32)
        grads = grad_context[rows, :].astype(F32)
        own = jnp.sum(queries * keys, axis=0, keepdims=True)
        own = jnp.where(masked, own - log_total[index : index + 1, :], MASKED)
        alone = jnp.exp(own)
        pulled = jnp.sum(grads * values, axis=0, keepdims=True) - inner[index : index + 1, :]
        pulled = (alone * pulled).astype(BF).astype(F32)
        alone = alone.astype(BF).astype(F32)
        part = (grad_q[rows, :] + keys * pulled) * HDIM**-0.5
        grad_t[HDIM * head : HDIM * (head + 1), :] = part.astype(BF)
        part = grad_kv[rows, :] + queries * pulled
        grad_t[PAIR + HDIM * head : PAIR + HDIM * (head + 1), :] = part.astype(BF)
        part = grad_kv[PAIR + HDIM * head : PAIR + HDIM * (head + 1), :] + grads * alone
        grad_t[2 * PAIR + HDIM * head : 2 * PAIR + HDIM * (head + 1), :] = part.astype(BF)
    grad_weight[...] = mm(tokens_t[...], grad_t[...], NT).astype(BF)


def backward(pair, meta, q_t, k_t, v_t, kc, vc, kct, grad_context, log_total, inner, slot, tokens_t):
    width, length = tokens_t.shape
    pair_rows = pl.BlockSpec((PAIR, length), lambda step: (pair, 0))
    pair_lanes = pl.BlockSpec((length, PAIR), lambda step: (0, pair))
    return pl.pallas_call(
        partial(backward_kernel, pair),
        grid=(1,),
        in_specs=[SMEM]
        + [pair_rows] * 3
        + [pair_lanes] * 2
        + [pair_rows] * 2
        + [whole(HEADS, length)] * 2
        + [whole(1, length), whole(width, length)],
        out_specs=[whole(3 * PAIR, length), whole(width, 3 * PAIR)],
        out_shape=[
            jax.ShapeDtypeStruct((3 * PAIR, length), BF),
            jax.ShapeDtypeStruct((width, 3 * PAIR), BF),
        ],
        scratch_shapes=[
            pltpu.VMEM((2, PAIR, length), BF),
            pltpu.VMEM((2, PAIR, length), BF),
            pltpu.VMEM((PAIR, length), F32),
            pltpu.VMEM((2 * PAIR, length), F32),
            pltpu.VMEM((2 * PAIR, KEY_BLOCK), BF),
        ],
        compiler_params=params(36),
        cost_estimate=cost(12e9, 10e6, 6e6),
        name=f"attend_backward_{pair}",
    )(meta, q_t, k_t, v_t, kc, vc, kct, grad_context, log_total, inner, slot, tokens_t)


def feature_mean(values):
    return jnp.sum(values, axis=0, keepdims=True) * (1.0 / values.shape[0])


def normalise(values):
    centred = values - feature_mean(values)
    scale = lax.rsqrt(feature_mean(centred * centred) + NORM_EPS)
    return centred * scale, scale


def pull_norm(grad, scaled, scale, gain):
    lifted = grad * gain
    return scale * (lifted - feature_mean(lifted) - scaled * feature_mean(lifted * scaled))


def lane_sums(values):
    width = 128
    out = values[:, :width]
    for begin in range(width, values.shape[1], width):
        out = out + values[:, begin : begin + width]
    return out


def dense_kernel(count, mine, *refs):
    pieces = refs[:count]
    tokens_t, context, cot_t = refs[count : count + 3]
    out, grad_context, grad_first, inner, g_proj, g_up, g_down, g_norm = refs[count + 3 : count + 11]
    weights, total, norm_total = refs[count + 11 :]
    step = pl.program_id(0)
    width = tokens_t.shape[0]

    @pl.when(step == 0)
    def _():
        fetch_rows(pieces, mine[0], weights)
        total[...] = jnp.zeros(total.shape, F32)
        norm_total[...] = jnp.zeros(norm_total.shape, F32)

    proj = weights[:, :width]
    up = weights[:, width : 2 * width]
    down = weights[:, 2 * width : 3 * width]
    rows = weights[:, 3 * width :].astype(F32)
    gain1, bias1, gain2, bias2 = (rows[:, index : index + 1] for index in range(4))

    context_low = context[...]
    scaled1, scale1 = normalise(tokens_t[...].astype(F32) + mm(proj, context_low, TN))
    middle = scaled1 * gain1 + bias1
    middle_low = middle.astype(BF)
    hidden = mm(up, middle_low, TN)
    cdf = 0.5 * (1.0 + lax.erf(hidden * 2.0**-0.5))
    slope = cdf + hidden * jnp.exp(hidden * hidden * -0.5) * 0.3989422804014327
    active = (hidden * cdf).astype(BF)
    scaled2, scale2 = normalise(middle + mm(down, active, TN))
    out[...] = (scaled2 * gain2 + bias2).astype(BF).T

    cot = cot_t[...].astype(F32)
    norm_total[2] += lane_sums(cot * scaled2)
    norm_total[3] += lane_sums(cot)
    grad_second = pull_norm(cot, scaled2, scale2, gain2)
    grad_low = grad_second.astype(BF)
    total[2] += mm(active, grad_low, NT)
    grad_hidden = (mm(down, grad_low, NN) * slope).astype(BF)
    total[1] += mm(middle_low, grad_hidden, NT)
    grad_middle = grad_second + mm(up, grad_hidden, NN)
    norm_total[0] += lane_sums(grad_middle * scaled1)
    norm_total[1] += lane_sums(grad_middle)
    grad_h1 = pull_norm(grad_middle, scaled1, scale1, gain1)
    grad_first[...] = grad_h1
    proj_low = grad_h1.astype(BF)
    total[0] += mm(context_low, proj_low, NT)
    pulled = mm(proj, proj_low, NN).astype(BF)
    grad_context[...] = pulled
    both = pulled.astype(F32) * context_low.astype(F32)
    for head in range(HEADS):
        part = both[HDIM * head : HDIM * (head + 1), :]
        inner[head : head + 1, :] = jnp.sum(part, axis=0, keepdims=True)

    @pl.when(step == pl.num_programs(0) - 1)
    def _():
        g_proj[...] = total[0].astype(BF)
        g_up[...] = total[1].astype(BF)
        g_down[...] = total[2].astype(BF)
        lane = iota((width, 128), 1)
        packed = jnp.zeros((width, 128), F32)
        for index in range(4):
            column = jnp.sum(norm_total[index], axis=1, keepdims=True)
            packed = jnp.where(lane == index, column, packed)
        g_norm[...] = packed


def dense(mine, pieces, tokens_t, context, cot_t):
    width, length = tokens_t.shape
    block = 512
    count = len(pieces)
    columns = pl.BlockSpec((width, block), lambda step: (0, step))
    square = jax.ShapeDtypeStruct((width, width), BF)
    return pl.pallas_call(
        partial(dense_kernel, count),
        grid=(length // block,),
        in_specs=[SMEM] + [VMEM] * count + [columns] * 3,
        out_specs=[
            pl.BlockSpec((block, width), lambda step: (step, 0)),
            columns,
            columns,
            pl.BlockSpec((HEADS, block), lambda step: (0, step)),
        ]
        + [whole(width, width)] * 3
        + [whole(width, 128)],
        out_shape=[
            jax.ShapeDtypeStruct((length, width), BF),
            jax.ShapeDtypeStruct((width, length), BF),
            jax.ShapeDtypeStruct((width, length), F32),
            jax.ShapeDtypeStruct((HEADS, length), F32),
        ]
        + [square] * 3
        + [jax.ShapeDtypeStruct((width, 128), F32)],
        scratch_shapes=[
            pltpu.VMEM((width, 3 * width + 128), BF),
            pltpu.VMEM((3, width, width), F32),
            pltpu.VMEM((4, width, 128), F32),
        ],
        compiler_params=params(40),
        cost_estimate=cost(10e9, 20e6, 4e6),
        name="dense",
    )(mine, *pieces, tokens_t, context, cot_t)


def input_kernel(count, mine, *refs):
    pieces = refs[:count]
    grads = refs[count : count + PAIRS]
    grad_first, out = refs[count + PAIRS : count + PAIRS + 2]
    (weights,) = refs[count + PAIRS + 2 :]

    @pl.when(pl.program_id(0) == 0)
    def _():
        fetch_rows(pieces, mine[0], weights)

    total = grad_first[...]
    for pair in range(PAIRS):
        total = total + mm(weights[:, 3 * PAIR * pair : 3 * PAIR * (pair + 1)], grads[pair][...], NN)
    out[...] = total.astype(BF).T


def input_side(mine, pieces, grads, grad_first):
    width, length = grad_first.shape
    block = 512
    count = len(pieces)
    return pl.pallas_call(
        partial(input_kernel, count),
        grid=(length // block,),
        in_specs=[SMEM]
        + [VMEM] * count
        + [pl.BlockSpec((3 * PAIR, block), lambda step: (0, step))] * PAIRS
        + [pl.BlockSpec((width, block), lambda step: (0, step))],
        out_specs=pl.BlockSpec((block, width), lambda step: (step, 0)),
        out_shape=jax.ShapeDtypeStruct((length, width), BF),
        scratch_shapes=[pltpu.VMEM((width, 3 * width), BF)],
        compiler_params=params(24),
        cost_estimate=cost(3.3e9, 14e6),
        name="input_side",
    )(mine, *pieces, *grads, grad_first)


def swap(value, axis, size, mask):
    return lax.ppermute(value, axis, [(index, index ^ mask) for index in range(size)])


def masks_of(size):
    return [1 << bit for bit in range(size.bit_length() - 1)]


def gather_pieces(piece, axis, size, meanwhile):
    pieces = {0: piece}
    for mask in reversed(masks_of(size)):
        for known in list(pieces):
            pieces[known ^ mask] = swap(pieces[known], axis, size, mask)
            if meanwhile is not None:
                meanwhile, pieces[mask] = lax.optimization_barrier((meanwhile, pieces[mask]))
                meanwhile = None
    return [pieces[index] for index in range(size)]


def halving(value, axis, size):
    mine = lax.axis_index(axis)
    rows = value.shape[0] // size
    value = value.reshape(size, rows, -1)
    for bit, mask in enumerate(masks_of(size)):
        value = value.reshape(value.shape[0] // 2, 2, rows, -1).swapaxes(0, 1)
        side = (mine >> bit) & 1
        send = lax.dynamic_index_in_dim(value, 1 - side, 0, keepdims=False)
        got = yield send, axis, size, mask
        keep = lax.dynamic_index_in_dim(value, side, 0, keepdims=False)
        value = (keep.astype(F32) + got.astype(F32)).astype(value.dtype)
    return value.reshape(rows, -1)


def doubling(value, axis, size):
    for mask in masks_of(size):
        got = yield value, axis, size, mask
        value = (value.astype(F32) + got.astype(F32)).astype(value.dtype)
    return value


def side_steps(value, fsdp, dp):
    value = yield from halving(value, "fsdp", fsdp)
    return (yield from doubling(value, "dp", dp))


def small_steps(value, fsdp, dp):
    value = yield from doubling(value, "fsdp", fsdp)
    return (yield from doubling(value, "dp", dp))


class Chain:
    def __init__(self, steps):
        self.steps, self.result, self.got = steps, None, None
        self.request = next(steps)

    def send(self, value):
        _, axis, size, mask = self.request
        self.got = swap(value, axis, size, mask)

    def land(self, value):
        try:
            self.request = self.steps.send(value)
        except StopIteration as end:
            self.request, self.result = None, end.value

    def finish(self):
        while self.request is not None:
            if self.got is None:
                self.send(self.request[0])
            value, self.got = self.got, None
            self.land(value)
        return self.result


def start_steps(anchor, chains):
    live = [chain for chain in chains if chain.request is not None]
    anchor, *values = lax.optimization_barrier((anchor, *(chain.request[0] for chain in live)))
    for chain, value in zip(live, values):
        chain.send(value)
    return anchor


def end_steps(anchor, chains):
    live = [chain for chain in chains if chain.got is not None]
    anchor, *values = lax.optimization_barrier((anchor, *(chain.got for chain in live)))
    for chain, value in zip(live, values):
        chain.got = None
        chain.land(value)
    return anchor


def total_by_exchange(value, axis, size):
    rows, columns = value.shape
    parts = lax.all_to_all(value, axis, 0, 0, tiled=True).reshape(size, rows // size, columns)
    mine = jnp.sum(parts.astype(F32), axis=0).astype(BF)
    return lax.all_to_all(jnp.tile(mine, (size, 1)), axis, 0, 0, tiled=True)


def moments(gradient, first_old, second_old):
    first_new = BETA * first_old + (1.0 - BETA) * gradient
    second_new = BETA * second_old + (1.0 - BETA) * gradient * gradient
    return first_new, second_new


def update_of(first_new, second_new):
    debias = 1.0 - BETA**STEP
    return first_new / debias / (jnp.sqrt(second_new / debias) + ADAM_EPS)


def square_row(values):
    total = jnp.sum(values * values, axis=0, keepdims=True)
    return lane_sums(total)


def moments_kernel(count, paired, gradient, *refs):
    olds, outs, squares = refs[: 3 * count], refs[3 * count : 5 * count], refs[5 * count]
    at = 0
    squares[...] = jnp.zeros(squares.shape, F32)
    for index in range(count):
        weight, first_old, second_old = (ref[...] for ref in olds[3 * index : 3 * index + 3])
        columns = weight.shape[1]
        if paired:
            places = [
                3 * PAIR * (PAIRS - 1 - pair) + PAIR * kind
                for kind in range(3)
                for pair in range(PAIRS)
            ]
            grad = jnp.concatenate([gradient[:, at : at + PAIR] for at in places], axis=1)
        else:
            grad = gradient[:, at : at + columns]
        grad = grad.astype(F32)
        at += columns
        first_new, second_new = moments(grad, first_old, second_old)
        outs[2 * index][...] = first_new
        outs[2 * index + 1][...] = second_new
        update = update_of(first_new, second_new) + MATRIX_DECAY * weight
        squares[index : index + 1, :] = square_row(weight)
        squares[4 + index : 5 + index, :] = square_row(update)


def new_moments(gradient, olds, paired):
    shapes = [jax.ShapeDtypeStruct(old.shape, F32) for old in olds]
    count = len(olds) // 3
    outs = [shape for shape in shapes[::3] for _ in range(2)]
    results = pl.pallas_call(
        partial(moments_kernel, count, paired),
        out_shape=outs + [jax.ShapeDtypeStruct((8, 128), F32)],
        compiler_params=params(16),
        cost_estimate=cost(5e6, 5e6),
        name="moments",
    )(gradient, *olds)
    return results[:-1], results[-1]


def apply_kernel(count, squares, *refs):
    inputs, outs, norms = refs[: 3 * count], refs[3 * count : 5 * count], refs[5 * count]
    total = jnp.sum(jnp.sum(squares[...], axis=0), axis=1, keepdims=True)
    size = jnp.sqrt(total)
    ratio = size[0:4] / size[4:8]
    lane = iota((1, 4), 1)
    rows = [jnp.zeros((1, 4), F32)] * 3
    for index in range(count):
        weight, first_new, second_new = (ref[...] for ref in inputs[3 * index : 3 * index + 3])
        update = update_of(first_new, second_new) + MATRIX_DECAY * weight
        trust = ratio[index : index + 1]
        weight = weight - MATRIX_RATE * trust * update
        outs[2 * index][...] = weight
        outs[2 * index + 1][...] = weight.astype(BF)
        for place, value in enumerate((size[index : index + 1], size[4 + index : 5 + index], trust)):
            rows[place] = jnp.where(lane == index, value, rows[place])
    for place in range(3):
        norms[place : place + 1, :] = rows[place]


def apply_updates(squares, arrays):
    count = len(arrays) // 3
    outs = []
    for weight in arrays[::3]:
        outs += [jax.ShapeDtypeStruct(weight.shape, F32), jax.ShapeDtypeStruct(weight.shape, BF)]
    results = pl.pallas_call(
        partial(apply_kernel, count),
        out_shape=outs + [jax.ShapeDtypeStruct((3, 4), F32)],
        compiler_params=params(16),
        cost_estimate=cost(5e6, 8e6),
        name="apply",
    )(squares, *arrays)
    return results[:-1], results[-1]


def pair_major(columns):
    rows = columns.shape[0]
    return columns.reshape(rows, 3, PAIRS, PAIR).swapaxes(1, 2).reshape(rows, -1)


def shards(
    fsdp,
    dp,
    tokens,
    cotangent,
    known_genes,
    cell_kind,
    gene_counts,
    study_index,
    qkv_weight,
    qkv_first,
    qkv_second,
    proj_weight,
    proj_first,
    proj_second,
    up_weight,
    up_first,
    up_second,
    down_weight,
    down_first,
    down_second,
    norm_params,
    norm_first,
    norm_second,
):
    _, length, width = tokens.shape
    mine = lax.axis_index("fsdp").astype(jnp.int32)
    mine_ref = mine.reshape(1)

    tokens_t, cot_t, packed, slot, meta = prep(
        cell_kind, gene_counts.reshape(-1), known_genes.reshape(-1), tokens[0], cotangent[0]
    )
    qkv_pieces = gather_pieces(pair_major(qkv_weight.astype(BF)), "fsdp", fsdp, slot)
    norm_columns = jnp.pad(norm_params.T, ((0, 0), (0, 124)))
    rest = jnp.concatenate([proj_weight, up_weight, down_weight, norm_columns], axis=1).astype(BF)
    *qkv_pieces, rest, slot = lax.optimization_barrier((*qkv_pieces, rest, slot))
    q_t, k_t, v_t, kc, vc, kct, context, log_total = forward(
        mine_ref, meta, qkv_pieces, tokens_t, packed, slot
    )
    rest_pieces = gather_pieces(rest, "fsdp", fsdp, q_t)
    out, grad_context, grad_first, inner, g_proj, g_up, g_down, g_norm = dense(
        mine_ref, rest_pieces, tokens_t, context, cot_t
    )

    first_cells = out.reshape(-1, SHORT_LENGTH, width)[:, 0, :].astype(F32)
    slot_index = jnp.arange(first_cells.shape[0], dtype=jnp.int32)
    used_slots = (cell_kind[0] == 0) | (slot_index == 0)
    member = (
        (study_index[0][:, None] == jnp.arange(STUDY_COUNT, dtype=jnp.int32)[None, :])
        & used_slots[:, None]
    ).astype(F32)
    counts = jnp.broadcast_to(jnp.sum(member, axis=0)[:, None], (STUDY_COUNT, width))
    sums = jnp.sum(member[:, :, None] * first_cells[:, None, :], axis=0)
    squares = jnp.sum(member[:, :, None] * (first_cells * first_cells)[:, None, :], axis=0)
    small = jnp.concatenate([counts, sums, squares, g_norm[:, :8].T], axis=0)
    small_chain = Chain(small_steps(small, fsdp, dp))
    side_chain = Chain(side_steps(jnp.concatenate([g_proj, g_up, g_down], axis=1), fsdp, dp))
    chains = [side_chain, small_chain]
    half_chains = []
    grads = []
    parts = []
    for pair in reversed(range(PAIRS)):
        meta = start_steps(meta, chains)
        grad_t, part = backward(
            pair, meta, q_t, k_t, v_t, kc, vc, kct, grad_context, log_total, inner, slot, tokens_t
        )
        part = end_steps(part, chains)
        grads.append(grad_t)
        parts.append(part)
        if len(parts) * 2 == PAIRS:
            half_chains.append(Chain(halving(jnp.concatenate(parts, axis=1), "fsdp", fsdp)))
            chains.append(half_chains[-1])
            parts = []
    mine_ref = start_steps(mine_ref, chains)
    input_grad = input_side(mine_ref, qkv_pieces, grads[::-1], grad_first)
    input_grad = end_steps(input_grad, chains)

    qkv_share = jnp.concatenate([chain.finish() for chain in half_chains], axis=1)
    qkv_share = total_by_exchange(qkv_share, "dp", dp)
    side_share = side_chain.finish()
    small = small_chain.finish()
    study_mean = small[8:16] / small[:8]
    study_var = small[16:24] / small[:8] - study_mean * study_mean
    norm_share = lax.dynamic_slice_in_dim(small[24:28], mine * (width // fsdp), width // fsdp, 1)
    norm_first, norm_second = moments(norm_share, norm_first, norm_second)
    norm_params = norm_params - VECTOR_RATE * update_of(norm_first, norm_second)

    side_old = (proj_weight, proj_first, proj_second, up_weight, up_first, up_second)
    side_old += (down_weight, down_first, down_second)
    (qkv_first, qkv_second), qkv_squares = new_moments(
        qkv_share, (qkv_weight, qkv_first, qkv_second), True
    )
    side_new, side_squares = new_moments(side_share, side_old, False)
    squares = jnp.concatenate(
        [qkv_squares[0:1], side_squares[0:3], qkv_squares[4:5], side_squares[4:7]], axis=0
    )
    squares = lax.all_gather(squares, "fsdp", axis=0)
    arrays = (qkv_weight, qkv_first, qkv_second, proj_weight, side_new[0], side_new[1])
    arrays += (up_weight, side_new[2], side_new[3], down_weight, side_new[4], side_new[5])
    applied, matrix_norms = apply_updates(squares, arrays)
    results = []
    for index in range(4):
        results += [arrays[3 * index + 1], arrays[3 * index + 2]]
        results += [applied[2 * index], applied[2 * index + 1]]
    return (
        out.reshape(tokens.shape),
        input_grad.reshape(tokens.shape),
        study_mean,
        study_var,
        *results,
        norm_first,
        norm_second,
        norm_params,
        norm_params.astype(BF),
        matrix_norms,
    )


def solution(mesh):
    whole_groups = P(("dp", "fsdp"))
    rows = P("fsdp", None)
    columns = P(None, "fsdp")
    return jax.shard_map(
        partial(shards, mesh.shape["fsdp"], mesh.shape["dp"]),
        mesh=mesh,
        in_specs=(whole_groups,) * 6 + (rows,) * 12 + (columns,) * 3,
        out_specs=(whole_groups,) * 2 + (P(), P()) + (rows,) * 16 + (columns,) * 4 + (P(),),
        check_vma=False,
    )
```

```python
from functools import partial

import jax
import jax.numpy as jnp
from jax import lax
from jax.experimental import pallas as pl
from jax.experimental.pallas import tpu as pltpu
from jax.sharding import PartitionSpec as P

HEADS = 8
HDIM = 64
SHORT_LENGTH = 512
STUDY_COUNT = 8
STEP = 5
PAIR = 2 * HDIM
PAIRS = HEADS // 2
KEY_BLOCK = 256
TAIL = 128


BETA = 0.5
ADAM_EPS = 1e-06
NORM_EPS = 1e-05
MATRIX_RATE = 0.5
VECTOR_RATE = 0.3
MATRIX_DECAY = 0.01
MASKED = -1000000000.0
SAFE_SCORE = 40.0

BF = jnp.bfloat16
F32 = jnp.float32
NN = (((1,), (0,)), ((), ()))
NT = (((1,), (1,)), ((), ()))
TN = (((0,), (0,)), ((), ()))
SMEM = pl.BlockSpec(memory_space=pltpu.SMEM)
ANY = pl.BlockSpec(memory_space=pl.ANY)


def mm(left, right, dims):
    return lax.dot_general(left, right, dims, preferred_element_type=F32)


def whole(*shape):
    return pl.BlockSpec(shape, lambda *_: (0,) * len(shape))


def params(mebibytes):
    return pltpu.CompilerParams(vmem_limit_bytes=mebibytes * 2**20)


def cost(flops, nbytes, trans=0):
    return pl.CostEstimate(flops=int(flops), bytes_accessed=int(nbytes), transcendentals=int(trans))


def iota(shape, dim):
    return lax.broadcasted_iota(jnp.int32, shape, dim)


def prep_kernel(kind, counts, known, tokens, cot, tokens_t, cot_t, packed, slot, meta):
    length = tokens.shape[0]
    cells = length // SHORT_LENGTH
    is_long = kind[0] == 1
    shape = (8, SHORT_LENGTH)
    row = iota(shape, 0)
    col = iota(shape, 1)
    given = jnp.zeros(shape, jnp.int32)
    for cell in range(cells):
        given = jnp.where(row == cell, known[0:1, pl.ds(cell * SHORT_LENGTH, SHORT_LENGTH)], given)
    limit = jnp.zeros(shape, jnp.int32)
    for cell in range(cells):
        limit = jnp.where(row == cell, counts[cell], limit)
    limit = jnp.where(is_long, counts[0] - SHORT_LENGTH * row, limit)
    first = (col == 0) & (jnp.logical_not(is_long) | (row == 0))
    usable = (col < limit) & ((given == 1) | first) & (row < cells)
    usable_f = jnp.where(usable, 1.0, 0.0)
    square = (SHORT_LENGTH, SHORT_LENGTH)
    before = jnp.where(iota(square, 0) < iota(square, 1), 1.0, 0.0).astype(BF)
    rank = mm(usable_f.astype(BF), before, NN).astype(jnp.int32)
    totals = [jnp.sum(usable_f[cell : cell + 1, :]).astype(jnp.int32) for cell in range(cells)]
    base = jnp.zeros(shape, jnp.int32)
    running = jnp.int32(0)
    for cell in range(cells):
        start = jnp.where(is_long, running, SHORT_LENGTH * cell)
        base = jnp.where(row == cell, start, base)
        running = running + totals[cell]
    place = jnp.where(usable, rank + base, -1)
    for cell in range(cells):
        slot[0:1, pl.ds(cell * SHORT_LENGTH, SHORT_LENGTH)] = place[cell : cell + 1, :]
    meta[0] = kind[0]
    for cell in range(cells):
        meta[1 + cell] = jnp.where(is_long, running if cell == 0 else 0, totals[cell])

    for block in range(length // KEY_BLOCK):
        rows = pl.ds(block * KEY_BLOCK, KEY_BLOCK)
        tokens_t[:, rows] = tokens[rows, :].T
        cot_t[:, rows] = cot[rows, :].T
        cell = block * KEY_BLOCK // SHORT_LENGTH
        inside = block * KEY_BLOCK - cell * SHORT_LENGTH
        needed = jnp.where(is_long, block * KEY_BLOCK < running, inside < totals[cell])

        @pl.when(needed)
        def _(block=block, rows=rows):
            hot = one_hot(slot, block * KEY_BLOCK, KEY_BLOCK)
            packed[rows, :] = mm(hot, tokens[...], NN).astype(BF)


def one_hot(slot, begin, rows):
    shape = (rows, slot.shape[1])
    hit = (iota(shape, 0) + begin) == slot[0:1, :]
    return jnp.where(hit, 1.0, 0.0).astype(BF)


def prep(kind, counts, known, tokens, cot):
    length, width = tokens.shape
    return pl.pallas_call(
        prep_kernel,
        in_specs=[SMEM, SMEM, whole(1, length), whole(length, width), whole(length, width)],
        out_specs=[
            whole(width, length),
            whole(width, length),
            whole(length, width),
            whole(1, length),
            SMEM,
        ],
        out_shape=[
            jax.ShapeDtypeStruct((width, length), BF),
            jax.ShapeDtypeStruct((width, length), BF),
            jax.ShapeDtypeStruct((length, width), BF),
            jax.ShapeDtypeStruct((1, length), jnp.int32),
            jax.ShapeDtypeStruct((8,), jnp.int32),
        ],
        compiler_params=params(56),
        cost_estimate=cost(3e9, 12e6),
        name="prep",
    )(kind, counts, known, tokens, cot)


def fetch_rows(pieces, mine, target, sem, kinds=1):
    rows = pieces[0].shape[0]
    copies = []
    for index, piece in enumerate(pieces):
        owner = jnp.bitwise_xor(mine, index)
        place = pl.ds(pl.multiple_of(owner * rows, rows), rows)
        if kinds == 1:
            copies.append((piece, target.at[place, :]))
            continue
        for pair in range(PAIRS):
            for kind in range(kinds):
                come = piece.at[:, pl.ds(PAIR * (PAIRS * kind + pair), PAIR)]
                copies.append((come, target.at[place, pl.ds(PAIR * (kinds * pair + kind), PAIR)]))
    copies = [pltpu.make_async_copy(*ends, sem.at[index]) for index, ends in enumerate(copies)]
    for copy in copies:
        copy.start()
    for copy in copies:
        copy.wait()


def head_lanes(shape, head):
    lane = iota(shape, 1)
    return (lane >= HDIM * head) & (lane < HDIM * (head + 1))


def spare(head):
    return HDIM * (1 - head)


def key_side(block, head, begin, count):
    lane = iota(block.shape, 1) - spare(head)
    row = iota(block.shape, 0) + begin
    bias = jnp.where(row < count, 0.0, MASKED)
    extra = jnp.where(lane == 0, bias, jnp.where((lane > 0) & (lane < 4), 1.0, 0.0))
    return jnp.where(head_lanes(block.shape, head), block.astype(F32), extra).astype(BF)


def value_side(block, head):
    lane = iota(block.shape, 1) - spare(head)
    extra = jnp.where((lane > 0) & (lane < 4), 1.0, 0.0)
    return jnp.where(head_lanes(block.shape, head), block.astype(F32), extra).astype(BF)


def split_rows(shift):
    high = shift.astype(BF).astype(F32)
    rest = shift - high
    mid = rest.astype(BF).astype(F32)
    low = rest - mid
    shape = (16, shift.shape[1])
    row = iota(shape, 0)
    out = jnp.where(row == 0, 1.0, 0.0)
    out = jnp.where(row == 1, -high, out)
    out = jnp.where(row == 2, -mid, out)
    return jnp.where(row == 3, -low, out).astype(BF)


def query_side(target, head, rows, shift):
    other = spare(head)
    target[head, HDIM * head : HDIM * (head + 1), :] = rows
    target[head, other : other + 16, :] = split_rows(shift)
    target[head, other + 16 : other + HDIM, :] = jnp.zeros((HDIM - 16, rows.shape[1]), BF)


def walk(meta, length, body):
    @pl.when(meta[0] == 1)
    def _():
        cell_walk(meta[1], 0, 0, length, body)

    @pl.when(meta[0] != 1)
    def _():
        for cell in range(length // SHORT_LENGTH):
            cell_walk(meta[1 + cell], cell * SHORT_LENGTH, cell * SHORT_LENGTH, SHORT_LENGTH, body)


def cell_walk(count, slot_begin, query_begin, queries, body):
    rest = lax.rem(count, KEY_BLOCK)
    tail = (rest > 0) & (rest <= TAIL)
    full = count // KEY_BLOCK + jnp.where(rest > TAIL, 1, 0)
    end = slot_begin + count

    @pl.loop(0, full)
    def _(index):
        begin = pl.multiple_of(slot_begin + index * KEY_BLOCK, KEY_BLOCK)
        body(begin, KEY_BLOCK, query_begin, queries, end)

    @pl.when(tail)
    def _():
        begin = pl.multiple_of(slot_begin + full * KEY_BLOCK, KEY_BLOCK)
        body(begin, TAIL, query_begin, queries, end)


def forward_kernel(count, mine, meta, *refs):
    pieces = refs[:count]
    tokens_t, packed, slot = refs[count : count + 3]
    q_out, k_out, v_out, kc_out, vc_out, kct_out, context, log_total = refs[count + 3 : count + 11]
    weights, vct, side, total, shift, sem = refs[count + 11 :]
    step = pl.program_id(0)
    length = tokens_t.shape[1]

    @pl.when(step == 0)
    def _():
        fetch_rows(pieces, mine[0], weights, sem, 3)

    columns = pl.ds(pl.multiple_of(step * 3 * PAIR, 3 * PAIR), 3 * PAIR)
    part = weights[:, columns]
    joined = mm(part, tokens_t[...], TN)
    q_out[...] = (joined[:PAIR] * HDIM**-0.5).astype(BF)
    k_out[...] = joined[PAIR : 2 * PAIR].astype(BF)
    v_out[...] = joined[2 * PAIR :].astype(BF)

    def project(begin, rows, *_):
        place = pl.ds(begin, rows)
        both = mm(packed[place, :], part[:, PAIR:], NN).astype(BF)
        kc_out[place, :] = both[:, :PAIR]
        vc_out[place, :] = both[:, PAIR:]
        kct_out[:, place] = both[:, :PAIR].T
        turned = both[:, PAIR:].T
        ones = jnp.where(iota((16, rows), 0) == 0, 1.0, 0.0).astype(BF)
        for head in range(2):
            vct[head, :HDIM, place] = turned[HDIM * head : HDIM * (head + 1)]
            vct[head, HDIM:, place] = ones

    walk(meta, length, project)

    masked = slot[...] < 0
    own = []
    for head in range(2):
        rows = slice(HDIM * head, HDIM * (head + 1))
        queries = q_out[rows, :].astype(F32)
        keys = k_out[rows, :].astype(F32)
        own.append(jnp.where(masked, jnp.sum(queries * keys, axis=0, keepdims=True), MASKED))
        top_q = jnp.max(jnp.sum(queries * queries, axis=0, keepdims=True))
        top_k = jnp.max(jnp.sum(keys * keys, axis=0, keepdims=True))
        unsafe = jnp.logical_not(top_q * top_k < SAFE_SCORE * SAFE_SCORE)
        shift[head : head + 1, :] = jnp.zeros((1, length), F32)
        query_side(side, head, q_out[rows, :], jnp.zeros((1, length), F32))

        @pl.when(unsafe)
        def _(head=head, rows=rows):
            shift[head : head + 1, :] = own[head]

            def raise_top(begin, rows, first, queries, end):
                keys = key_side(kc_out[pl.ds(begin, rows), :], head, begin, end)
                place = pl.ds(first, queries)
                scores = mm(keys, side[head, :, place], NN)
                top = jnp.max(scores, axis=0, keepdims=True)
                shift[head : head + 1, place] = jnp.maximum(shift[head : head + 1, place], top)

            walk(meta, length, raise_top)
            query_side(side, head, q_out[rows, :], shift[head : head + 1, :])

    total[...] = jnp.zeros(total.shape, F32)

    def attend(begin, rows, first, queries, end):
        slots = pl.ds(begin, rows)
        place = pl.ds(first, queries)
        for head in range(2):
            keys = key_side(kc_out[slots, :], head, begin, end)
            raised = jnp.exp(mm(keys, side[head, :, place], NN)).astype(BF)
            total[head, :, place] += mm(vct[head, :, slots], raised, NN)

    walk(meta, length, attend)

    for head in range(2):
        rows = slice(HDIM * head, HDIM * (head + 1))
        alone = jnp.exp(own[head] - shift[head : head + 1, :])
        row_total = total[head, HDIM : HDIM + 1, :] + alone
        gathered = total[head, :HDIM, :] + v_out[rows, :].astype(F32) * alone
        context[rows, :] = (gathered / row_total).astype(BF)
        log_total[pl.ds(step * 2 + head, 1), :] = shift[head : head + 1, :] + jnp.log(row_total)


def forward(mine, meta, pieces, tokens_t, packed, slot):
    width, length = tokens_t.shape
    pair_rows = pl.BlockSpec((PAIR, length), lambda step: (step, 0))
    pair_lanes = pl.BlockSpec((length, PAIR), lambda step: (0, step))
    transposed = jax.ShapeDtypeStruct((width, length), BF)
    natural = jax.ShapeDtypeStruct((length, width), BF)
    count = len(pieces)
    return pl.pallas_call(
        partial(forward_kernel, count),
        grid=(PAIRS,),
        in_specs=[SMEM, SMEM]
        + [ANY] * count
        + [whole(width, length), whole(length, width), whole(1, length)],
        out_specs=[pair_rows] * 3 + [pair_lanes] * 2 + [pair_rows] * 2 + [whole(HEADS, length)],
        out_shape=[transposed] * 3
        + [natural] * 2
        + [transposed] * 2
        + [jax.ShapeDtypeStruct((HEADS, length), F32)],
        scratch_shapes=[
            pltpu.VMEM((width, 3 * width), BF),
            pltpu.VMEM((2, HDIM + 16, length), BF),
            pltpu.VMEM((2, PAIR, length), BF),
            pltpu.VMEM((2, HDIM + 16, length), F32),
            pltpu.VMEM((8, length), F32),
            pltpu.SemaphoreType.DMA((3 * PAIRS * count,)),
        ],
        compiler_params=params(56),
        cost_estimate=cost(15e9, 25e6, 20e6),
        name="attend_forward",
    )(mine, meta, *pieces, tokens_t, packed, slot)


def backward_kernel(pair, meta, *refs):
    q_t, k_t, v_t, kc, vc, kct, grad_context, log_total, inner, slot, tokens_t = refs[:11]
    grad_t, grad_weight = refs[11:13]
    q_side, g_side, grad_q, grad_kv, ready = refs[13:]
    length = tokens_t.shape[1]
    for head in range(2):
        rows = slice(HDIM * head, HDIM * (head + 1))
        index = 2 * pair + head
        query_side(q_side, head, q_t[rows, :], log_total[index : index + 1, :])
        query_side(g_side, head, grad_context[rows, :], inner[index : index + 1, :])
    grad_q[...] = jnp.zeros(grad_q.shape, F32)
    grad_kv[...] = jnp.zeros(grad_kv.shape, F32)

    def pull(begin, rows, first, queries, end):
        slots = pl.ds(begin, rows)
        place = pl.ds(first, queries)
        for head in range(2):
            lanes = slice(HDIM * head, HDIM * (head + 1))
            keys = key_side(kc[slots, :], head, begin, end)
            values = value_side(vc[slots, :], head)
            probs = jnp.exp(mm(keys, q_side[head, :, place], NN))
            grad_scores = (probs * mm(values, g_side[head, :, place], NN)).astype(BF)
            grad_q[lanes, place] += mm(kct[lanes, slots], grad_scores, NN)
            ready[HDIM * head : HDIM * (head + 1), :rows] = mm(
                q_t[lanes, place], grad_scores, NT
            ).astype(BF)
            ready[PAIR + HDIM * head : PAIR + HDIM * (head + 1), :rows] = mm(
                grad_context[lanes, place], probs.astype(BF), NT
            ).astype(BF)
        hit = (iota((rows, queries), 0) + begin) == slot[0:1, place]
        spread = jnp.where(hit, 1.0, 0.0).astype(BF)
        grad_kv[:, place] += mm(ready[:, :rows], spread, NN)

    walk(meta, length, pull)

    masked = slot[...] < 0
    for head in range(2):
        rows = slice(HDIM * head, HDIM * (head + 1))
        index = 2 * pair + head
        queries = q_t[rows, :].astype(F32)
        keys = k_t[rows, :].astype(F32)
        values = v_t[rows, :].astype(F32)
        grads = grad_context[rows, :].astype(F32)
        own = jnp.sum(queries * keys, axis=0, keepdims=True)
        own = jnp.where(masked, own - log_total[index : index + 1, :], MASKED)
        alone = jnp.exp(own)
        pulled = jnp.sum(grads * values, axis=0, keepdims=True) - inner[index : index + 1, :]
        pulled = (alone * pulled).astype(BF).astype(F32)
        alone = alone.astype(BF).astype(F32)
        part = (grad_q[rows, :] + keys * pulled) * HDIM**-0.5
        grad_t[HDIM * head : HDIM * (head + 1), :] = part.astype(BF)
        part = grad_kv[rows, :] + queries * pulled
        grad_t[PAIR + HDIM * head : PAIR + HDIM * (head + 1), :] = part.astype(BF)
        part = grad_kv[PAIR + HDIM * head : PAIR + HDIM * (head + 1), :] + grads * alone
        grad_t[2 * PAIR + HDIM * head : 2 * PAIR + HDIM * (head + 1), :] = part.astype(BF)
    grad_weight[...] = mm(tokens_t[...], grad_t[...], NT).astype(BF)


def backward(pair, meta, q_t, k_t, v_t, kc, vc, kct, grad_context, log_total, inner, slot, tokens_t):
    width, length = tokens_t.shape
    pair_rows = pl.BlockSpec((PAIR, length), lambda step: (pair, 0))
    pair_lanes = pl.BlockSpec((length, PAIR), lambda step: (0, pair))
    return pl.pallas_call(
        partial(backward_kernel, pair),
        grid=(1,),
        in_specs=[SMEM]
        + [pair_rows] * 3
        + [pair_lanes] * 2
        + [pair_rows] * 2
        + [whole(HEADS, length)] * 2
        + [whole(1, length), whole(width, length)],
        out_specs=[whole(3 * PAIR, length), whole(width, 3 * PAIR)],
        out_shape=[
            jax.ShapeDtypeStruct((3 * PAIR, length), BF),
            jax.ShapeDtypeStruct((width, 3 * PAIR), BF),
        ],
        scratch_shapes=[
            pltpu.VMEM((2, PAIR, length), BF),
            pltpu.VMEM((2, PAIR, length), BF),
            pltpu.VMEM((PAIR, length), F32),
            pltpu.VMEM((2 * PAIR, length), F32),
            pltpu.VMEM((2 * PAIR, KEY_BLOCK), BF),
        ],
        compiler_params=params(56),
        cost_estimate=cost(12e9, 10e6, 6e6),
        name=f"attend_backward_{pair}",
    )(meta, q_t, k_t, v_t, kc, vc, kct, grad_context, log_total, inner, slot, tokens_t)


def feature_mean(values):
    return jnp.sum(values, axis=0, keepdims=True) * (1.0 / values.shape[0])


def normalise(values):
    centred = values - feature_mean(values)
    scale = lax.rsqrt(feature_mean(centred * centred) + NORM_EPS)
    return centred * scale, scale


def pull_norm(grad, scaled, scale, gain):
    lifted = grad * gain
    return scale * (lifted - feature_mean(lifted) - scaled * feature_mean(lifted * scaled))


def lane_sums(values):
    width = 128
    out = values[:, :width]
    for begin in range(width, values.shape[1], width):
        out = out + values[:, begin : begin + width]
    return out


def dense_kernel(count, mine, *refs):
    pieces = refs[:count]
    tokens_t, context, cot_t = refs[count : count + 3]
    out, grad_context, grad_first, inner, g_proj, g_up, g_down, g_norm = refs[count + 3 : count + 11]
    weights, total, norm_total, sem = refs[count + 11 :]
    step = pl.program_id(0)
    width = tokens_t.shape[0]

    @pl.when(step == 0)
    def _():
        fetch_rows(pieces, mine[0], weights, sem)
        total[...] = jnp.zeros(total.shape, F32)
        norm_total[...] = jnp.zeros(norm_total.shape, F32)

    proj = weights[:, :width]
    up = weights[:, width : 2 * width]
    down = weights[:, 2 * width : 3 * width]
    rows = weights[:, 3 * width :].astype(F32)
    gain1, bias1, gain2, bias2 = (rows[:, index : index + 1] for index in range(4))

    context_low = context[...]
    scaled1, scale1 = normalise(tokens_t[...].astype(F32) + mm(proj, context_low, TN))
    middle = scaled1 * gain1 + bias1
    middle_low = middle.astype(BF)
    hidden = mm(up, middle_low, TN)
    cdf = 0.5 * (1.0 + lax.erf(hidden * 2.0**-0.5))
    slope = cdf + hidden * jnp.exp(hidden * hidden * -0.5) * 0.3989422804014327
    active = (hidden * cdf).astype(BF)
    scaled2, scale2 = normalise(middle + mm(down, active, TN))
    out[...] = (scaled2 * gain2 + bias2).astype(BF).T

    cot = cot_t[...].astype(F32)
    norm_total[2] += lane_sums(cot * scaled2)
    norm_total[3] += lane_sums(cot)
    grad_second = pull_norm(cot, scaled2, scale2, gain2)
    grad_low = grad_second.astype(BF)
    total[2] += mm(active, grad_low, NT)
    grad_hidden = (mm(down, grad_low, NN) * slope).astype(BF)
    total[1] += mm(middle_low, grad_hidden, NT)
    grad_middle = grad_second + mm(up, grad_hidden, NN)
    norm_total[0] += lane_sums(grad_middle * scaled1)
    norm_total[1] += lane_sums(grad_middle)
    grad_h1 = pull_norm(grad_middle, scaled1, scale1, gain1)
    grad_first[...] = grad_h1
    proj_low = grad_h1.astype(BF)
    total[0] += mm(context_low, proj_low, NT)
    pulled = mm(proj, proj_low, NN).astype(BF)
    grad_context[...] = pulled
    both = pulled.astype(F32) * context_low.astype(F32)
    for head in range(HEADS):
        part = both[HDIM * head : HDIM * (head + 1), :]
        inner[head : head + 1, :] = jnp.sum(part, axis=0, keepdims=True)

    @pl.when(step == pl.num_programs(0) - 1)
    def _():
        g_proj[...] = total[0].astype(BF)
        g_up[...] = total[1].astype(BF)
        g_down[...] = total[2].astype(BF)
        lane = iota((width, 128), 1)
        packed = jnp.zeros((width, 128), F32)
        for index in range(4):
            column = jnp.sum(norm_total[index], axis=1, keepdims=True)
            packed = jnp.where(lane == index, column, packed)
        g_norm[...] = packed


def dense(mine, pieces, tokens_t, context, cot_t):
    width, length = tokens_t.shape
    block = 512
    count = len(pieces)
    columns = pl.BlockSpec((width, block), lambda step: (0, step))
    square = jax.ShapeDtypeStruct((width, width), BF)
    return pl.pallas_call(
        partial(dense_kernel, count),
        grid=(length // block,),
        in_specs=[SMEM] + [ANY] * count + [columns] * 3,
        out_specs=[
            pl.BlockSpec((block, width), lambda step: (step, 0)),
            columns,
            columns,
            pl.BlockSpec((HEADS, block), lambda step: (0, step)),
        ]
        + [whole(width, width)] * 3
        + [whole(width, 128)],
        out_shape=[
            jax.ShapeDtypeStruct((length, width), BF),
            jax.ShapeDtypeStruct((width, length), BF),
            jax.ShapeDtypeStruct((width, length), F32),
            jax.ShapeDtypeStruct((HEADS, length), F32),
        ]
        + [square] * 3
        + [jax.ShapeDtypeStruct((width, 128), F32)],
        scratch_shapes=[
            pltpu.VMEM((width, 3 * width + 128), BF),
            pltpu.VMEM((3, width, width), F32),
            pltpu.VMEM((4, width, 128), F32),
            pltpu.SemaphoreType.DMA((count,)),
        ],
        compiler_params=params(56),
        cost_estimate=cost(10e9, 20e6, 4e6),
        name="dense",
    )(mine, *pieces, tokens_t, context, cot_t)


def input_kernel(count, mine, *refs):
    pieces = refs[:count]
    grads = refs[count : count + PAIRS]
    grad_first, out = refs[count + PAIRS : count + PAIRS + 2]
    weights, sem = refs[count + PAIRS + 2 :]

    @pl.when(pl.program_id(0) == 0)
    def _():
        fetch_rows(pieces, mine[0], weights, sem, 3)

    total = grad_first[...]
    for pair in range(PAIRS):
        total = total + mm(weights[:, 3 * PAIR * pair : 3 * PAIR * (pair + 1)], grads[pair][...], NN)
    out[...] = total.astype(BF).T


def input_side(mine, pieces, grads, grad_first):
    width, length = grad_first.shape
    block = 512
    count = len(pieces)
    return pl.pallas_call(
        partial(input_kernel, count),
        grid=(length // block,),
        in_specs=[SMEM]
        + [ANY] * count
        + [pl.BlockSpec((3 * PAIR, block), lambda step: (0, step))] * PAIRS
        + [pl.BlockSpec((width, block), lambda step: (0, step))],
        out_specs=pl.BlockSpec((block, width), lambda step: (step, 0)),
        out_shape=jax.ShapeDtypeStruct((length, width), BF),
        scratch_shapes=[
            pltpu.VMEM((width, 3 * width), BF),
            pltpu.SemaphoreType.DMA((3 * PAIRS * count,)),
        ],
        compiler_params=params(56),
        cost_estimate=cost(3.3e9, 14e6),
        name="input_side",
    )(mine, *pieces, *grads, grad_first)


def swap(value, axis, size, mask):
    return lax.ppermute(value, axis, [(index, index ^ mask) for index in range(size)])


def masks_of(size):
    return [1 << bit for bit in range(size.bit_length() - 1)]


def gather_pieces(piece, axis, size, meanwhile):
    pieces = {0: piece}
    for mask in reversed(masks_of(size)):
        for known in list(pieces):
            pieces[known ^ mask] = swap(pieces[known], axis, size, mask)
            if meanwhile is not None:
                meanwhile, pieces[mask] = lax.optimization_barrier((meanwhile, pieces[mask]))
                meanwhile = None
    return [pieces[index] for index in range(size)]


def halving(value, axis, size):
    mine = lax.axis_index(axis)
    rows = value.shape[0] // size
    value = value.reshape(size, rows, -1)
    for bit, mask in enumerate(masks_of(size)):
        value = value.reshape(value.shape[0] // 2, 2, rows, -1).swapaxes(0, 1)
        side = (mine >> bit) & 1
        send = lax.dynamic_index_in_dim(value, 1 - side, 0, keepdims=False)
        got = yield send, axis, size, mask
        keep = lax.dynamic_index_in_dim(value, side, 0, keepdims=False)
        value = (keep.astype(F32) + got.astype(F32)).astype(value.dtype)
    return value.reshape(rows, -1)


def doubling(value, axis, size):
    for mask in masks_of(size):
        got = yield value, axis, size, mask
        value = (value.astype(F32) + got.astype(F32)).astype(value.dtype)
    return value


def side_steps(value, fsdp, dp):
    value = yield from halving(value, "fsdp", fsdp)
    return (yield from doubling(value, "dp", dp))


def small_steps(value, fsdp, dp):
    value = yield from doubling(value, "fsdp", fsdp)
    return (yield from doubling(value, "dp", dp))


class Chain:
    def __init__(self, steps):
        self.steps, self.result, self.got = steps, None, None
        self.request = next(steps)

    def send(self, value):
        _, axis, size, mask = self.request
        self.got = swap(value, axis, size, mask)

    def land(self, value):
        try:
            self.request = self.steps.send(value)
        except StopIteration as end:
            self.request, self.result = None, end.value

    def finish(self):
        while self.request is not None:
            if self.got is None:
                self.send(self.request[0])
            value, self.got = self.got, None
            self.land(value)
        return self.result


def start_steps(anchor, chains):
    live = [chain for chain in chains if chain.request is not None]
    anchor, *values = lax.optimization_barrier((anchor, *(chain.request[0] for chain in live)))
    for chain, value in zip(live, values):
        chain.send(value)
    return anchor


def end_steps(anchor, chains):
    live = [chain for chain in chains if chain.got is not None]
    anchor, *values = lax.optimization_barrier((anchor, *(chain.got for chain in live)))
    for chain, value in zip(live, values):
        chain.got = None
        chain.land(value)
    return anchor


def total_by_exchange(value, axis, size):
    rows, columns = value.shape
    parts = lax.all_to_all(value, axis, 0, 0, tiled=True).reshape(size, rows // size, columns)
    mine = jnp.sum(parts.astype(F32), axis=0).astype(BF)
    return lax.all_to_all(jnp.tile(mine, (size, 1)), axis, 0, 0, tiled=True)


def moments(gradient, first_old, second_old):
    first_new = BETA * first_old + (1.0 - BETA) * gradient
    second_new = BETA * second_old + (1.0 - BETA) * gradient * gradient
    return first_new, second_new


def update_of(first_new, second_new):
    debias = 1.0 - BETA**STEP
    return first_new / debias / (jnp.sqrt(second_new / debias) + ADAM_EPS)


def square_row(values):
    total = jnp.sum(values * values, axis=0, keepdims=True)
    return lane_sums(total)


def moments_kernel(count, paired, gradient, *refs):
    olds, outs, squares = refs[: 3 * count], refs[3 * count : 5 * count], refs[5 * count]
    at = 0
    squares[...] = jnp.zeros(squares.shape, F32)
    for index in range(count):
        weight, first_old, second_old = (ref[...] for ref in olds[3 * index : 3 * index + 3])
        columns = weight.shape[1]
        if paired:
            places = [
                3 * PAIR * (PAIRS - 1 - pair) + PAIR * kind
                for kind in range(3)
                for pair in range(PAIRS)
            ]
            grad = jnp.concatenate([gradient[:, at : at + PAIR] for at in places], axis=1)
        else:
            grad = gradient[:, at : at + columns]
        grad = grad.astype(F32)
        at += columns
        first_new, second_new = moments(grad, first_old, second_old)
        outs[2 * index][...] = first_new
        outs[2 * index + 1][...] = second_new
        update = update_of(first_new, second_new) + MATRIX_DECAY * weight
        squares[index : index + 1, :] = square_row(weight)
        squares[4 + index : 5 + index, :] = square_row(update)


def new_moments(gradient, olds, paired):
    shapes = [jax.ShapeDtypeStruct(old.shape, F32) for old in olds]
    count = len(olds) // 3
    outs = [shape for shape in shapes[::3] for _ in range(2)]
    results = pl.pallas_call(
        partial(moments_kernel, count, paired),
        out_shape=outs + [jax.ShapeDtypeStruct((8, 128), F32)],
        compiler_params=params(56),
        cost_estimate=cost(5e6, 5e6),
        name="moments",
    )(gradient, *olds)
    return results[:-1], results[-1]


def apply_kernel(count, squares, *refs):
    inputs, outs, norms = refs[: 3 * count], refs[3 * count : 5 * count], refs[5 * count]
    total = jnp.sum(jnp.sum(squares[...], axis=0), axis=1, keepdims=True)
    size = jnp.sqrt(total)
    ratio = size[0:4] / size[4:8]
    lane = iota((1, 4), 1)
    rows = [jnp.zeros((1, 4), F32)] * 3
    for index in range(count):
        weight, first_new, second_new = (ref[...] for ref in inputs[3 * index : 3 * index + 3])
        update = update_of(first_new, second_new) + MATRIX_DECAY * weight
        trust = ratio[index : index + 1]
        weight = weight - MATRIX_RATE * trust * update
        outs[2 * index][...] = weight
        outs[2 * index + 1][...] = weight.astype(BF)
        for place, value in enumerate((size[index : index + 1], size[4 + index : 5 + index], trust)):
            rows[place] = jnp.where(lane == index, value, rows[place])
    for place in range(3):
        norms[place : place + 1, :] = rows[place]


def apply_updates(squares, arrays):
    count = len(arrays) // 3
    outs = []
    for weight in arrays[::3]:
        outs += [jax.ShapeDtypeStruct(weight.shape, F32), jax.ShapeDtypeStruct(weight.shape, BF)]
    results = pl.pallas_call(
        partial(apply_kernel, count),
        out_shape=outs + [jax.ShapeDtypeStruct((3, 4), F32)],
        compiler_params=params(56),
        cost_estimate=cost(5e6, 8e6),
        name="apply",
    )(squares, *arrays)
    return results[:-1], results[-1]


def shards(
    fsdp,
    dp,
    tokens,
    cotangent,
    known_genes,
    cell_kind,
    gene_counts,
    study_index,
    qkv_weight,
    qkv_first,
    qkv_second,
    proj_weight,
    proj_first,
    proj_second,
    up_weight,
    up_first,
    up_second,
    down_weight,
    down_first,
    down_second,
    norm_params,
    norm_first,
    norm_second,
):
    _, length, width = tokens.shape
    mine = lax.axis_index("fsdp").astype(jnp.int32)
    mine_ref = mine.reshape(1)

    tokens_t, cot_t, packed, slot, meta = prep(
        cell_kind, gene_counts.reshape(-1), known_genes, tokens[0], cotangent[0]
    )
    qkv_pieces = gather_pieces(qkv_weight.astype(BF), "fsdp", fsdp, slot)
    norm_columns = jnp.pad(norm_params.T, ((0, 0), (0, 124)))
    rest = jnp.concatenate([proj_weight, up_weight, down_weight, norm_columns], axis=1).astype(BF)
    *qkv_pieces, rest, slot = lax.optimization_barrier((*qkv_pieces, rest, slot))
    q_t, k_t, v_t, kc, vc, kct, context, log_total = forward(
        mine_ref, meta, qkv_pieces, tokens_t, packed, slot
    )
    rest_pieces = gather_pieces(rest, "fsdp", fsdp, q_t)
    out, grad_context, grad_first, inner, g_proj, g_up, g_down, g_norm = dense(
        mine_ref, rest_pieces, tokens_t, context, cot_t
    )

    first_cells = out.reshape(-1, SHORT_LENGTH, width)[:, 0, :].astype(F32)
    slot_index = jnp.arange(first_cells.shape[0], dtype=jnp.int32)
    used_slots = (cell_kind[0] == 0) | (slot_index == 0)
    member = (
        (study_index[0][:, None] == jnp.arange(STUDY_COUNT, dtype=jnp.int32)[None, :])
        & used_slots[:, None]
    ).astype(F32)
    counts = jnp.broadcast_to(jnp.sum(member, axis=0)[:, None], (STUDY_COUNT, width))
    sums = jnp.sum(member[:, :, None] * first_cells[:, None, :], axis=0)
    squares = jnp.sum(member[:, :, None] * (first_cells * first_cells)[:, None, :], axis=0)
    small = jnp.concatenate([counts, sums, squares, g_norm[:, :8].T], axis=0)
    small_chain = Chain(small_steps(small, fsdp, dp))
    side_chain = Chain(side_steps(jnp.concatenate([g_proj, g_up, g_down], axis=1), fsdp, dp))
    chains = [side_chain, small_chain]
    half_chains = []
    grads = []
    parts = []
    for pair in reversed(range(PAIRS)):
        meta = start_steps(meta, chains)
        grad_t, part = backward(
            pair, meta, q_t, k_t, v_t, kc, vc, kct, grad_context, log_total, inner, slot, tokens_t
        )
        part = end_steps(part, chains)
        grads.append(grad_t)
        parts.append(part)
        if len(parts) * 2 == PAIRS:
            half_chains.append(Chain(halving(jnp.concatenate(parts, axis=1), "fsdp", fsdp)))
            chains.append(half_chains[-1])
            parts = []
    mine_ref = start_steps(mine_ref, chains)
    mine_ref = end_steps(mine_ref, half_chains)
    mine_ref = start_steps(mine_ref, half_chains)
    input_grad = input_side(mine_ref, qkv_pieces, grads[::-1], grad_first)
    input_grad = end_steps(input_grad, half_chains)
    qkv_share = jnp.concatenate([chain.finish() for chain in half_chains], axis=1)
    qkv_share = total_by_exchange(qkv_share, "dp", dp)
    qkv_share = end_steps(qkv_share, chains)
    side_share = side_chain.finish()
    small = small_chain.finish()
    study_mean = small[8:16] / small[:8]
    study_var = small[16:24] / small[:8] - study_mean * study_mean
    norm_share = lax.dynamic_slice_in_dim(small[24:28], mine * (width // fsdp), width // fsdp, 1)
    norm_first, norm_second = moments(norm_share, norm_first, norm_second)
    norm_params = norm_params - VECTOR_RATE * update_of(norm_first, norm_second)

    side_old = (proj_weight, proj_first, proj_second, up_weight, up_first, up_second)
    side_old += (down_weight, down_first, down_second)
    (qkv_first, qkv_second), qkv_squares = new_moments(
        qkv_share, (qkv_weight, qkv_first, qkv_second), True
    )
    side_new, side_squares = new_moments(side_share, side_old, False)
    squares = jnp.concatenate(
        [qkv_squares[0:1], side_squares[0:3], qkv_squares[4:5], side_squares[4:7]], axis=0
    )
    squares = lax.all_gather(squares, "fsdp", axis=0)
    arrays = (qkv_weight, qkv_first, qkv_second, proj_weight, side_new[0], side_new[1])
    arrays += (up_weight, side_new[2], side_new[3], down_weight, side_new[4], side_new[5])
    applied, matrix_norms = apply_updates(squares, arrays)
    results = []
    for index in range(4):
        results += [arrays[3 * index + 1], arrays[3 * index + 2]]
        results += [applied[2 * index], applied[2 * index + 1]]
    return (
        out.reshape(tokens.shape),
        input_grad.reshape(tokens.shape),
        study_mean,
        study_var,
        *results,
        norm_first,
        norm_second,
        norm_params,
        norm_params.astype(BF),
        matrix_norms,
    )


def solution(mesh):
    whole_groups = P(("dp", "fsdp"))
    rows = P("fsdp", None)
    columns = P(None, "fsdp")
    return jax.shard_map(
        partial(shards, mesh.shape["fsdp"], mesh.shape["dp"]),
        mesh=mesh,
        in_specs=(whole_groups,) * 6 + (rows,) * 12 + (columns,) * 3,
        out_specs=(whole_groups,) * 2 + (P(), P()) + (rows,) * 16 + (columns,) * 4 + (P(),),
        check_vma=False,
    )
```

```python
from functools import partial

import jax
import jax.numpy as jnp
from jax import lax
from jax.experimental import pallas as pl
from jax.experimental.pallas import tpu as pltpu
from jax.sharding import PartitionSpec as P

HEADS = 8
HDIM = 64
SHORT_LENGTH = 512
STUDY_COUNT = 8
STEP = 5
PAIR = 2 * HDIM
PAIRS = HEADS // 2
KEY_BLOCK = 256
TAIL = 128


BETA = 0.5
ADAM_EPS = 1e-06
NORM_EPS = 1e-05
MATRIX_RATE = 0.5
VECTOR_RATE = 0.3
MATRIX_DECAY = 0.01
MASKED = -1000000000.0
SAFE_SCORE = 40.0

BF = jnp.bfloat16
F32 = jnp.float32
NN = (((1,), (0,)), ((), ()))
NT = (((1,), (1,)), ((), ()))
TN = (((0,), (0,)), ((), ()))
SMEM = pl.BlockSpec(memory_space=pltpu.SMEM)
ANY = pl.BlockSpec(memory_space=pl.ANY)


def mm(left, right, dims):
    return lax.dot_general(left, right, dims, preferred_element_type=F32)


def whole(*shape):
    return pl.BlockSpec(shape, lambda *_: (0,) * len(shape))


def params(mebibytes):
    return pltpu.CompilerParams(vmem_limit_bytes=mebibytes * 2**20)


def cost(flops, nbytes, trans=0):
    return pl.CostEstimate(flops=int(flops), bytes_accessed=int(nbytes), transcendentals=int(trans))


def iota(shape, dim):
    return lax.broadcasted_iota(jnp.int32, shape, dim)


def prep_kernel(kind, counts, known, tokens, cot, tokens_t, cot_t, packed, slot, meta):
    length = tokens.shape[0]
    cells = length // SHORT_LENGTH
    is_long = kind[0] == 1
    shape = (8, SHORT_LENGTH)
    row = iota(shape, 0)
    col = iota(shape, 1)
    given = jnp.zeros(shape, jnp.int32)
    for cell in range(cells):
        given = jnp.where(row == cell, known[0:1, pl.ds(cell * SHORT_LENGTH, SHORT_LENGTH)], given)
    limit = jnp.zeros(shape, jnp.int32)
    for cell in range(cells):
        limit = jnp.where(row == cell, counts[cell], limit)
    limit = jnp.where(is_long, counts[0] - SHORT_LENGTH * row, limit)
    first = (col == 0) & (jnp.logical_not(is_long) | (row == 0))
    usable = (col < limit) & ((given == 1) | first) & (row < cells)
    usable_f = jnp.where(usable, 1.0, 0.0)
    square = (SHORT_LENGTH, SHORT_LENGTH)
    before = jnp.where(iota(square, 0) < iota(square, 1), 1.0, 0.0).astype(BF)
    rank = mm(usable_f.astype(BF), before, NN).astype(jnp.int32)
    totals = [jnp.sum(usable_f[cell : cell + 1, :]).astype(jnp.int32) for cell in range(cells)]
    base = jnp.zeros(shape, jnp.int32)
    running = jnp.int32(0)
    for cell in range(cells):
        start = jnp.where(is_long, running, SHORT_LENGTH * cell)
        base = jnp.where(row == cell, start, base)
        running = running + totals[cell]
    place = jnp.where(usable, rank + base, -1)
    for cell in range(cells):
        slot[0:1, pl.ds(cell * SHORT_LENGTH, SHORT_LENGTH)] = place[cell : cell + 1, :]
    meta[0] = kind[0]
    for cell in range(cells):
        meta[1 + cell] = jnp.where(is_long, running if cell == 0 else 0, totals[cell])

    for block in range(length // KEY_BLOCK):
        rows = pl.ds(block * KEY_BLOCK, KEY_BLOCK)
        tokens_t[:, rows] = tokens[rows, :].T
        cot_t[:, rows] = cot[rows, :].T
        cell = block * KEY_BLOCK // SHORT_LENGTH
        inside = block * KEY_BLOCK - cell * SHORT_LENGTH
        needed = jnp.where(is_long, block * KEY_BLOCK < running, inside < totals[cell])

        @pl.when(needed)
        def _(block=block, rows=rows):
            hot = one_hot(slot, block * KEY_BLOCK, KEY_BLOCK)
            packed[rows, :] = mm(hot, tokens[...], NN).astype(BF)


def one_hot(slot, begin, rows):
    shape = (rows, slot.shape[1])
    hit = (iota(shape, 0) + begin) == slot[0:1, :]
    return jnp.where(hit, 1.0, 0.0).astype(BF)


def prep(kind, counts, known, tokens, cot):
    length, width = tokens.shape
    return pl.pallas_call(
        prep_kernel,
        in_specs=[SMEM, SMEM, whole(1, length), whole(length, width), whole(length, width)],
        out_specs=[
            whole(width, length),
            whole(width, length),
            whole(length, width),
            whole(1, length),
            SMEM,
        ],
        out_shape=[
            jax.ShapeDtypeStruct((width, length), BF),
            jax.ShapeDtypeStruct((width, length), BF),
            jax.ShapeDtypeStruct((length, width), BF),
            jax.ShapeDtypeStruct((1, length), jnp.int32),
            jax.ShapeDtypeStruct((8,), jnp.int32),
        ],
        compiler_params=params(56),
        cost_estimate=cost(3e9, 12e6),
        name="prep",
    )(kind, counts, known, tokens, cot)


def fetch_rows(pieces, mine, target, sem, kinds=1):
    rows = pieces[0].shape[0]
    copies = []
    for index, piece in enumerate(pieces):
        owner = jnp.bitwise_xor(mine, index)
        place = pl.ds(pl.multiple_of(owner * rows, rows), rows)
        if kinds == 1:
            copies.append((piece, target.at[place, :]))
            continue
        for pair in range(PAIRS):
            for kind in range(kinds):
                come = piece.at[:, pl.ds(PAIR * (PAIRS * kind + pair), PAIR)]
                copies.append((come, target.at[place, pl.ds(PAIR * (kinds * pair + kind), PAIR)]))
    copies = [pltpu.make_async_copy(*ends, sem.at[index]) for index, ends in enumerate(copies)]
    for copy in copies:
        copy.start()
    for copy in copies:
        copy.wait()


def head_lanes(shape, head):
    lane = iota(shape, 1)
    return (lane >= HDIM * head) & (lane < HDIM * (head + 1))


def spare(head):
    return HDIM * (1 - head)


def key_side(block, head, begin, count):
    lane = iota(block.shape, 1) - spare(head)
    row = iota(block.shape, 0) + begin
    bias = jnp.where(row < count, 0.0, MASKED)
    extra = jnp.where(lane == 0, bias, jnp.where((lane > 0) & (lane < 4), 1.0, 0.0))
    return jnp.where(head_lanes(block.shape, head), block.astype(F32), extra).astype(BF)


def value_side(block, head):
    lane = iota(block.shape, 1) - spare(head)
    extra = jnp.where((lane > 0) & (lane < 4), 1.0, 0.0)
    return jnp.where(head_lanes(block.shape, head), block.astype(F32), extra).astype(BF)


def split_rows(shift):
    high = shift.astype(BF).astype(F32)
    rest = shift - high
    mid = rest.astype(BF).astype(F32)
    low = rest - mid
    shape = (16, shift.shape[1])
    row = iota(shape, 0)
    out = jnp.where(row == 0, 1.0, 0.0)
    out = jnp.where(row == 1, -high, out)
    out = jnp.where(row == 2, -mid, out)
    return jnp.where(row == 3, -low, out).astype(BF)


def query_side(target, head, rows, shift):
    other = spare(head)
    target[head, HDIM * head : HDIM * (head + 1), :] = rows
    target[head, other : other + 16, :] = split_rows(shift)
    target[head, other + 16 : other + HDIM, :] = jnp.zeros((HDIM - 16, rows.shape[1]), BF)


def walk(meta, length, body):
    @pl.when(meta[0] == 1)
    def _():
        cell_walk(meta[1], 0, 0, length, body)

    @pl.when(meta[0] != 1)
    def _():
        for cell in range(length // SHORT_LENGTH):
            cell_walk(meta[1 + cell], cell * SHORT_LENGTH, cell * SHORT_LENGTH, SHORT_LENGTH, body)


def cell_walk(count, slot_begin, query_begin, queries, body):
    rest = lax.rem(count, KEY_BLOCK)
    tail = (rest > 0) & (rest <= TAIL)
    full = count // KEY_BLOCK + jnp.where(rest > TAIL, 1, 0)
    end = slot_begin + count

    @pl.loop(0, full)
    def _(index):
        begin = pl.multiple_of(slot_begin + index * KEY_BLOCK, KEY_BLOCK)
        body(begin, KEY_BLOCK, query_begin, queries, end)

    @pl.when(tail)
    def _():
        begin = pl.multiple_of(slot_begin + full * KEY_BLOCK, KEY_BLOCK)
        body(begin, TAIL, query_begin, queries, end)


def forward_kernel(count, mine, meta, *refs):
    pieces = refs[:count]
    tokens_t, packed, slot = refs[count : count + 3]
    q_out, k_out, v_out, kc_out, vc_out, kct_out, context, log_total = refs[count + 3 : count + 11]
    weights, kept_all, turned_all, vct, side, total, shift, sem = refs[count + 11 :]
    step = pl.program_id(0)
    width, length = tokens_t.shape

    @pl.when(step == 0)
    def _():
        fetch_rows(pieces, mine[0], weights, sem)

        def project(begin, rows, *_):
            place = pl.ds(begin, rows)
            both = mm(packed[place, :], weights[:, width:], NN)
            kept_all[place, :] = both.astype(BF)
            turned_all[:, place] = both.T.astype(BF)

        walk(meta, length, project)

    def here(kind):
        return pl.ds(pl.multiple_of(kind * width + step * PAIR, PAIR), PAIR)

    part = jnp.concatenate([weights[:, here(kind)] for kind in range(3)], axis=1)
    joined = mm(part, tokens_t[...], TN)
    q_out[...] = (joined[:PAIR] * HDIM**-0.5).astype(BF)
    k_out[...] = joined[PAIR : 2 * PAIR].astype(BF)
    v_out[...] = joined[2 * PAIR :].astype(BF)
    kc_out[...] = kept_all[:, here(0)]
    vc_out[...] = kept_all[:, here(1)]
    kct_out[...] = turned_all[here(0), :]
    ones = jnp.where(iota((16, length), 0) == 0, 1.0, 0.0).astype(BF)
    for head in range(2):
        begin = pl.multiple_of(width + step * PAIR + HDIM * head, HDIM)
        vct[head, :HDIM, :] = turned_all[pl.ds(begin, HDIM), :]
        vct[head, HDIM:, :] = ones

    masked = slot[...] < 0
    own = []
    for head in range(2):
        rows = slice(HDIM * head, HDIM * (head + 1))
        queries = q_out[rows, :].astype(F32)
        keys = k_out[rows, :].astype(F32)
        own.append(jnp.where(masked, jnp.sum(queries * keys, axis=0, keepdims=True), MASKED))
        top_q = jnp.max(jnp.sum(queries * queries, axis=0, keepdims=True))
        top_k = jnp.max(jnp.sum(keys * keys, axis=0, keepdims=True))
        unsafe = jnp.logical_not(top_q * top_k < SAFE_SCORE * SAFE_SCORE)
        shift[head : head + 1, :] = jnp.zeros((1, length), F32)
        query_side(side, head, q_out[rows, :], jnp.zeros((1, length), F32))

        @pl.when(unsafe)
        def _(head=head, rows=rows):
            shift[head : head + 1, :] = own[head]

            def raise_top(begin, rows, first, queries, end):
                keys = key_side(kc_out[pl.ds(begin, rows), :], head, begin, end)
                place = pl.ds(first, queries)
                scores = mm(keys, side[head, :, place], NN)
                top = jnp.max(scores, axis=0, keepdims=True)
                shift[head : head + 1, place] = jnp.maximum(shift[head : head + 1, place], top)

            walk(meta, length, raise_top)
            query_side(side, head, q_out[rows, :], shift[head : head + 1, :])

    total[...] = jnp.zeros(total.shape, F32)

    def attend(begin, rows, first, queries, end):
        slots = pl.ds(begin, rows)
        place = pl.ds(first, queries)
        for head in range(2):
            keys = key_side(kc_out[slots, :], head, begin, end)
            raised = jnp.exp(mm(keys, side[head, :, place], NN)).astype(BF)
            total[head, :, place] += mm(vct[head, :, slots], raised, NN)

    walk(meta, length, attend)

    for head in range(2):
        rows = slice(HDIM * head, HDIM * (head + 1))
        alone = jnp.exp(own[head] - shift[head : head + 1, :])
        row_total = total[head, HDIM : HDIM + 1, :] + alone
        gathered = total[head, :HDIM, :] + v_out[rows, :].astype(F32) * alone
        context[rows, :] = (gathered * (1.0 / row_total)).astype(BF)
        log_total[pl.ds(step * 2 + head, 1), :] = shift[head : head + 1, :] + jnp.log(row_total)


def forward(mine, meta, pieces, tokens_t, packed, slot):
    width, length = tokens_t.shape
    pair_rows = pl.BlockSpec((PAIR, length), lambda step: (step, 0))
    pair_lanes = pl.BlockSpec((length, PAIR), lambda step: (0, step))
    transposed = jax.ShapeDtypeStruct((width, length), BF)
    natural = jax.ShapeDtypeStruct((length, width), BF)
    count = len(pieces)
    return pl.pallas_call(
        partial(forward_kernel, count),
        grid=(PAIRS,),
        in_specs=[SMEM, SMEM]
        + [ANY] * count
        + [whole(width, length), whole(length, width), whole(1, length)],
        out_specs=[pair_rows] * 3 + [pair_lanes] * 2 + [pair_rows] * 2 + [whole(HEADS, length)],
        out_shape=[transposed] * 3
        + [natural] * 2
        + [transposed] * 2
        + [jax.ShapeDtypeStruct((HEADS, length), F32)],
        scratch_shapes=[
            pltpu.VMEM((width, 3 * width), BF),
            pltpu.VMEM((length, 2 * width), BF),
            pltpu.VMEM((2 * width, length), BF),
            pltpu.VMEM((2, HDIM + 16, length), BF),
            pltpu.VMEM((2, PAIR, length), BF),
            pltpu.VMEM((2, HDIM + 16, length), F32),
            pltpu.VMEM((8, length), F32),
            pltpu.SemaphoreType.DMA((count,)),
        ],
        compiler_params=params(56),
        cost_estimate=cost(15e9, 25e6, 20e6),
        name="attend_forward",
    )(mine, meta, *pieces, tokens_t, packed, slot)


def backward_kernel(pair, meta, *refs):
    q_t, k_t, v_t, kc, vc, kct, grad_context, log_total, inner, slot, tokens_t = refs[:11]
    grad_t, grad_weight = refs[11:13]
    q_side, g_side, grad_q, grad_kv, ready = refs[13:]
    length = tokens_t.shape[1]
    for head in range(2):
        rows = slice(HDIM * head, HDIM * (head + 1))
        index = 2 * pair + head
        query_side(q_side, head, q_t[rows, :], log_total[index : index + 1, :])
        query_side(g_side, head, grad_context[rows, :], inner[index : index + 1, :])
    grad_q[...] = jnp.zeros(grad_q.shape, F32)
    grad_kv[...] = jnp.zeros(grad_kv.shape, F32)

    def pull(begin, rows, first, queries, end):
        slots = pl.ds(begin, rows)
        place = pl.ds(first, queries)
        for head in range(2):
            lanes = slice(HDIM * head, HDIM * (head + 1))
            keys = key_side(kc[slots, :], head, begin, end)
            values = value_side(vc[slots, :], head)
            probs = jnp.exp(mm(keys, q_side[head, :, place], NN))
            grad_scores = (probs * mm(values, g_side[head, :, place], NN)).astype(BF)
            grad_q[lanes, place] += mm(kct[lanes, slots], grad_scores, NN)
            ready[HDIM * head : HDIM * (head + 1), :rows] = mm(
                q_t[lanes, place], grad_scores, NT
            ).astype(BF)
            ready[PAIR + HDIM * head : PAIR + HDIM * (head + 1), :rows] = mm(
                grad_context[lanes, place], probs.astype(BF), NT
            ).astype(BF)
        hit = (iota((rows, queries), 0) + begin) == slot[0:1, place]
        spread = jnp.where(hit, 1.0, 0.0).astype(BF)
        grad_kv[:, place] += mm(ready[:, :rows], spread, NN)

    walk(meta, length, pull)

    masked = slot[...] < 0
    for head in range(2):
        rows = slice(HDIM * head, HDIM * (head + 1))
        index = 2 * pair + head
        queries = q_t[rows, :].astype(F32)
        keys = k_t[rows, :].astype(F32)
        values = v_t[rows, :].astype(F32)
        grads = grad_context[rows, :].astype(F32)
        own = jnp.sum(queries * keys, axis=0, keepdims=True)
        own = jnp.where(masked, own - log_total[index : index + 1, :], MASKED)
        alone = jnp.exp(own)
        pulled = jnp.sum(grads * values, axis=0, keepdims=True) - inner[index : index + 1, :]
        pulled = (alone * pulled).astype(BF).astype(F32)
        alone = alone.astype(BF).astype(F32)
        part = (grad_q[rows, :] + keys * pulled) * HDIM**-0.5
        grad_t[HDIM * head : HDIM * (head + 1), :] = part.astype(BF)
        part = grad_kv[rows, :] + queries * pulled
        grad_t[PAIR + HDIM * head : PAIR + HDIM * (head + 1), :] = part.astype(BF)
        part = grad_kv[PAIR + HDIM * head : PAIR + HDIM * (head + 1), :] + grads * alone
        grad_t[2 * PAIR + HDIM * head : 2 * PAIR + HDIM * (head + 1), :] = part.astype(BF)
    grad_weight[...] = mm(tokens_t[...], grad_t[...], NT).astype(BF)


def backward(pair, meta, q_t, k_t, v_t, kc, vc, kct, grad_context, log_total, inner, slot, tokens_t):
    width, length = tokens_t.shape
    pair_rows = pl.BlockSpec((PAIR, length), lambda step: (pair, 0))
    pair_lanes = pl.BlockSpec((length, PAIR), lambda step: (0, pair))
    return pl.pallas_call(
        partial(backward_kernel, pair),
        grid=(1,),
        in_specs=[SMEM]
        + [pair_rows] * 3
        + [pair_lanes] * 2
        + [pair_rows] * 2
        + [whole(HEADS, length)] * 2
        + [whole(1, length), whole(width, length)],
        out_specs=[whole(3 * PAIR, length), whole(width, 3 * PAIR)],
        out_shape=[
            jax.ShapeDtypeStruct((3 * PAIR, length), BF),
            jax.ShapeDtypeStruct((width, 3 * PAIR), BF),
        ],
        scratch_shapes=[
            pltpu.VMEM((2, PAIR, length), BF),
            pltpu.VMEM((2, PAIR, length), BF),
            pltpu.VMEM((PAIR, length), F32),
            pltpu.VMEM((2 * PAIR, length), F32),
            pltpu.VMEM((2 * PAIR, KEY_BLOCK), BF),
        ],
        compiler_params=params(56),
        cost_estimate=cost(12e9, 10e6, 6e6),
        name=f"attend_backward_{pair}",
    )(meta, q_t, k_t, v_t, kc, vc, kct, grad_context, log_total, inner, slot, tokens_t)


def feature_mean(values):
    return jnp.sum(values, axis=0, keepdims=True) * (1.0 / values.shape[0])


def normalise(values):
    centred = values - feature_mean(values)
    scale = lax.rsqrt(feature_mean(centred * centred) + NORM_EPS)
    return centred * scale, scale


def pull_norm(grad, scaled, scale, gain):
    lifted = grad * gain
    return scale * (lifted - feature_mean(lifted) - scaled * feature_mean(lifted * scaled))


def lane_sums(values):
    width = 128
    out = values[:, :width]
    for begin in range(width, values.shape[1], width):
        out = out + values[:, begin : begin + width]
    return out


def dense_kernel(count, mine, *refs):
    pieces = refs[:count]
    tokens_t, context, cot_t = refs[count : count + 3]
    out, grad_context, grad_first, inner, g_side, g_norm = refs[count + 3 : count + 9]
    weights, total, norm_total, sem = refs[count + 9 :]
    step = pl.program_id(0)
    width = tokens_t.shape[0]

    @pl.when(step == 0)
    def _():
        fetch_rows(pieces, mine[0], weights, sem)
        total[...] = jnp.zeros(total.shape, F32)
        norm_total[...] = jnp.zeros(norm_total.shape, F32)

    proj = weights[:, :width]
    up = weights[:, width : 2 * width]
    down = weights[:, 2 * width : 3 * width]
    rows = weights[:, 3 * width :].astype(F32)
    gain1, bias1, gain2, bias2 = (rows[:, index : index + 1] for index in range(4))

    def half(place):
        context_low = context[:, place]
        first_sum = tokens_t[:, place].astype(F32) + mm(proj, context_low, TN)
        yield
        scaled1, scale1 = normalise(first_sum)
        middle = scaled1 * gain1 + bias1
        middle_low = middle.astype(BF)
        hidden = mm(up, middle_low, TN)
        yield
        cdf = 0.5 * (1.0 + lax.erf(hidden * 2.0**-0.5))
        slope = cdf + hidden * jnp.exp(hidden * hidden * -0.5) * 0.3989422804014327
        active = (hidden * cdf).astype(BF)
        second_sum = middle + mm(down, active, TN)
        yield
        scaled2, scale2 = normalise(second_sum)
        out[place, :] = (scaled2 * gain2 + bias2).astype(BF).T
        cot = cot_t[:, place].astype(F32)
        norm_total[2] += lane_sums(cot * scaled2)
        norm_total[3] += lane_sums(cot)
        grad_second = pull_norm(cot, scaled2, scale2, gain2)
        grad_low = grad_second.astype(BF)
        pulled = mm(down, grad_low, NN)
        total[2] += mm(active, grad_low, NT)
        yield
        grad_hidden = (pulled * slope).astype(BF)
        grad_middle = grad_second + mm(up, grad_hidden, NN)
        total[1] += mm(middle_low, grad_hidden, NT)
        yield
        norm_total[0] += lane_sums(grad_middle * scaled1)
        norm_total[1] += lane_sums(grad_middle)
        grad_h1 = pull_norm(grad_middle, scaled1, scale1, gain1)
        grad_first[:, place] = grad_h1
        proj_low = grad_h1.astype(BF)
        pulled = mm(proj, proj_low, NN)
        total[0] += mm(context_low, proj_low, NT)
        yield
        pulled = pulled.astype(BF)
        grad_context[:, place] = pulled
        both = pulled.astype(F32) * context_low.astype(F32)
        for head in range(HEADS):
            part = both[HDIM * head : HDIM * (head + 1), :]
            inner[head : head + 1, place] = jnp.sum(part, axis=0, keepdims=True)

    columns = tokens_t.shape[1] // 2
    halves = [half(slice(columns * index, columns * (index + 1))) for index in range(2)]
    while halves:
        halves = [stage for stage in halves if next(stage, stage) is None]

    @pl.when(step == pl.num_programs(0) - 1)
    def _():
        for index in range(3):
            g_side[:, width * index : width * (index + 1)] = total[index].astype(BF)
        lane = iota((width, 128), 1)
        packed = jnp.zeros((width, 128), F32)
        for index in range(4):
            column = jnp.sum(norm_total[index], axis=1, keepdims=True)
            packed = jnp.where(lane == index, column, packed)
        g_norm[...] = packed


def dense(mine, pieces, tokens_t, context, cot_t):
    width, length = tokens_t.shape
    block = 1024
    count = len(pieces)
    columns = pl.BlockSpec((width, block), lambda step: (0, step))
    return pl.pallas_call(
        partial(dense_kernel, count),
        grid=(length // block,),
        in_specs=[SMEM] + [ANY] * count + [columns] * 3,
        out_specs=[
            pl.BlockSpec((block, width), lambda step: (step, 0)),
            columns,
            columns,
            pl.BlockSpec((HEADS, block), lambda step: (0, step)),
        ]
        + [whole(width, 3 * width), whole(width, 128)],
        out_shape=[
            jax.ShapeDtypeStruct((length, width), BF),
            jax.ShapeDtypeStruct((width, length), BF),
            jax.ShapeDtypeStruct((width, length), F32),
            jax.ShapeDtypeStruct((HEADS, length), F32),
            jax.ShapeDtypeStruct((width, 3 * width), BF),
            jax.ShapeDtypeStruct((width, 128), F32),
        ],
        scratch_shapes=[
            pltpu.VMEM((width, 3 * width + 128), BF),
            pltpu.VMEM((3, width, width), F32),
            pltpu.VMEM((4, width, 128), F32),
            pltpu.SemaphoreType.DMA((count,)),
        ],
        compiler_params=params(56),
        cost_estimate=cost(10e9, 20e6, 4e6),
        name="dense",
    )(mine, *pieces, tokens_t, context, cot_t)


def input_kernel(count, mine, *refs):
    pieces = refs[:count]
    grads = refs[count : count + PAIRS]
    grad_first, out = refs[count + PAIRS : count + PAIRS + 2]
    weights, sem = refs[count + PAIRS + 2 :]

    @pl.when(pl.program_id(0) == 0)
    def _():
        fetch_rows(pieces, mine[0], weights, sem, 3)

    total = grad_first[...]
    for pair in range(PAIRS):
        total = total + mm(weights[:, 3 * PAIR * pair : 3 * PAIR * (pair + 1)], grads[pair][...], NN)
    out[...] = total.astype(BF).T


def input_side(mine, pieces, grads, grad_first):
    width, length = grad_first.shape
    block = 512
    count = len(pieces)
    return pl.pallas_call(
        partial(input_kernel, count),
        grid=(length // block,),
        in_specs=[SMEM]
        + [ANY] * count
        + [pl.BlockSpec((3 * PAIR, block), lambda step: (0, step))] * PAIRS
        + [pl.BlockSpec((width, block), lambda step: (0, step))],
        out_specs=pl.BlockSpec((block, width), lambda step: (step, 0)),
        out_shape=jax.ShapeDtypeStruct((length, width), BF),
        scratch_shapes=[
            pltpu.VMEM((width, 3 * width), BF),
            pltpu.SemaphoreType.DMA((3 * PAIRS * count,)),
        ],
        compiler_params=params(56),
        cost_estimate=cost(3.3e9, 14e6),
        name="input_side",
    )(mine, *pieces, *grads, grad_first)


def swap(value, axis, size, mask):
    return lax.ppermute(value, axis, [(index, index ^ mask) for index in range(size)])


def masks_of(size):
    return [1 << bit for bit in range(size.bit_length() - 1)]


def gather_pieces(piece, axis, size, meanwhile):
    pieces = {0: piece}
    for mask in reversed(masks_of(size)):
        for known in list(pieces):
            pieces[known ^ mask] = swap(pieces[known], axis, size, mask)
            if meanwhile is not None:
                meanwhile, pieces[mask] = lax.optimization_barrier((meanwhile, pieces[mask]))
                meanwhile = None
    return [pieces[index] for index in range(size)]


def halving(value, axis, size):
    mine = lax.axis_index(axis)
    rows = value.shape[0] // size
    value = value.reshape(size, rows, -1)
    for bit, mask in enumerate(masks_of(size)):
        value = value.reshape(value.shape[0] // 2, 2, rows, -1).swapaxes(0, 1)
        side = (mine >> bit) & 1
        send = lax.dynamic_index_in_dim(value, 1 - side, 0, keepdims=False)
        got = yield send, axis, size, mask
        keep = lax.dynamic_index_in_dim(value, side, 0, keepdims=False)
        value = (keep.astype(F32) + got.astype(F32)).astype(value.dtype)
    return value.reshape(rows, -1)


def doubling(value, axis, size):
    for mask in masks_of(size):
        got = yield value, axis, size, mask
        value = (value.astype(F32) + got.astype(F32)).astype(value.dtype)
    return value


def side_steps(value, fsdp, dp):
    value = yield from halving(value, "fsdp", fsdp)
    return (yield from doubling(value, "dp", dp))


def small_steps(value, fsdp, dp):
    value = yield from doubling(value, "fsdp", fsdp)
    return (yield from doubling(value, "dp", dp))


class Chain:
    def __init__(self, steps):
        self.steps, self.result, self.got = steps, None, None
        self.request = next(steps)

    def send(self, value):
        _, axis, size, mask = self.request
        self.got = swap(value, axis, size, mask)

    def land(self, value):
        try:
            self.request = self.steps.send(value)
        except StopIteration as end:
            self.request, self.result = None, end.value

    def finish(self):
        while self.request is not None:
            if self.got is None:
                self.send(self.request[0])
            value, self.got = self.got, None
            self.land(value)
        return self.result


def start_steps(anchor, chains):
    live = [chain for chain in chains if chain.request is not None]
    anchor, *values = lax.optimization_barrier((anchor, *(chain.request[0] for chain in live)))
    for chain, value in zip(live, values):
        chain.send(value)
    return anchor


def end_steps(anchor, chains):
    live = [chain for chain in chains if chain.got is not None]
    anchor, *values = lax.optimization_barrier((anchor, *(chain.got for chain in live)))
    for chain, value in zip(live, values):
        chain.got = None
        chain.land(value)
    return anchor


def total_by_exchange(value, axis, size):
    rows, columns = value.shape
    parts = lax.all_to_all(value, axis, 0, 0, tiled=True).reshape(size, rows // size, columns)
    mine = jnp.sum(parts.astype(F32), axis=0).astype(BF)
    return lax.all_to_all(jnp.tile(mine, (size, 1)), axis, 0, 0, tiled=True)


def moments(gradient, first_old, second_old):
    first_new = BETA * first_old + (1.0 - BETA) * gradient
    second_new = BETA * second_old + (1.0 - BETA) * gradient * gradient
    return first_new, second_new


def update_of(first_new, second_new):
    debias = 1.0 - BETA**STEP
    return first_new / debias / (jnp.sqrt(second_new / debias) + ADAM_EPS)


def square_row(values):
    total = jnp.sum(values * values, axis=0, keepdims=True)
    return lane_sums(total)


def moments_kernel(count, paired, gradient, *refs):
    olds, outs, squares = refs[: 3 * count], refs[3 * count : 5 * count], refs[5 * count]
    at = 0

    @pl.when(pl.program_id(0) == 0)
    def _():
        squares[...] = jnp.zeros(squares.shape, F32)

    for index in range(count):
        weight, first_old, second_old = (ref[...] for ref in olds[3 * index : 3 * index + 3])
        columns = weight.shape[1]
        if paired:
            places = [
                3 * PAIR * (PAIRS - 1 - pair) + PAIR * kind
                for kind in range(3)
                for pair in range(PAIRS)
            ]
            grad = jnp.concatenate([gradient[:, at : at + PAIR] for at in places], axis=1)
        else:
            grad = gradient[:, at : at + columns]
        grad = grad.astype(F32)
        at += columns
        first_new, second_new = moments(grad, first_old, second_old)
        outs[2 * index][...] = first_new
        outs[2 * index + 1][...] = second_new
        update = update_of(first_new, second_new) + MATRIX_DECAY * weight
        squares[index : index + 1, :] += square_row(weight)
        squares[4 + index : 5 + index, :] += square_row(update)


def row_blocks(arrays):
    rows = arrays[0].shape[0]
    steps = rows // 32 if rows % 32 == 0 else 1
    return steps, [
        pl.BlockSpec((rows // steps, array.shape[1]), lambda step: (step, 0)) for array in arrays
    ]


def new_moments(gradient, olds, paired):
    count = len(olds) // 3
    outs = [jax.ShapeDtypeStruct(old.shape, F32) for old in olds[::3] for _ in range(2)]
    steps, in_specs = row_blocks((gradient, *olds))
    results = pl.pallas_call(
        partial(moments_kernel, count, paired),
        grid=(steps,),
        in_specs=in_specs,
        out_specs=row_blocks(outs)[1] + [whole(8, 128)],
        out_shape=outs + [jax.ShapeDtypeStruct((8, 128), F32)],
        compiler_params=params(32),
        cost_estimate=cost(5e6, 5e6),
        name="moments",
    )(gradient, *olds)
    return results[:-1], results[-1]


def apply_kernel(count, squares, *refs):
    inputs, outs, norms = refs[: 3 * count], refs[3 * count : 5 * count], refs[5 * count]
    total = jnp.sum(jnp.sum(squares[...], axis=0), axis=1, keepdims=True)
    size = jnp.sqrt(total)
    ratio = size[0:4] / size[4:8]
    lane = iota((1, 4), 1)
    rows = [jnp.zeros((1, 4), F32)] * 3
    for index in range(count):
        weight, first_new, second_new = (ref[...] for ref in inputs[3 * index : 3 * index + 3])
        update = update_of(first_new, second_new) + MATRIX_DECAY * weight
        trust = ratio[index : index + 1]
        weight = weight - MATRIX_RATE * trust * update
        outs[2 * index][...] = weight
        outs[2 * index + 1][...] = weight.astype(BF)
        for place, value in enumerate((size[index : index + 1], size[4 + index : 5 + index], trust)):
            rows[place] = jnp.where(lane == index, value, rows[place])
    for place in range(3):
        norms[place : place + 1, :] = rows[place]


def apply_updates(squares, arrays):
    count = len(arrays) // 3
    outs = []
    for weight in arrays[::3]:
        outs += [jax.ShapeDtypeStruct(weight.shape, F32), jax.ShapeDtypeStruct(weight.shape, BF)]
    steps, in_specs = row_blocks(arrays)
    results = pl.pallas_call(
        partial(apply_kernel, count),
        grid=(steps,),
        in_specs=[whole(*squares.shape)] + in_specs,
        out_specs=row_blocks(outs)[1] + [whole(3, 4)],
        out_shape=outs + [jax.ShapeDtypeStruct((3, 4), F32)],
        compiler_params=params(32),
        cost_estimate=cost(5e6, 8e6),
        name="apply",
    )(squares, *arrays)
    return results[:-1], results[-1]


def shards(
    fsdp,
    dp,
    tokens,
    cotangent,
    known_genes,
    cell_kind,
    gene_counts,
    study_index,
    qkv_weight,
    qkv_first,
    qkv_second,
    proj_weight,
    proj_first,
    proj_second,
    up_weight,
    up_first,
    up_second,
    down_weight,
    down_first,
    down_second,
    norm_params,
    norm_first,
    norm_second,
):
    _, length, width = tokens.shape
    mine = lax.axis_index("fsdp").astype(jnp.int32)
    mine_ref = mine.reshape(1)

    tokens_t, cot_t, packed, slot, meta = prep(
        cell_kind, gene_counts.reshape(-1), known_genes, tokens[0], cotangent[0]
    )
    qkv_pieces = gather_pieces(qkv_weight.astype(BF), "fsdp", fsdp, slot)
    norm_columns = jnp.pad(norm_params.T, ((0, 0), (0, 124)))
    rest = jnp.concatenate([proj_weight, up_weight, down_weight, norm_columns], axis=1).astype(BF)
    *qkv_pieces, rest, slot = lax.optimization_barrier((*qkv_pieces, rest, slot))
    q_t, k_t, v_t, kc, vc, kct, context, log_total = forward(
        mine_ref, meta, qkv_pieces, tokens_t, packed, slot
    )
    rest_pieces = gather_pieces(rest, "fsdp", fsdp, q_t)
    out, grad_context, grad_first, inner, g_side, g_norm = dense(
        mine_ref, rest_pieces, tokens_t, context, cot_t
    )

    side_chain = Chain(side_steps(g_side, fsdp, dp))
    g_norm = start_steps(g_norm, [side_chain])
    first_cells = out.reshape(-1, SHORT_LENGTH, width)[:, 0, :].astype(F32)
    slot_index = jnp.arange(first_cells.shape[0], dtype=jnp.int32)
    used_slots = (cell_kind[0] == 0) | (slot_index == 0)
    member = (
        (study_index[0][:, None] == jnp.arange(STUDY_COUNT, dtype=jnp.int32)[None, :])
        & used_slots[:, None]
    ).astype(F32)
    counts = jnp.broadcast_to(jnp.sum(member, axis=0)[:, None], (STUDY_COUNT, width))
    sums = jnp.sum(member[:, :, None] * first_cells[:, None, :], axis=0)
    squares = jnp.sum(member[:, :, None] * (first_cells * first_cells)[:, None, :], axis=0)
    small = jnp.concatenate([counts, sums, squares, g_norm[:, :8].T], axis=0)
    small, meta = lax.optimization_barrier((small, meta))
    small_chain = Chain(small_steps(small, fsdp, dp))
    meta = end_steps(meta, [side_chain])
    chains = [side_chain, small_chain]
    half_chains = []
    grads = []
    parts = []
    for pair in reversed(range(PAIRS)):
        meta = start_steps(meta, chains)
        grad_t, part = backward(
            pair, meta, q_t, k_t, v_t, kc, vc, kct, grad_context, log_total, inner, slot, tokens_t
        )
        part = end_steps(part, chains)
        grads.append(grad_t)
        parts.append(part)
        if len(parts) * 2 == PAIRS:
            half_chains.append(Chain(halving(jnp.concatenate(parts, axis=1), "fsdp", fsdp)))
            chains.append(half_chains[-1])
            parts = []
    late = half_chains[-1:]
    side_share = side_chain.finish()
    side_share = start_steps(side_share, late)
    side_old = (proj_weight, proj_first, proj_second, up_weight, up_first, up_second)
    side_old += (down_weight, down_first, down_second)
    side_new, side_squares = new_moments(side_share, side_old, False)
    side_squares = end_steps(side_squares, late)
    mine_ref, side_squares = lax.optimization_barrier((mine_ref, side_squares))
    mine_ref = start_steps(mine_ref, late + [small_chain])
    input_grad = input_side(mine_ref, qkv_pieces, grads[::-1], grad_first)
    input_grad = end_steps(input_grad, late + [small_chain])
    qkv_share = jnp.concatenate([chain.finish() for chain in half_chains], axis=1)
    qkv_share = total_by_exchange(qkv_share, "dp", dp)
    small = small_chain.finish()
    study_mean = small[8:16] / small[:8]
    study_var = small[16:24] / small[:8] - study_mean * study_mean
    norm_share = lax.dynamic_slice_in_dim(small[24:28], mine * (width // fsdp), width // fsdp, 1)
    norm_first, norm_second = moments(norm_share, norm_first, norm_second)
    norm_params = norm_params - VECTOR_RATE * update_of(norm_first, norm_second)

    (qkv_first, qkv_second), qkv_squares = new_moments(
        qkv_share, (qkv_weight, qkv_first, qkv_second), True
    )
    squares = jnp.concatenate(
        [qkv_squares[0:1], side_squares[0:3], qkv_squares[4:5], side_squares[4:7]], axis=0
    )
    squares = lax.all_gather(squares, "fsdp", axis=0)
    arrays = (qkv_weight, qkv_first, qkv_second, proj_weight, side_new[0], side_new[1])
    arrays += (up_weight, side_new[2], side_new[3], down_weight, side_new[4], side_new[5])
    applied, matrix_norms = apply_updates(squares, arrays)
    results = []
    for index in range(4):
        results += [arrays[3 * index + 1], arrays[3 * index + 2]]
        results += [applied[2 * index], applied[2 * index + 1]]
    return (
        out.reshape(tokens.shape),
        input_grad.reshape(tokens.shape),
        study_mean,
        study_var,
        *results,
        norm_first,
        norm_second,
        norm_params,
        norm_params.astype(BF),
        matrix_norms,
    )


def solution(mesh):
    whole_groups = P(("dp", "fsdp"))
    rows = P("fsdp", None)
    columns = P(None, "fsdp")
    return jax.shard_map(
        partial(shards, mesh.shape["fsdp"], mesh.shape["dp"]),
        mesh=mesh,
        in_specs=(whole_groups,) * 6 + (rows,) * 12 + (columns,) * 3,
        out_specs=(whole_groups,) * 2 + (P(), P()) + (rows,) * 16 + (columns,) * 4 + (P(),),
        check_vma=False,
    )
```

```python
from functools import partial

import jax
import jax.numpy as jnp
from jax import lax
from jax.experimental import pallas as pl
from jax.experimental.pallas import tpu as pltpu
from jax.sharding import PartitionSpec as P

HEADS = 8
HDIM = 64
SHORT_LENGTH = 512
STUDY_COUNT = 8
STEP = 5
PAIR = 2 * HDIM
PAIRS = HEADS // 2
KEY_BLOCK = 256
FORWARD_WALK = 512, (128, 256)
BACKWARD_WALK = 256, (128,)


BETA = 0.5
ADAM_EPS = 1e-06
NORM_EPS = 1e-05
MATRIX_RATE = 0.5
VECTOR_RATE = 0.3
MATRIX_DECAY = 0.01
MASKED = -1000000000.0
SAFE_SCORE = 40.0

BF = jnp.bfloat16
F32 = jnp.float32
NN = (((1,), (0,)), ((), ()))
NT = (((1,), (1,)), ((), ()))
TN = (((0,), (0,)), ((), ()))
SMEM = pl.BlockSpec(memory_space=pltpu.SMEM)
ANY = pl.BlockSpec(memory_space=pl.ANY)


def mm(left, right, dims):
    return lax.dot_general(left, right, dims, preferred_element_type=F32)


def whole(*shape):
    return pl.BlockSpec(shape, lambda *_: (0,) * len(shape))


def params(mebibytes):
    return pltpu.CompilerParams(vmem_limit_bytes=mebibytes * 2**20)


def cost(flops, nbytes, trans=0):
    return pl.CostEstimate(flops=int(flops), bytes_accessed=int(nbytes), transcendentals=int(trans))


def iota(shape, dim):
    return lax.broadcasted_iota(jnp.int32, shape, dim)


def prep_kernel(kind, counts, known, tokens, tokens_t, packed, slot, meta):
    length = tokens.shape[0]
    cells = length // SHORT_LENGTH
    is_long = kind[0] == 1
    shape = (8, SHORT_LENGTH)
    row = iota(shape, 0)
    col = iota(shape, 1)
    given = jnp.zeros(shape, jnp.int32)
    for cell in range(cells):
        given = jnp.where(row == cell, known[0:1, pl.ds(cell * SHORT_LENGTH, SHORT_LENGTH)], given)
    limit = jnp.zeros(shape, jnp.int32)
    for cell in range(cells):
        limit = jnp.where(row == cell, counts[cell], limit)
    limit = jnp.where(is_long, counts[0] - SHORT_LENGTH * row, limit)
    first = (col == 0) & (jnp.logical_not(is_long) | (row == 0))
    usable = (col < limit) & ((given == 1) | first) & (row < cells)
    usable_f = jnp.where(usable, 1.0, 0.0)
    square = (SHORT_LENGTH, SHORT_LENGTH)
    before = jnp.where(iota(square, 0) < iota(square, 1), 1.0, 0.0).astype(BF)
    rank = mm(usable_f.astype(BF), before, NN).astype(jnp.int32)
    totals = [jnp.sum(usable_f[cell : cell + 1, :]).astype(jnp.int32) for cell in range(cells)]
    base = jnp.zeros(shape, jnp.int32)
    running = jnp.int32(0)
    for cell in range(cells):
        start = jnp.where(is_long, running, SHORT_LENGTH * cell)
        base = jnp.where(row == cell, start, base)
        running = running + totals[cell]
    place = jnp.where(usable, rank + base, -1)
    for cell in range(cells):
        slot[0:1, pl.ds(cell * SHORT_LENGTH, SHORT_LENGTH)] = place[cell : cell + 1, :]
    meta[0] = kind[0]
    for cell in range(cells):
        meta[1 + cell] = jnp.where(is_long, running if cell == 0 else 0, totals[cell])

    for block in range(length // KEY_BLOCK):
        rows = pl.ds(block * KEY_BLOCK, KEY_BLOCK)
        tokens_t[:, rows] = tokens[rows, :].T
        cell = block * KEY_BLOCK // SHORT_LENGTH
        inside = block * KEY_BLOCK - cell * SHORT_LENGTH
        needed = jnp.where(is_long, block * KEY_BLOCK < running, inside < totals[cell])

        @pl.when(needed)
        def _(block=block, rows=rows):
            hot = one_hot(slot, block * KEY_BLOCK, KEY_BLOCK)
            packed[rows, :] = mm(hot, tokens[...], NN).astype(BF)


def one_hot(slot, begin, rows):
    shape = (rows, slot.shape[1])
    hit = (iota(shape, 0) + begin) == slot[0:1, :]
    return jnp.where(hit, 1.0, 0.0).astype(BF)


def prep(kind, counts, known, tokens):
    length, width = tokens.shape
    return pl.pallas_call(
        prep_kernel,
        in_specs=[SMEM, SMEM, whole(1, length), whole(length, width)],
        out_specs=[
            whole(width, length),
            whole(length, width),
            whole(1, length),
            SMEM,
        ],
        out_shape=[
            jax.ShapeDtypeStruct((width, length), BF),
            jax.ShapeDtypeStruct((length, width), BF),
            jax.ShapeDtypeStruct((1, length), jnp.int32),
            jax.ShapeDtypeStruct((8,), jnp.int32),
        ],
        compiler_params=params(56),
        cost_estimate=cost(3e9, 12e6),
        name="prep",
    )(kind, counts, known, tokens)


def fetch_rows(pieces, mine, target, sem, kinds=1):
    rows = pieces[0].shape[0]
    copies = []
    for index, piece in enumerate(pieces):
        owner = jnp.bitwise_xor(mine, index)
        place = pl.ds(pl.multiple_of(owner * rows, rows), rows)
        if kinds == 1:
            copies.append((piece, target.at[place, :]))
            continue
        for pair in range(PAIRS):
            for kind in range(kinds):
                come = piece.at[:, pl.ds(PAIR * (PAIRS * kind + pair), PAIR)]
                copies.append((come, target.at[place, pl.ds(PAIR * (kinds * pair + kind), PAIR)]))
    copies = [pltpu.make_async_copy(*ends, sem.at[index]) for index, ends in enumerate(copies)]
    for copy in copies:
        copy.start()
    for copy in copies:
        copy.wait()


def head_lanes(shape, head):
    lane = iota(shape, 1)
    return (lane >= HDIM * head) & (lane < HDIM * (head + 1))


def spare(head):
    return HDIM * (1 - head)


def key_lanes(block, head, begin, count):
    lane = iota(block.shape, 1) - spare(head)
    row = iota(block.shape, 0) + begin
    bias = jnp.where(row < count, 0.0, MASKED)
    extra = jnp.where(lane == 0, bias, jnp.where((lane > 0) & (lane < 4), 1.0, 0.0))
    return jnp.where(head_lanes(block.shape, head), block.astype(F32), extra).astype(BF)


def split_rows(shift):
    high = shift.astype(BF).astype(F32)
    rest = shift - high
    mid = rest.astype(BF).astype(F32)
    low = rest - mid
    shape = (16, shift.shape[1])
    row = iota(shape, 0)
    out = jnp.where(row == 0, 1.0, 0.0)
    out = jnp.where(row == 1, -high, out)
    out = jnp.where(row == 2, -mid, out)
    return jnp.where(row == 3, -low, out).astype(BF)


def query_side(target, head, rows, shift):
    other = spare(head)
    target[head, HDIM * head : HDIM * (head + 1), :] = rows
    target[head, other : other + 16, :] = split_rows(shift)
    target[head, other + 16 : other + HDIM, :] = jnp.zeros((HDIM - 16, rows.shape[1]), BF)


def walk(meta, length, body, size, tails):
    @pl.when(meta[0] == 1)
    def _():
        cell_walk(meta[1], 0, 0, length, body, size, tails)

    @pl.when(meta[0] != 1)
    def _():
        @pl.loop(0, length // SHORT_LENGTH)
        def _(cell):
            begin = pl.multiple_of(cell * SHORT_LENGTH, SHORT_LENGTH)
            cell_walk(meta[1 + cell], begin, begin, SHORT_LENGTH, body, min(size, SHORT_LENGTH), tails)


def cell_walk(count, slot_begin, query_begin, queries, body, size, tails):
    tails = [tail for tail in tails if tail < size]
    rest = lax.rem(count, size)
    full = count // size + jnp.where(rest > tails[-1], 1, 0)
    end = slot_begin + count

    @pl.loop(0, full)
    def _(index):
        begin = pl.multiple_of(slot_begin + index * size, size)
        body(begin, size, query_begin, queries, end)

    for low, tail in zip([0] + tails, tails):

        @pl.when((rest > low) & (rest <= tail))
        def _(tail=tail):
            begin = pl.multiple_of(slot_begin + full * size, size)
            body(begin, tail, query_begin, queries, end)


def forward_kernel(count, mine, meta, *refs):
    pieces = refs[:count]
    tokens_t, packed, slot = refs[count : count + 3]
    q_out, k_out, v_out, kc_out, kct_out, vct_out, context, log_total = refs[count + 3 : count + 11]
    weights, kept_all, turned_all, vct, side, total, shift, sem = refs[count + 11 :]
    step = pl.program_id(0)
    width, length = tokens_t.shape

    @pl.when(step == 0)
    def _():
        fetch_rows(pieces, mine[0], weights, sem)

        def project(begin, rows, *_):
            place = pl.ds(begin, rows)
            both = mm(packed[place, :], weights[:, width:], NN)
            kept_all[place, :] = both[:, :width].astype(BF)
            turned_all[:, place] = both.T.astype(BF)

        walk(meta, length, project, *FORWARD_WALK)

    def here(kind):
        return pl.ds(pl.multiple_of(kind * width + step * PAIR, PAIR), PAIR)

    part = jnp.concatenate([weights[:, here(kind)] for kind in range(3)], axis=1)
    joined = mm(part, tokens_t[...], TN)
    q_out[...] = (joined[:PAIR] * HDIM**-0.5).astype(BF)
    k_out[...] = joined[PAIR : 2 * PAIR].astype(BF)
    v_out[...] = joined[2 * PAIR :].astype(BF)
    kc_out[...] = kept_all[:, here(0)]
    kct_out[...] = turned_all[here(0), :]
    vct_out[...] = turned_all[here(1), :]
    ones = jnp.where(iota((16, length), 0) == 0, 1.0, 0.0).astype(BF)
    for head in range(2):
        vct[head, :HDIM, :] = vct_out[HDIM * head : HDIM * (head + 1), :]
        vct[head, HDIM:, :] = ones

    masked = slot[...] < 0
    own = []
    for head in range(2):
        rows = slice(HDIM * head, HDIM * (head + 1))
        queries = q_out[rows, :].astype(F32)
        keys = k_out[rows, :].astype(F32)
        own.append(jnp.where(masked, jnp.sum(queries * keys, axis=0, keepdims=True), MASKED))
        top_q = jnp.max(jnp.sum(queries * queries, axis=0, keepdims=True))
        top_k = jnp.max(jnp.sum(keys * keys, axis=0, keepdims=True))
        unsafe = jnp.logical_not(top_q * top_k < SAFE_SCORE * SAFE_SCORE)
        shift[head : head + 1, :] = jnp.zeros((1, length), F32)
        query_side(side, head, q_out[rows, :], jnp.zeros((1, length), F32))

        @pl.when(unsafe)
        def _(head=head, rows=rows):
            shift[head : head + 1, :] = own[head]

            def raise_top(begin, rows, first, queries, end):
                keys = key_lanes(kc_out[pl.ds(begin, rows), :], head, begin, end)
                place = pl.ds(first, queries)
                scores = mm(keys, side[head, :, place], NN)
                top = jnp.max(scores, axis=0, keepdims=True)
                shift[head : head + 1, place] = jnp.maximum(shift[head : head + 1, place], top)

            walk(meta, length, raise_top, *FORWARD_WALK)
            query_side(side, head, q_out[rows, :], shift[head : head + 1, :])

    total[...] = jnp.zeros(total.shape, F32)

    def attend(begin, rows, first, queries, end):
        slots = pl.ds(begin, rows)
        place = pl.ds(first, queries)
        for head in range(2):
            keys = key_lanes(kc_out[slots, :], head, begin, end)
            raised = jnp.exp(mm(keys, side[head, :, place], NN)).astype(BF)
            total[head, :, place] += mm(vct[head, :, slots], raised, NN)

    walk(meta, length, attend, *FORWARD_WALK)

    for head in range(2):
        rows = slice(HDIM * head, HDIM * (head + 1))
        alone = jnp.exp(own[head] - shift[head : head + 1, :])
        row_total = total[head, HDIM : HDIM + 1, :] + alone
        gathered = total[head, :HDIM, :] + v_out[rows, :].astype(F32) * alone
        context[rows, :] = (gathered * (1.0 / row_total)).astype(BF)
        log_total[pl.ds(step * 2 + head, 1), :] = shift[head : head + 1, :] + jnp.log(row_total)


def forward(mine, meta, pieces, tokens_t, packed, slot):
    width, length = tokens_t.shape
    pair_rows = pl.BlockSpec((PAIR, length), lambda step: (step, 0))
    pair_lanes = pl.BlockSpec((length, PAIR), lambda step: (0, step))
    transposed = jax.ShapeDtypeStruct((width, length), BF)
    natural = jax.ShapeDtypeStruct((length, width), BF)
    count = len(pieces)
    return pl.pallas_call(
        partial(forward_kernel, count),
        grid=(PAIRS,),
        in_specs=[SMEM, SMEM]
        + [ANY] * count
        + [whole(width, length), whole(length, width), whole(1, length)],
        out_specs=[pair_rows] * 3 + [pair_lanes] + [pair_rows] * 3 + [whole(HEADS, length)],
        out_shape=[transposed] * 3
        + [natural]
        + [transposed] * 3
        + [jax.ShapeDtypeStruct((HEADS, length), F32)],
        scratch_shapes=[
            pltpu.VMEM((width, 3 * width), BF),
            pltpu.VMEM((length, width), BF),
            pltpu.VMEM((2 * width, length), BF),
            pltpu.VMEM((2, HDIM + 16, length), BF),
            pltpu.VMEM((2, PAIR, length), BF),
            pltpu.VMEM((2, HDIM + 16, length), F32),
            pltpu.VMEM((8, length), F32),
            pltpu.SemaphoreType.DMA((count,)),
        ],
        compiler_params=params(56),
        cost_estimate=cost(15e9, 25e6, 20e6),
        name="attend_forward",
    )(mine, meta, *pieces, tokens_t, packed, slot)


def backward_kernel(owners, pair_ref, mine, meta, *refs):
    pair = pair_ref[0]
    q_t, kc, kct, vct, grad_context, log_total, inner, slot, k_far, v_far, tokens_far = refs[:11]
    before = refs[11:-14]
    grad_far, keep, send = refs[-14:-11]
    turned_side, q_side, g_side, grad_q, grad_kv, ready, k_t, v_t, tokens_t, grad_t, sem = refs[-11:]
    length = q_t.shape[1]
    rows = pl.ds(pl.multiple_of(PAIR * pair, PAIR), PAIR)
    come = [
        pltpu.make_async_copy(k_far.at[rows, :], k_t, sem.at[0]),
        pltpu.make_async_copy(v_far.at[rows, :], v_t, sem.at[1]),
        pltpu.make_async_copy(tokens_far, tokens_t, sem.at[2]),
    ]
    for index, (part, target) in enumerate(zip(before, (keep, send))):
        target = target.at[:, pl.ds(0, part.shape[1])]
        come.append(pltpu.make_async_copy(part, target, sem.at[4 + index]))
    for copy in come:
        copy.start()

    for head in range(2):
        lanes = slice(HDIM * head, HDIM * (head + 1))
        index = 2 * pair + head
        query_side(turned_side, head, q_t[lanes, :], log_total[pl.ds(index, 1), :])
        q_side[head] = turned_side[head].T
        query_side(turned_side, head, grad_context[lanes, :], inner[pl.ds(index, 1), :])
        g_side[head] = turned_side[head].T
    grad_q[...] = jnp.zeros(grad_q.shape, F32)
    grad_kv[...] = jnp.zeros(grad_kv.shape, F32)
    ready[...] = jnp.zeros(ready.shape, BF)

    def pull(begin, count, first, queries, end):
        slots = pl.ds(begin, count)
        place = pl.ds(first, queries)
        keys = kc[slots, :]
        for head in range(2):
            lanes = slice(HDIM * head, HDIM * (head + 1))
            key_rows = key_side(kct[lanes, slots], head, begin, end)
            value_rows = key_side(vct[lanes, slots], head, begin, None)
            probs = jnp.exp(mm(q_side[head, place, :], key_rows, NN))
            pulled = mm(g_side[head, place, :], value_rows, NN)
            grad_scores = (probs * pulled).astype(BF)
            own_keys = jnp.where(head_lanes(keys.shape, head), keys.astype(F32), 0.0).astype(BF)
            grad_q[place, :] += mm(grad_scores, own_keys, NN)
            ready[lanes, slots] = mm(q_t[lanes, place], grad_scores, NN).astype(BF)
            ready[PAIR + HDIM * head : PAIR + HDIM * (head + 1), slots] = mm(
                grad_context[lanes, place], probs.astype(BF), NN
            ).astype(BF)

    walk(meta, length, pull, *BACKWARD_WALK)

    def scatter(begin, count, first, queries, end):
        slots = pl.ds(begin, count)
        place = pl.ds(first, queries)
        hit = (iota((count, queries), 0) + begin) == slot[0:1, place]
        spread = jnp.where(hit, 1.0, 0.0).astype(BF)
        grad_kv[:, place] += mm(ready[:, slots], spread, NN)

    walk(meta, length, scatter, *FORWARD_WALK)

    for copy in come:
        copy.wait()
    masked = slot[...] < 0
    turned = grad_q[...].T
    for head in range(2):
        lanes = slice(HDIM * head, HDIM * (head + 1))
        index = 2 * pair + head
        queries = q_t[lanes, :].astype(F32)
        keys = k_t[lanes, :].astype(F32)
        values = v_t[lanes, :].astype(F32)
        grads = grad_context[lanes, :].astype(F32)
        own = jnp.sum(queries * keys, axis=0, keepdims=True)
        own = jnp.where(masked, own - log_total[pl.ds(index, 1), :], MASKED)
        alone = jnp.exp(own)
        pulled = jnp.sum(grads * values, axis=0, keepdims=True) - inner[pl.ds(index, 1), :]
        pulled = (alone * pulled).astype(BF).astype(F32)
        alone = alone.astype(BF).astype(F32)
        part = (turned[lanes, :] + keys * pulled) * HDIM**-0.5
        grad_t[HDIM * head : HDIM * (head + 1), :] = part.astype(BF)
        part = grad_kv[lanes, :] + queries * pulled
        grad_t[PAIR + HDIM * head : PAIR + HDIM * (head + 1), :] = part.astype(BF)
        part = grad_kv[PAIR + HDIM * head : PAIR + HDIM * (head + 1), :] + grads * alone
        grad_t[2 * PAIR + HDIM * head : 2 * PAIR + HDIM * (head + 1), :] = part.astype(BF)
    leave = pltpu.make_async_copy(grad_t, grad_far, sem.at[3])
    leave.start()
    take_apart([mm(tokens_t[...], grad_t[...], NT)], mine[0], keep, send, owners)
    leave.wait()


def key_side(rows, head, begin, end):
    shape = (16, rows.shape[1])
    row = iota(shape, 0)
    extra = jnp.where((row > 0) & (row < 4), 1.0, 0.0)
    if end is not None:
        bias = jnp.where(iota(shape, 1) + begin < end, 0.0, MASKED)
        extra = jnp.where(row == 0, bias, extra)
    blank = jnp.zeros((HDIM - 16, rows.shape[1]), BF)
    extra = [extra.astype(BF), blank]
    return jnp.concatenate([rows] + extra if head == 0 else extra + [rows], axis=0)


def backward(
    pair, mine, owners, before, meta, q_t, k_t, v_t, kc, kct, vct, grad_context, log_total, inner,
    slot, tokens_t,
):
    width, length = tokens_t.shape
    pair_rows = pl.BlockSpec((PAIR, length), lambda step, place: (place[0], 0))
    pair_lanes = pl.BlockSpec((length, PAIR), lambda step, place: (0, place[0]))
    columns = 3 * PAIR + (before[0].shape[1] if before else 0)
    half = jax.ShapeDtypeStruct((width // 2, columns), BF)
    return pl.pallas_call(
        partial(backward_kernel, owners),
        grid_spec=pltpu.PrefetchScalarGridSpec(
            num_scalar_prefetch=1,
            grid=(1,),
            in_specs=[SMEM, SMEM, pair_rows, pair_lanes]
            + [pair_rows] * 3
            + [whole(HEADS, length)] * 2
            + [whole(1, length)]
            + [ANY] * (3 + len(before)),
            out_specs=[ANY] + [whole(*half.shape)] * 2,
            scratch_shapes=[
                pltpu.VMEM((2, PAIR, length), BF),
                pltpu.VMEM((2, length, PAIR), BF),
                pltpu.VMEM((2, length, PAIR), BF),
                pltpu.VMEM((length, PAIR), F32),
                pltpu.VMEM((2 * PAIR, length), F32),
                pltpu.VMEM((2 * PAIR, length), BF),
                pltpu.VMEM((PAIR, length), BF),
                pltpu.VMEM((PAIR, length), BF),
                pltpu.VMEM((width, length), BF),
                pltpu.VMEM((3 * PAIR, length), BF),
                pltpu.SemaphoreType.DMA((6,)),
            ],
        ),
        out_shape=[jax.ShapeDtypeStruct((3 * PAIR, length), BF), half, half],
        compiler_params=params(56),
        cost_estimate=cost(12e9, 10e6, 6e6),
        name="attend_backward",
    )(
        jnp.full((1,), pair, jnp.int32), mine, meta, q_t, kc, kct, vct, grad_context, log_total,
        inner, slot, k_t, v_t, tokens_t, *before,
    )


def feature_mean(values):
    return jnp.sum(values, axis=0, keepdims=True) * (1.0 / values.shape[0])


def normalise(values):
    centred = values - feature_mean(values)
    scale = lax.rsqrt(feature_mean(centred * centred) + NORM_EPS)
    return centred * scale, scale


def pull_norm(grad, scaled, scale, gain):
    lifted = grad * gain
    return scale * (lifted - feature_mean(lifted) - scaled * feature_mean(lifted * scaled))


def lane_sums(values):
    width = 128
    out = values[:, :width]
    for begin in range(width, values.shape[1], width):
        out = out + values[:, begin : begin + width]
    return out


def dense_kernel(count, mine, kind, study, *refs):
    pieces = refs[:count]
    tokens_t, context, cot_far = refs[count : count + 3]
    out, grad_context, grad_first, inner, keep, send, small = refs[count + 3 : count + 10]
    weights, total, norm_total, firsts, sem = refs[count + 10 :]
    step = pl.program_id(0)
    width = tokens_t.shape[0]

    @pl.when(step == 0)
    def _():
        fetch_rows(pieces, mine[0], weights, sem)
        total[...] = jnp.zeros(total.shape, F32)
        norm_total[...] = jnp.zeros(norm_total.shape, F32)

    proj = weights[:, :width]
    up = weights[:, width : 2 * width]
    down = weights[:, 2 * width : 3 * width]
    rows = weights[:, 3 * width :].astype(F32)
    gain1, bias1, gain2, bias2 = (rows[:, index : index + 1] for index in range(4))

    def half(place):
        context_low = context[:, place]
        first_sum = tokens_t[:, place].astype(F32) + mm(proj, context_low, TN)
        yield
        scaled1, scale1 = normalise(first_sum)
        middle = scaled1 * gain1 + bias1
        middle_low = middle.astype(BF)
        hidden = mm(up, middle_low, TN)
        yield
        cdf = 0.5 * (1.0 + lax.erf(hidden * 2.0**-0.5))
        slope = cdf + hidden * jnp.exp(hidden * hidden * -0.5) * 0.3989422804014327
        active = (hidden * cdf).astype(BF)
        second_sum = middle + mm(down, active, TN)
        yield
        scaled2, scale2 = normalise(second_sum)
        result = (scaled2 * gain2 + bias2).astype(BF).T
        out[place, :] = result
        firsts[pl.ds(2 * step + place.start // columns, 1), :] = result[:8].astype(F32)[0:1]
        cot = cot_far[place, :].T.astype(F32)
        norm_total[2] += lane_sums(cot * scaled2)
        norm_total[3] += lane_sums(cot)
        grad_second = pull_norm(cot, scaled2, scale2, gain2)
        grad_low = grad_second.astype(BF)
        pulled = mm(down, grad_low, NN)
        total[2] += mm(active, grad_low, NT)
        yield
        grad_hidden = (pulled * slope).astype(BF)
        grad_middle = grad_second + mm(up, grad_hidden, NN)
        total[1] += mm(middle_low, grad_hidden, NT)
        yield
        norm_total[0] += lane_sums(grad_middle * scaled1)
        norm_total[1] += lane_sums(grad_middle)
        grad_h1 = pull_norm(grad_middle, scaled1, scale1, gain1)
        proj_low = grad_h1.astype(BF)
        grad_first[:, place] = proj_low
        pulled = mm(proj, proj_low, NN)
        total[0] += mm(context_low, proj_low, NT)
        yield
        pulled = pulled.astype(BF)
        grad_context[:, place] = pulled
        both = pulled.astype(F32) * context_low.astype(F32)
        for head in range(HEADS):
            part = both[HDIM * head : HDIM * (head + 1), :]
            inner[head : head + 1, place] = jnp.sum(part, axis=0, keepdims=True)

    columns = tokens_t.shape[1] // 2
    halves = [half(slice(columns * index, columns * (index + 1))) for index in range(2)]
    while halves:
        halves = [stage for stage in halves if next(stage, stage) is None]

    @pl.when(step == pl.num_programs(0) - 1)
    def _():
        take_apart([total.at[index] for index in range(3)], mine[0], keep, send, count)
        lane = iota((width, 128), 1)
        packed = jnp.zeros((width, 128), F32)
        for index in range(4):
            column = jnp.sum(norm_total[index], axis=1, keepdims=True)
            packed = jnp.where(lane == index, column, packed)
        row = iota((STUDY_COUNT, width), 0)
        sums = [jnp.zeros((STUDY_COUNT, width), F32)] * 3
        for cell in range(firsts.shape[0]):
            hit = (row == study[cell]) & ((kind[0] == 0) | (cell == 0))
            first = firsts[cell : cell + 1, :]
            for index, term in enumerate((1.0, first, first * first)):
                sums[index] = sums[index] + jnp.where(hit, term, 0.0)
        for index in range(3):
            small[STUDY_COUNT * index : STUDY_COUNT * (index + 1), :] = sums[index]
        small[3 * STUDY_COUNT :, :] = packed.T[:8]


def take_apart(totals, mine, keep, send, owners):
    first = lax.rem(mine, 2) == 0
    at = keep.shape[1] - sum(total.shape[1] for total in totals)
    for total in totals:
        rows, columns = total.shape[0] // owners, total.shape[1]
        for half in range(owners // 2):
            even = total[2 * half * rows : (2 * half + 1) * rows, :].astype(BF)
            odd = total[(2 * half + 1) * rows : (2 * half + 2) * rows, :].astype(BF)
            here = slice(half * rows, (half + 1) * rows)
            keep[here, at : at + columns] = jnp.where(first, even, odd)
            send[here, at : at + columns] = jnp.where(first, odd, even)
        at += columns


def dense(mine, kind, study, pieces, tokens_t, context, cot):
    width, length = tokens_t.shape
    block = 2 * SHORT_LENGTH
    count = len(pieces)
    columns = pl.BlockSpec((width, block), lambda step: (0, step))
    rows = pl.BlockSpec((block, width), lambda step: (step, 0))
    return pl.pallas_call(
        partial(dense_kernel, count),
        grid=(length // block,),
        in_specs=[SMEM] * 3 + [ANY] * count + [columns, columns, rows],
        out_specs=[
            rows,
            columns,
            columns,
            pl.BlockSpec((HEADS, block), lambda step: (0, step)),
            whole(width // 2, 3 * width),
            whole(width // 2, 3 * width),
            whole(4 * STUDY_COUNT, width),
        ],
        out_shape=[
            jax.ShapeDtypeStruct((length, width), BF),
            jax.ShapeDtypeStruct((width, length), BF),
            jax.ShapeDtypeStruct((width, length), BF),
            jax.ShapeDtypeStruct((HEADS, length), F32),
            jax.ShapeDtypeStruct((width // 2, 3 * width), BF),
            jax.ShapeDtypeStruct((width // 2, 3 * width), BF),
            jax.ShapeDtypeStruct((4 * STUDY_COUNT, width), F32),
        ],
        scratch_shapes=[
            pltpu.VMEM((width, 3 * width + 128), BF),
            pltpu.VMEM((3, width, width), F32),
            pltpu.VMEM((4, width, 128), F32),
            pltpu.VMEM((length // SHORT_LENGTH, width), F32),
            pltpu.SemaphoreType.DMA((count,)),
        ],
        compiler_params=params(56),
        cost_estimate=cost(10e9, 20e6, 4e6),
        name="dense",
    )(mine, kind, study, *pieces, tokens_t, context, cot)


def input_kernel(count, mine, *refs):
    pieces = refs[:count]
    grads = refs[count : count + PAIRS]
    grad_first, out = refs[count + PAIRS : count + PAIRS + 2]
    weights, sem = refs[count + PAIRS + 2 :]

    @pl.when(pl.program_id(0) == 0)
    def _():
        fetch_rows(pieces, mine[0], weights, sem, 3)

    total = grad_first[...].T.astype(F32)
    for pair in range(PAIRS):
        part = weights[:, 3 * PAIR * pair : 3 * PAIR * (pair + 1)]
        total = total + mm(grads[pair][...], part, (((0,), (1,)), ((), ())))
    out[...] = total.astype(BF)


def input_side(mine, pieces, grads, grad_first):
    width, length = grad_first.shape
    block = 512
    count = len(pieces)
    return pl.pallas_call(
        partial(input_kernel, count),
        grid=(length // block,),
        in_specs=[SMEM]
        + [ANY] * count
        + [pl.BlockSpec((3 * PAIR, block), lambda step: (0, step))] * PAIRS
        + [pl.BlockSpec((width, block), lambda step: (0, step))],
        out_specs=pl.BlockSpec((block, width), lambda step: (step, 0)),
        out_shape=jax.ShapeDtypeStruct((length, width), BF),
        scratch_shapes=[
            pltpu.VMEM((width, 3 * width), BF),
            pltpu.SemaphoreType.DMA((3 * PAIRS * count,)),
        ],
        compiler_params=params(56),
        cost_estimate=cost(3.3e9, 14e6),
        name="input_side",
    )(mine, *pieces, *grads, grad_first)


def swap(value, axis, size, mask):
    return lax.ppermute(value, axis, [(index, index ^ mask) for index in range(size)])


def masks_of(size):
    return [1 << bit for bit in range(size.bit_length() - 1)]


def gather_pieces(piece, axis, size, meanwhile):
    pieces = {0: piece}
    for mask in reversed(masks_of(size)):
        for known in list(pieces):
            pieces[known ^ mask] = swap(pieces[known], axis, size, mask)
            if meanwhile is not None:
                meanwhile, pieces[mask] = lax.optimization_barrier((meanwhile, pieces[mask]))
                meanwhile = None
    return [pieces[index] for index in range(size)]


def gather_direct(piece, axis, size):
    return [piece] + [swap(piece, axis, size, mask) for mask in range(1, size)]


def halving(keep, send, axis, size):
    mine = lax.axis_index(axis)
    rows = 2 * keep.shape[0] // size
    got = yield send, axis, size, 1
    value = (keep.astype(F32) + got.astype(F32)).astype(BF).reshape(size // 2, rows, -1)
    for bit, mask in list(enumerate(masks_of(size)))[1:]:
        value = value.reshape(value.shape[0] // 2, 2, rows, -1).swapaxes(0, 1)
        side = (mine >> bit) & 1
        send = lax.dynamic_index_in_dim(value, 1 - side, 0, keepdims=False)
        got = yield send, axis, size, mask
        keep = lax.dynamic_index_in_dim(value, side, 0, keepdims=False)
        value = (keep.astype(F32) + got.astype(F32)).astype(value.dtype)
    return value.reshape(rows, -1)


def doubling(value, axis, size):
    for mask in masks_of(size):
        got = yield value, axis, size, mask
        value = (value.astype(F32) + got.astype(F32)).astype(value.dtype)
    return value


def side_steps(keep, send, fsdp, dp):
    value = yield from halving(keep, send, "fsdp", fsdp)
    return (yield from doubling(value, "dp", dp))


def small_steps(value, fsdp, dp):
    value = yield from doubling(value, "fsdp", fsdp)
    return (yield from doubling(value, "dp", dp))


class Chain:
    def __init__(self, steps):
        self.steps, self.result, self.got = steps, None, None
        self.request = next(steps)

    def send(self, value):
        _, axis, size, mask = self.request
        self.got = swap(value, axis, size, mask)

    def land(self, value):
        try:
            self.request = self.steps.send(value)
        except StopIteration as end:
            self.request, self.result = None, end.value

    def finish(self):
        while self.request is not None:
            if self.got is None:
                self.send(self.request[0])
            value, self.got = self.got, None
            self.land(value)
        return self.result


def start_steps(anchor, chains):
    live = [chain for chain in chains if chain.request is not None]
    anchor, *values = lax.optimization_barrier((anchor, *(chain.request[0] for chain in live)))
    for chain, value in zip(live, values):
        chain.send(value)
    return anchor


def end_steps(anchor, chains):
    live = [chain for chain in chains if chain.got is not None]
    anchor, *values = lax.optimization_barrier((anchor, *(chain.got for chain in live)))
    for chain, value in zip(live, values):
        chain.got = None
        chain.land(value)
    return anchor


def spread_kernel(parts, out):
    total = jnp.sum(parts[...].astype(F32), axis=0).astype(BF)
    for index in range(out.shape[0]):
        out[index] = total


def total_by_exchange(value, axis, size):
    rows, columns = value.shape
    parts = lax.all_to_all(value, axis, 0, 0, tiled=True).reshape(size, rows // size, columns)
    parts = pl.pallas_call(
        spread_kernel,
        out_shape=jax.ShapeDtypeStruct(parts.shape, BF),
        cost_estimate=cost(1e6, 1e6),
        name="spread",
    )(parts)
    return lax.all_to_all(parts.reshape(rows, columns), axis, 0, 0, tiled=True)


def moments(gradient, first_old, second_old):
    first_new = BETA * first_old + (1.0 - BETA) * gradient
    second_new = BETA * second_old + (1.0 - BETA) * gradient * gradient
    return first_new, second_new


def update_of(first_new, second_new):
    debias = 1.0 - BETA**STEP
    return first_new / debias / (jnp.sqrt(second_new / debias) + ADAM_EPS)


def square_row(values):
    total = jnp.sum(values * values, axis=0, keepdims=True)
    return lane_sums(total)


def moments_kernel(count, paired, gradient, *refs):
    olds, outs, squares = refs[: 3 * count], refs[3 * count : 5 * count], refs[5 * count]
    at = 0

    @pl.when(pl.program_id(0) == 0)
    def _():
        squares[...] = jnp.zeros(squares.shape, F32)

    for index in range(count):
        weight, first_old, second_old = (ref[...] for ref in olds[3 * index : 3 * index + 3])
        columns = weight.shape[1]
        if paired:
            places = [
                3 * PAIR * (PAIRS - 1 - pair) + PAIR * kind
                for kind in range(3)
                for pair in range(PAIRS)
            ]
            grad = jnp.concatenate([gradient[:, at : at + PAIR] for at in places], axis=1)
        else:
            grad = gradient[:, at : at + columns]
        grad = grad.astype(F32)
        at += columns
        first_new, second_new = moments(grad, first_old, second_old)
        outs[2 * index][...] = first_new
        outs[2 * index + 1][...] = second_new
        update = update_of(first_new, second_new) + MATRIX_DECAY * weight
        squares[index : index + 1, :] += square_row(weight)
        squares[4 + index : 5 + index, :] += square_row(update)


def row_blocks(arrays):
    rows = arrays[0].shape[0]
    steps = rows // 32 if rows % 32 == 0 else 1
    return steps, [
        pl.BlockSpec((rows // steps, array.shape[1]), lambda step: (step, 0)) for array in arrays
    ]


def new_moments(gradient, olds, paired):
    count = len(olds) // 3
    outs = [jax.ShapeDtypeStruct(old.shape, F32) for old in olds[::3] for _ in range(2)]
    steps, in_specs = row_blocks((gradient, *olds))
    results = pl.pallas_call(
        partial(moments_kernel, count, paired),
        grid=(steps,),
        in_specs=in_specs,
        out_specs=row_blocks(outs)[1] + [whole(8, 128)],
        out_shape=outs + [jax.ShapeDtypeStruct((8, 128), F32)],
        compiler_params=params(32),
        cost_estimate=cost(5e6, 5e6),
        name="moments",
    )(gradient, *olds)
    return results[:-1], results[-1]


def apply_kernel(count, squares, *refs):
    inputs, outs, norms = refs[: 3 * count], refs[3 * count : 5 * count], refs[5 * count]
    total = jnp.sum(jnp.sum(squares[...], axis=0), axis=1, keepdims=True)
    size = jnp.sqrt(total)
    ratio = size[0:4] / size[4:8]
    lane = iota((1, 4), 1)
    rows = [jnp.zeros((1, 4), F32)] * 3
    for index in range(count):
        weight, first_new, second_new = (ref[...] for ref in inputs[3 * index : 3 * index + 3])
        update = update_of(first_new, second_new) + MATRIX_DECAY * weight
        trust = ratio[index : index + 1]
        weight = weight - MATRIX_RATE * trust * update
        outs[2 * index][...] = weight
        outs[2 * index + 1][...] = weight.astype(BF)
        for place, value in enumerate((size[index : index + 1], size[4 + index : 5 + index], trust)):
            rows[place] = jnp.where(lane == index, value, rows[place])
    for place in range(3):
        norms[place : place + 1, :] = rows[place]


def apply_updates(squares, arrays):
    count = len(arrays) // 3
    outs = []
    for weight in arrays[::3]:
        outs += [jax.ShapeDtypeStruct(weight.shape, F32), jax.ShapeDtypeStruct(weight.shape, BF)]
    steps, in_specs = row_blocks(arrays)
    results = pl.pallas_call(
        partial(apply_kernel, count),
        grid=(steps,),
        in_specs=[whole(*squares.shape)] + in_specs,
        out_specs=row_blocks(outs)[1] + [whole(3, 4)],
        out_shape=outs + [jax.ShapeDtypeStruct((3, 4), F32)],
        compiler_params=params(32),
        cost_estimate=cost(5e6, 8e6),
        name="apply",
    )(squares, *arrays)
    return results[:-1], results[-1]


def shards(
    fsdp,
    dp,
    tokens,
    cotangent,
    known_genes,
    cell_kind,
    gene_counts,
    study_index,
    qkv_weight,
    qkv_first,
    qkv_second,
    proj_weight,
    proj_first,
    proj_second,
    up_weight,
    up_first,
    up_second,
    down_weight,
    down_first,
    down_second,
    norm_params,
    norm_first,
    norm_second,
):
    _, length, width = tokens.shape
    mine = lax.axis_index("fsdp").astype(jnp.int32)
    mine_ref = mine.reshape(1)

    tokens_t, packed, slot, meta = prep(
        cell_kind, gene_counts.reshape(-1), known_genes, tokens[0]
    )
    qkv_pieces = gather_pieces(qkv_weight.astype(BF), "fsdp", fsdp, slot)
    norm_columns = jnp.pad(norm_params.T, ((0, 0), (0, 124)))
    rest = jnp.concatenate([proj_weight, up_weight, down_weight, norm_columns], axis=1).astype(BF)
    *qkv_pieces, rest, slot = lax.optimization_barrier((*qkv_pieces, rest, slot))
    q_t, k_t, v_t, kc, kct, vct, context, log_total = forward(
        mine_ref, meta, qkv_pieces, tokens_t, packed, slot
    )
    rest_pieces = gather_direct(rest, "fsdp", fsdp)
    *rest_pieces, context = lax.optimization_barrier((*rest_pieces, context))
    out, grad_context, grad_first, inner, keep, send, small = dense(
        mine_ref, cell_kind, study_index.reshape(-1), rest_pieces, tokens_t, context, cotangent[0]
    )
    side_chain = Chain(side_steps(keep, send, fsdp, dp))
    small_chain = Chain(small_steps(small, fsdp, dp))
    meta = start_steps(meta, [side_chain])
    meta = end_steps(meta, [side_chain])
    chains = [side_chain, small_chain]
    half_chains = []
    grads = []
    before = ()
    for pair in reversed(range(PAIRS)):
        meta = start_steps(meta, chains)
        grad_t, *before = backward(
            pair, mine_ref, fsdp, before, meta, q_t, k_t, v_t, kc, kct, vct, grad_context, log_total,
            inner, slot, tokens_t,
        )
        before[0] = end_steps(before[0], chains)
        grads.append(grad_t)
        if pair % 2 == 0:
            half_chains.append(Chain(halving(*before, "fsdp", fsdp)))
            chains.append(half_chains[-1])
            before = ()
    late = half_chains[-1:]
    side_share = side_chain.finish()
    side_share = start_steps(side_share, late)
    side_old = (proj_weight, proj_first, proj_second, up_weight, up_first, up_second)
    side_old += (down_weight, down_first, down_second)
    side_new, side_squares = new_moments(side_share, side_old, False)
    side_squares = end_steps(side_squares, late)
    mine_ref, side_squares = lax.optimization_barrier((mine_ref, side_squares))
    mine_ref = start_steps(mine_ref, late + [small_chain])
    input_grad = input_side(mine_ref, qkv_pieces, grads[::-1], grad_first)
    input_grad = end_steps(input_grad, late + [small_chain])
    qkv_share = jnp.concatenate([chain.finish() for chain in half_chains], axis=1)
    qkv_share = total_by_exchange(qkv_share, "dp", dp)
    small = small_chain.finish()
    study_mean = small[8:16] / small[:8]
    study_var = small[16:24] / small[:8] - study_mean * study_mean
    norm_share = lax.dynamic_slice_in_dim(small[24:28], mine * (width // fsdp), width // fsdp, 1)
    norm_first, norm_second = moments(norm_share, norm_first, norm_second)
    norm_params = norm_params - VECTOR_RATE * update_of(norm_first, norm_second)

    (qkv_first, qkv_second), qkv_squares = new_moments(
        qkv_share, (qkv_weight, qkv_first, qkv_second), True
    )
    squares = jnp.concatenate(
        [qkv_squares[0:1], side_squares[0:3], qkv_squares[4:5], side_squares[4:7]], axis=0
    )
    squares = jnp.stack(gather_direct(squares, "fsdp", fsdp))
    arrays = (qkv_weight, qkv_first, qkv_second, proj_weight, side_new[0], side_new[1])
    arrays += (up_weight, side_new[2], side_new[3], down_weight, side_new[4], side_new[5])
    applied, matrix_norms = apply_updates(squares, arrays)
    results = []
    for index in range(4):
        results += [arrays[3 * index + 1], arrays[3 * index + 2]]
        results += [applied[2 * index], applied[2 * index + 1]]
    return (
        out.reshape(tokens.shape),
        input_grad.reshape(tokens.shape),
        study_mean,
        study_var,
        *results,
        norm_first,
        norm_second,
        norm_params,
        norm_params.astype(BF),
        matrix_norms,
    )


def solution(mesh):
    whole_groups = P(("dp", "fsdp"))
    rows = P("fsdp", None)
    columns = P(None, "fsdp")
    return jax.shard_map(
        partial(shards, mesh.shape["fsdp"], mesh.shape["dp"]),
        mesh=mesh,
        in_specs=(whole_groups,) * 6 + (rows,) * 12 + (columns,) * 3,
        out_specs=(whole_groups,) * 2 + (P(), P()) + (rows,) * 16 + (columns,) * 4 + (P(),),
        check_vma=False,
    )
```

```python
from functools import partial

import jax
import jax.numpy as jnp
from jax import lax
from jax.experimental import pallas as pl
from jax.experimental.pallas import tpu as pltpu
from jax.sharding import PartitionSpec as P

HEADS = 8
HDIM = 64
SHORT_LENGTH = 512
STUDY_COUNT = 8
STEP = 5
PAIR = 2 * HDIM
PAIRS = HEADS // 2
KEY_BLOCK = 256
FORWARD_WALK = 512, (128, 256)
BACKWARD_WALK = 256, (128,)


BETA = 0.5
ADAM_EPS = 1e-06
NORM_EPS = 1e-05
MATRIX_RATE = 0.5
VECTOR_RATE = 0.3
MATRIX_DECAY = 0.01
MASKED = -1000000000.0
SAFE_SCORE = 40.0

BF = jnp.bfloat16
F32 = jnp.float32
NN = (((1,), (0,)), ((), ()))
NT = (((1,), (1,)), ((), ()))
TN = (((0,), (0,)), ((), ()))
SMEM = pl.BlockSpec(memory_space=pltpu.SMEM)
ANY = pl.BlockSpec(memory_space=pl.ANY)


def mm(left, right, dims):
    return lax.dot_general(left, right, dims, preferred_element_type=F32)


def whole(*shape):
    return pl.BlockSpec(shape, lambda *_: (0,) * len(shape))


def params(mebibytes):
    return pltpu.CompilerParams(vmem_limit_bytes=mebibytes * 2**20)


def cost(flops, nbytes, trans=0):
    return pl.CostEstimate(flops=int(flops), bytes_accessed=int(nbytes), transcendentals=int(trans))


def iota(shape, dim):
    return lax.broadcasted_iota(jnp.int32, shape, dim)


def prep_kernel(kind, counts, known, tokens, tokens_t, packed, slot, meta):
    length = tokens.shape[0]
    cells = length // SHORT_LENGTH
    is_long = kind[0] == 1
    shape = (8, SHORT_LENGTH)
    row = iota(shape, 0)
    col = iota(shape, 1)
    given = jnp.zeros(shape, jnp.int32)
    for cell in range(cells):
        given = jnp.where(row == cell, known[0:1, pl.ds(cell * SHORT_LENGTH, SHORT_LENGTH)], given)
    limit = jnp.zeros(shape, jnp.int32)
    for cell in range(cells):
        limit = jnp.where(row == cell, counts[cell], limit)
    limit = jnp.where(is_long, counts[0] - SHORT_LENGTH * row, limit)
    first = (col == 0) & (jnp.logical_not(is_long) | (row == 0))
    usable = (col < limit) & ((given == 1) | first) & (row < cells)
    usable_f = jnp.where(usable, 1.0, 0.0)
    square = (SHORT_LENGTH, SHORT_LENGTH)
    before = jnp.where(iota(square, 0) < iota(square, 1), 1.0, 0.0).astype(BF)
    rank = mm(usable_f.astype(BF), before, NN).astype(jnp.int32)
    totals = [jnp.sum(usable_f[cell : cell + 1, :]).astype(jnp.int32) for cell in range(cells)]
    base = jnp.zeros(shape, jnp.int32)
    running = jnp.int32(0)
    for cell in range(cells):
        start = jnp.where(is_long, running, SHORT_LENGTH * cell)
        base = jnp.where(row == cell, start, base)
        running = running + totals[cell]
    place = jnp.where(usable, rank + base, -1)
    for cell in range(cells):
        slot[0:1, pl.ds(cell * SHORT_LENGTH, SHORT_LENGTH)] = place[cell : cell + 1, :]
    meta[0] = kind[0]
    for cell in range(cells):
        meta[1 + cell] = jnp.where(is_long, running if cell == 0 else 0, totals[cell])

    for block in range(length // KEY_BLOCK):
        rows = pl.ds(block * KEY_BLOCK, KEY_BLOCK)
        tokens_t[:, rows] = tokens[rows, :].T
        cell = block * KEY_BLOCK // SHORT_LENGTH
        inside = block * KEY_BLOCK - cell * SHORT_LENGTH
        needed = jnp.where(is_long, block * KEY_BLOCK < running, inside < totals[cell])

        @pl.when(needed)
        def _(block=block, rows=rows):
            hot = one_hot(slot, block * KEY_BLOCK, KEY_BLOCK)
            packed[rows, :] = mm(hot, tokens[...], NN).astype(BF)


def one_hot(slot, begin, rows):
    shape = (rows, slot.shape[1])
    hit = (iota(shape, 0) + begin) == slot[0:1, :]
    return jnp.where(hit, 1.0, 0.0).astype(BF)


def prep(kind, counts, known, tokens):
    length, width = tokens.shape
    return pl.pallas_call(
        prep_kernel,
        in_specs=[SMEM, SMEM, whole(1, length), whole(length, width)],
        out_specs=[
            whole(width, length),
            whole(length, width),
            whole(1, length),
            SMEM,
        ],
        out_shape=[
            jax.ShapeDtypeStruct((width, length), BF),
            jax.ShapeDtypeStruct((length, width), BF),
            jax.ShapeDtypeStruct((1, length), jnp.int32),
            jax.ShapeDtypeStruct((8,), jnp.int32),
        ],
        compiler_params=params(56),
        cost_estimate=cost(3e9, 12e6),
        name="prep",
    )(kind, counts, known, tokens)


def fetch_rows(pieces, mine, target, sem, kinds=1):
    rows = pieces[0].shape[0]
    copies = []
    for index, piece in enumerate(pieces):
        owner = jnp.bitwise_xor(mine, index)
        place = pl.ds(pl.multiple_of(owner * rows, rows), rows)
        if kinds == 1:
            copies.append((piece, target.at[place, :]))
            continue
        for pair in range(PAIRS):
            for kind in range(kinds):
                come = piece.at[:, pl.ds(PAIR * (PAIRS * kind + pair), PAIR)]
                copies.append((come, target.at[place, pl.ds(PAIR * (kinds * pair + kind), PAIR)]))
    copies = [pltpu.make_async_copy(*ends, sem.at[index]) for index, ends in enumerate(copies)]
    for copy in copies:
        copy.start()
    for copy in copies:
        copy.wait()


def head_lanes(shape, head):
    lane = iota(shape, 1)
    return (lane >= HDIM * head) & (lane < HDIM * (head + 1))


def spare(head):
    return HDIM * (1 - head)


def key_lanes(block, head, begin, count):
    lane = iota(block.shape, 1) - spare(head)
    row = iota(block.shape, 0) + begin
    bias = jnp.where(row < count, 0.0, MASKED)
    extra = jnp.where(lane == 0, bias, jnp.where((lane > 0) & (lane < 4), 1.0, 0.0))
    return jnp.where(head_lanes(block.shape, head), block.astype(F32), extra).astype(BF)


def split_rows(shift):
    high = shift.astype(BF).astype(F32)
    rest = shift - high
    mid = rest.astype(BF).astype(F32)
    low = rest - mid
    shape = (16, shift.shape[1])
    row = iota(shape, 0)
    out = jnp.where(row == 0, 1.0, 0.0)
    out = jnp.where(row == 1, -high, out)
    out = jnp.where(row == 2, -mid, out)
    return jnp.where(row == 3, -low, out).astype(BF)


def query_side(target, head, rows, shift):
    other = spare(head)
    target[head, HDIM * head : HDIM * (head + 1), :] = rows
    target[head, other : other + 16, :] = split_rows(shift)
    target[head, other + 16 : other + HDIM, :] = jnp.zeros((HDIM - 16, rows.shape[1]), BF)


def walk(meta, length, body, size, tails):
    @pl.when(meta[0] == 1)
    def _():
        cell_walk(meta[1], 0, 0, length, body, size, tails)

    @pl.when(meta[0] != 1)
    def _():
        @pl.loop(0, length // SHORT_LENGTH)
        def _(cell):
            begin = pl.multiple_of(cell * SHORT_LENGTH, SHORT_LENGTH)
            cell_walk(meta[1 + cell], begin, begin, SHORT_LENGTH, body, min(size, SHORT_LENGTH), tails)


def cell_walk(count, slot_begin, query_begin, queries, body, size, tails):
    tails = [tail for tail in tails if tail < size]
    rest = lax.rem(count, size)
    full = count // size + jnp.where(rest > tails[-1], 1, 0)
    end = slot_begin + count

    @pl.loop(0, full)
    def _(index):
        begin = pl.multiple_of(slot_begin + index * size, size)
        body(begin, size, query_begin, queries, end)

    for low, tail in zip([0] + tails, tails):

        @pl.when((rest > low) & (rest <= tail))
        def _(tail=tail):
            begin = pl.multiple_of(slot_begin + full * size, size)
            body(begin, tail, query_begin, queries, end)


def forward_kernel(count, mine, meta, *refs):
    pieces = refs[:count]
    tokens_t, packed, slot = refs[count : count + 3]
    q_out, k_out, v_out, kc_out, kct_out, vct_out, context, log_total = refs[count + 3 : count + 11]
    weights, kept_all, turned_all, vct, side, total, shift, sem = refs[count + 11 :]
    step = pl.program_id(0)
    width, length = tokens_t.shape

    @pl.when(step == 0)
    def _():
        fetch_rows(pieces, mine[0], weights, sem)

        def project(begin, rows, *_):
            place = pl.ds(begin, rows)
            both = mm(packed[place, :], weights[:, width:], NN)
            kept_all[place, :] = both[:, :width].astype(BF)
            turned_all[:, place] = both.T.astype(BF)

        walk(meta, length, project, *FORWARD_WALK)

    def here(kind):
        return pl.ds(pl.multiple_of(kind * width + step * PAIR, PAIR), PAIR)

    part = jnp.concatenate([weights[:, here(kind)] for kind in range(3)], axis=1)
    joined = mm(part, tokens_t[...], TN)
    q_out[...] = (joined[:PAIR] * HDIM**-0.5).astype(BF)
    k_out[...] = joined[PAIR : 2 * PAIR].astype(BF)
    v_out[...] = joined[2 * PAIR :].astype(BF)
    kc_out[...] = kept_all[:, here(0)]
    kct_out[...] = turned_all[here(0), :]
    vct_out[...] = turned_all[here(1), :]
    ones = jnp.where(iota((16, length), 0) == 0, 1.0, 0.0).astype(BF)
    for head in range(2):
        vct[head, :HDIM, :] = vct_out[HDIM * head : HDIM * (head + 1), :]
        vct[head, HDIM:, :] = ones

    masked = slot[...] < 0
    own = []
    for head in range(2):
        rows = slice(HDIM * head, HDIM * (head + 1))
        queries = q_out[rows, :].astype(F32)
        keys = k_out[rows, :].astype(F32)
        own.append(jnp.where(masked, jnp.sum(queries * keys, axis=0, keepdims=True), MASKED))
        top_q = jnp.max(jnp.sum(queries * queries, axis=0, keepdims=True))
        top_k = jnp.max(jnp.sum(keys * keys, axis=0, keepdims=True))
        unsafe = jnp.logical_not(top_q * top_k < SAFE_SCORE * SAFE_SCORE)
        shift[head : head + 1, :] = jnp.zeros((1, length), F32)
        query_side(side, head, q_out[rows, :], jnp.zeros((1, length), F32))

        @pl.when(unsafe)
        def _(head=head, rows=rows):
            shift[head : head + 1, :] = own[head]

            def raise_top(begin, rows, first, queries, end):
                keys = key_lanes(kc_out[pl.ds(begin, rows), :], head, begin, end)
                place = pl.ds(first, queries)
                scores = mm(keys, side[head, :, place], NN)
                top = jnp.max(scores, axis=0, keepdims=True)
                shift[head : head + 1, place] = jnp.maximum(shift[head : head + 1, place], top)

            walk(meta, length, raise_top, *FORWARD_WALK)
            query_side(side, head, q_out[rows, :], shift[head : head + 1, :])

    total[...] = jnp.zeros(total.shape, F32)

    def attend(begin, rows, first, queries, end):
        slots = pl.ds(begin, rows)
        place = pl.ds(first, queries)
        for head in range(2):
            keys = key_lanes(kc_out[slots, :], head, begin, end)
            raised = jnp.exp(mm(keys, side[head, :, place], NN)).astype(BF)
            total[head, :, place] += mm(vct[head, :, slots], raised, NN)

    walk(meta, length, attend, *FORWARD_WALK)

    for head in range(2):
        rows = slice(HDIM * head, HDIM * (head + 1))
        alone = jnp.exp(own[head] - shift[head : head + 1, :])
        row_total = total[head, HDIM : HDIM + 1, :] + alone
        gathered = total[head, :HDIM, :] + v_out[rows, :].astype(F32) * alone
        context[rows, :] = (gathered * (1.0 / row_total)).astype(BF)
        log_total[pl.ds(step * 2 + head, 1), :] = shift[head : head + 1, :] + jnp.log(row_total)


def forward(mine, meta, pieces, tokens_t, packed, slot):
    width, length = tokens_t.shape
    pair_rows = pl.BlockSpec((PAIR, length), lambda step: (step, 0))
    pair_lanes = pl.BlockSpec((length, PAIR), lambda step: (0, step))
    transposed = jax.ShapeDtypeStruct((width, length), BF)
    natural = jax.ShapeDtypeStruct((length, width), BF)
    count = len(pieces)
    return pl.pallas_call(
        partial(forward_kernel, count),
        grid=(PAIRS,),
        in_specs=[SMEM, SMEM]
        + [ANY] * count
        + [whole(width, length), whole(length, width), whole(1, length)],
        out_specs=[pair_rows] * 3 + [pair_lanes] + [pair_rows] * 3 + [whole(HEADS, length)],
        out_shape=[transposed] * 3
        + [natural]
        + [transposed] * 3
        + [jax.ShapeDtypeStruct((HEADS, length), F32)],
        scratch_shapes=[
            pltpu.VMEM((width, 3 * width), BF),
            pltpu.VMEM((length, width), BF),
            pltpu.VMEM((2 * width, length), BF),
            pltpu.VMEM((2, HDIM + 16, length), BF),
            pltpu.VMEM((2, PAIR, length), BF),
            pltpu.VMEM((2, HDIM + 16, length), F32),
            pltpu.VMEM((8, length), F32),
            pltpu.SemaphoreType.DMA((count,)),
        ],
        compiler_params=params(56),
        cost_estimate=cost(15e9, 25e6, 20e6),
        name="attend_forward",
    )(mine, meta, *pieces, tokens_t, packed, slot)


def backward_kernel(owners, pair_ref, mine, meta, *refs):
    pair = pair_ref[0]
    q_t, kc, kct, vct, grad_context, log_total, inner, slot, k_far, v_far, tokens_far = refs[:11]
    before = refs[11:-14]
    grad_far, keep, send = refs[-14:-11]
    turned_side, q_side, g_side, grad_q, grad_kv, ready, k_t, v_t, tokens_t, grad_t, sem = refs[-11:]
    length = q_t.shape[1]
    rows = pl.ds(pl.multiple_of(PAIR * pair, PAIR), PAIR)
    come = [
        pltpu.make_async_copy(k_far.at[rows, :], k_t, sem.at[0]),
        pltpu.make_async_copy(v_far.at[rows, :], v_t, sem.at[1]),
        pltpu.make_async_copy(tokens_far, tokens_t, sem.at[2]),
    ]
    for index, (part, target) in enumerate(zip(before, (keep, send))):
        target = target.at[:, pl.ds(0, part.shape[1])]
        come.append(pltpu.make_async_copy(part, target, sem.at[4 + index]))
    for copy in come:
        copy.start()

    for head in range(2):
        lanes = slice(HDIM * head, HDIM * (head + 1))
        index = 2 * pair + head
        query_side(turned_side, head, q_t[lanes, :], log_total[pl.ds(index, 1), :])
        q_side[head] = turned_side[head].T
        query_side(turned_side, head, grad_context[lanes, :], inner[pl.ds(index, 1), :])
        g_side[head] = turned_side[head].T
    grad_q[...] = jnp.zeros(grad_q.shape, F32)
    grad_kv[...] = jnp.zeros(grad_kv.shape, F32)
    ready[...] = jnp.zeros(ready.shape, BF)

    def pull(begin, count, first, queries, end):
        slots = pl.ds(begin, count)
        place = pl.ds(first, queries)
        keys = kc[slots, :]
        for head in range(2):
            lanes = slice(HDIM * head, HDIM * (head + 1))
            key_rows = key_side(kct[lanes, slots], head, begin, end)
            value_rows = key_side(vct[lanes, slots], head, begin, None)
            probs = jnp.exp(mm(q_side[head, place, :], key_rows, NN))
            pulled = mm(g_side[head, place, :], value_rows, NN)
            grad_scores = (probs * pulled).astype(BF)
            own_keys = jnp.where(head_lanes(keys.shape, head), keys.astype(F32), 0.0).astype(BF)
            grad_q[place, :] += mm(grad_scores, own_keys, NN)
            ready[lanes, slots] = mm(q_t[lanes, place], grad_scores, NN).astype(BF)
            ready[PAIR + HDIM * head : PAIR + HDIM * (head + 1), slots] = mm(
                grad_context[lanes, place], probs.astype(BF), NN
            ).astype(BF)

    walk(meta, length, pull, *BACKWARD_WALK)

    def scatter(begin, count, first, queries, end):
        slots = pl.ds(begin, count)
        place = pl.ds(first, queries)
        hit = (iota((count, queries), 0) + begin) == slot[0:1, place]
        spread = jnp.where(hit, 1.0, 0.0).astype(BF)
        grad_kv[:, place] += mm(ready[:, slots], spread, NN)

    walk(meta, length, scatter, *FORWARD_WALK)

    for copy in come:
        copy.wait()
    masked = slot[...] < 0
    turned = grad_q[...].T
    for head in range(2):
        lanes = slice(HDIM * head, HDIM * (head + 1))
        index = 2 * pair + head
        queries = q_t[lanes, :].astype(F32)
        keys = k_t[lanes, :].astype(F32)
        values = v_t[lanes, :].astype(F32)
        grads = grad_context[lanes, :].astype(F32)
        own = jnp.sum(queries * keys, axis=0, keepdims=True)
        own = jnp.where(masked, own - log_total[pl.ds(index, 1), :], MASKED)
        alone = jnp.exp(own)
        pulled = jnp.sum(grads * values, axis=0, keepdims=True) - inner[pl.ds(index, 1), :]
        pulled = (alone * pulled).astype(BF).astype(F32)
        alone = alone.astype(BF).astype(F32)
        part = (turned[lanes, :] + keys * pulled) * HDIM**-0.5
        grad_t[HDIM * head : HDIM * (head + 1), :] = part.astype(BF)
        part = grad_kv[lanes, :] + queries * pulled
        grad_t[PAIR + HDIM * head : PAIR + HDIM * (head + 1), :] = part.astype(BF)
        part = grad_kv[PAIR + HDIM * head : PAIR + HDIM * (head + 1), :] + grads * alone
        grad_t[2 * PAIR + HDIM * head : 2 * PAIR + HDIM * (head + 1), :] = part.astype(BF)
    leave = pltpu.make_async_copy(grad_t, grad_far, sem.at[3])
    leave.start()
    take_apart([mm(tokens_t[...], grad_t[...], NT)], mine[0], keep, send, owners)
    leave.wait()


def key_side(rows, head, begin, end):
    shape = (16, rows.shape[1])
    row = iota(shape, 0)
    extra = jnp.where((row > 0) & (row < 4), 1.0, 0.0)
    if end is not None:
        bias = jnp.where(iota(shape, 1) + begin < end, 0.0, MASKED)
        extra = jnp.where(row == 0, bias, extra)
    blank = jnp.zeros((HDIM - 16, rows.shape[1]), BF)
    extra = [extra.astype(BF), blank]
    return jnp.concatenate([rows] + extra if head == 0 else extra + [rows], axis=0)


def backward(
    pair, mine, owners, before, meta, q_t, k_t, v_t, kc, kct, vct, grad_context, log_total, inner,
    slot, tokens_t,
):
    width, length = tokens_t.shape
    pair_rows = pl.BlockSpec((PAIR, length), lambda step, place: (place[0], 0))
    pair_lanes = pl.BlockSpec((length, PAIR), lambda step, place: (0, place[0]))
    columns = 3 * PAIR + (before[0].shape[1] if before else 0)
    half = jax.ShapeDtypeStruct((width // 2, columns), BF)
    return pl.pallas_call(
        partial(backward_kernel, owners),
        grid_spec=pltpu.PrefetchScalarGridSpec(
            num_scalar_prefetch=1,
            grid=(1,),
            in_specs=[SMEM, SMEM, pair_rows, pair_lanes]
            + [pair_rows] * 3
            + [whole(HEADS, length)] * 2
            + [whole(1, length)]
            + [ANY] * (3 + len(before)),
            out_specs=[ANY] + [whole(*half.shape)] * 2,
            scratch_shapes=[
                pltpu.VMEM((2, PAIR, length), BF),
                pltpu.VMEM((2, length, PAIR), BF),
                pltpu.VMEM((2, length, PAIR), BF),
                pltpu.VMEM((length, PAIR), F32),
                pltpu.VMEM((2 * PAIR, length), F32),
                pltpu.VMEM((2 * PAIR, length), BF),
                pltpu.VMEM((PAIR, length), BF),
                pltpu.VMEM((PAIR, length), BF),
                pltpu.VMEM((width, length), BF),
                pltpu.VMEM((3 * PAIR, length), BF),
                pltpu.SemaphoreType.DMA((6,)),
            ],
        ),
        out_shape=[jax.ShapeDtypeStruct((3 * PAIR, length), BF), half, half],
        compiler_params=params(56),
        cost_estimate=cost(12e9, 10e6, 6e6),
        name="attend_backward",
    )(
        jnp.full((1,), pair, jnp.int32), mine, meta, q_t, kc, kct, vct, grad_context, log_total,
        inner, slot, k_t, v_t, tokens_t, *before,
    )


def feature_mean(values):
    return jnp.sum(values, axis=0, keepdims=True) * (1.0 / values.shape[0])


def normalise(values):
    centred = values - feature_mean(values)
    scale = lax.rsqrt(feature_mean(centred * centred) + NORM_EPS)
    return centred * scale, scale


def pull_norm(grad, scaled, scale, gain):
    lifted = grad * gain
    return scale * (lifted - feature_mean(lifted) - scaled * feature_mean(lifted * scaled))


def lane_sums(values):
    width = 128
    out = values[:, :width]
    for begin in range(width, values.shape[1], width):
        out = out + values[:, begin : begin + width]
    return out


def dense_kernel(count, mine, kind, study, *refs):
    pieces = refs[:count]
    tokens_t, context, cot_far = refs[count : count + 3]
    out, grad_context, grad_first, inner, keep, send, small = refs[count + 3 : count + 10]
    weights, total, norm_total, firsts, sem = refs[count + 10 :]
    step = pl.program_id(0)
    width = tokens_t.shape[0]

    @pl.when(step == 0)
    def _():
        fetch_rows(pieces, mine[0], weights, sem)
        total[...] = jnp.zeros(total.shape, F32)
        norm_total[...] = jnp.zeros(norm_total.shape, F32)

    proj = weights[:, :width]
    up = weights[:, width : 2 * width]
    down = weights[:, 2 * width : 3 * width]
    rows = weights[:, 3 * width :].astype(F32)
    gain1, bias1, gain2, bias2 = (rows[:, index : index + 1] for index in range(4))

    def half(place):
        context_low = context[:, place]
        first_sum = tokens_t[:, place].astype(F32) + mm(proj, context_low, TN)
        yield
        scaled1, scale1 = normalise(first_sum)
        middle = scaled1 * gain1 + bias1
        middle_low = middle.astype(BF)
        hidden = mm(up, middle_low, TN)
        yield
        cdf = 0.5 * (1.0 + lax.erf(hidden * 2.0**-0.5))
        slope = cdf + hidden * jnp.exp(hidden * hidden * -0.5) * 0.3989422804014327
        active = (hidden * cdf).astype(BF)
        second_sum = middle + mm(down, active, TN)
        yield
        scaled2, scale2 = normalise(second_sum)
        result = (scaled2 * gain2 + bias2).astype(BF).T
        out[place, :] = result
        firsts[pl.ds(2 * step + place.start // columns, 1), :] = result[:8].astype(F32)[0:1]
        cot = cot_far[place, :].T.astype(F32)
        norm_total[2] += lane_sums(cot * scaled2)
        norm_total[3] += lane_sums(cot)
        grad_second = pull_norm(cot, scaled2, scale2, gain2)
        grad_low = grad_second.astype(BF)
        pulled = mm(down, grad_low, NN)
        total[2] += mm(active, grad_low, NT)
        yield
        grad_hidden = (pulled * slope).astype(BF)
        grad_middle = grad_second + mm(up, grad_hidden, NN)
        total[1] += mm(middle_low, grad_hidden, NT)
        yield
        norm_total[0] += lane_sums(grad_middle * scaled1)
        norm_total[1] += lane_sums(grad_middle)
        grad_h1 = pull_norm(grad_middle, scaled1, scale1, gain1)
        proj_low = grad_h1.astype(BF)
        grad_first[:, place] = proj_low
        pulled = mm(proj, proj_low, NN)
        total[0] += mm(context_low, proj_low, NT)
        yield
        pulled = pulled.astype(BF)
        grad_context[:, place] = pulled
        both = pulled.astype(F32) * context_low.astype(F32)
        for head in range(HEADS):
            part = both[HDIM * head : HDIM * (head + 1), :]
            inner[head : head + 1, place] = jnp.sum(part, axis=0, keepdims=True)

    columns = tokens_t.shape[1] // 2
    halves = [half(slice(columns * index, columns * (index + 1))) for index in range(2)]
    while halves:
        halves = [stage for stage in halves if next(stage, stage) is None]

    @pl.when(step == pl.num_programs(0) - 1)
    def _():
        take_apart([total.at[index] for index in range(3)], mine[0], keep, send, count)
        lane = iota((width, 128), 1)
        packed = jnp.zeros((width, 128), F32)
        for index in range(4):
            column = jnp.sum(norm_total[index], axis=1, keepdims=True)
            packed = jnp.where(lane == index, column, packed)
        row = iota((STUDY_COUNT, width), 0)
        sums = [jnp.zeros((STUDY_COUNT, width), F32)] * 3
        for cell in range(firsts.shape[0]):
            hit = (row == study[cell]) & ((kind[0] == 0) | (cell == 0))
            first = firsts[cell : cell + 1, :]
            for index, term in enumerate((1.0, first, first * first)):
                sums[index] = sums[index] + jnp.where(hit, term, 0.0)
        for index in range(3):
            small[STUDY_COUNT * index : STUDY_COUNT * (index + 1), :] = sums[index]
        small[3 * STUDY_COUNT :, :] = packed.T[:8]


def take_apart(totals, mine, keep, send, owners):
    first = lax.rem(mine, 2) == 0
    at = keep.shape[1] - sum(total.shape[1] for total in totals)
    for total in totals:
        rows, columns = total.shape[0] // owners, total.shape[1]
        for half in range(owners // 2):
            even = total[2 * half * rows : (2 * half + 1) * rows, :].astype(BF)
            odd = total[(2 * half + 1) * rows : (2 * half + 2) * rows, :].astype(BF)
            here = slice(half * rows, (half + 1) * rows)
            keep[here, at : at + columns] = jnp.where(first, even, odd)
            send[here, at : at + columns] = jnp.where(first, odd, even)
        at += columns


def dense(mine, kind, study, pieces, tokens_t, context, cot):
    width, length = tokens_t.shape
    block = 2 * SHORT_LENGTH
    count = len(pieces)
    columns = pl.BlockSpec((width, block), lambda step: (0, step))
    rows = pl.BlockSpec((block, width), lambda step: (step, 0))
    return pl.pallas_call(
        partial(dense_kernel, count),
        grid=(length // block,),
        in_specs=[SMEM] * 3 + [ANY] * count + [columns, columns, rows],
        out_specs=[
            rows,
            columns,
            columns,
            pl.BlockSpec((HEADS, block), lambda step: (0, step)),
            whole(width // 2, 3 * width),
            whole(width // 2, 3 * width),
            whole(4 * STUDY_COUNT, width),
        ],
        out_shape=[
            jax.ShapeDtypeStruct((length, width), BF),
            jax.ShapeDtypeStruct((width, length), BF),
            jax.ShapeDtypeStruct((width, length), BF),
            jax.ShapeDtypeStruct((HEADS, length), F32),
            jax.ShapeDtypeStruct((width // 2, 3 * width), BF),
            jax.ShapeDtypeStruct((width // 2, 3 * width), BF),
            jax.ShapeDtypeStruct((4 * STUDY_COUNT, width), F32),
        ],
        scratch_shapes=[
            pltpu.VMEM((width, 3 * width + 128), BF),
            pltpu.VMEM((3, width, width), F32),
            pltpu.VMEM((4, width, 128), F32),
            pltpu.VMEM((length // SHORT_LENGTH, width), F32),
            pltpu.SemaphoreType.DMA((count,)),
        ],
        compiler_params=params(56),
        cost_estimate=cost(10e9, 20e6, 4e6),
        name="dense",
    )(mine, kind, study, *pieces, tokens_t, context, cot)


def input_kernel(count, mine, *refs):
    pieces = refs[:count]
    grads = refs[count : count + PAIRS]
    grad_first = refs[count + PAIRS]
    out, weights, sem = refs[-3:]

    @pl.when(pl.program_id(0) == 0)
    def _():
        fetch_rows(pieces, mine[0], weights, sem, 3)

    total = grad_first[...].T.astype(F32)
    for pair in range(PAIRS):
        part = weights[:, 3 * PAIR * pair : 3 * PAIR * (pair + 1)]
        total = total + mm(grads[pair][...], part, (((0,), (1,)), ((), ())))
    out[...] = total.astype(BF)


def input_side(mine, pieces, grads, grad_first, into=None):
    width, length = grad_first.shape
    block = 512
    count = len(pieces)
    steps = length // block // 2
    begin = 0 if into is None else steps
    kept = [] if into is None else [into]
    return pl.pallas_call(
        partial(input_kernel, count),
        grid=(steps,),
        in_specs=[SMEM]
        + [ANY] * count
        + [pl.BlockSpec((3 * PAIR, block), lambda step: (0, step + begin))] * PAIRS
        + [pl.BlockSpec((width, block), lambda step: (0, step + begin))]
        + [ANY] * len(kept),
        out_specs=pl.BlockSpec((block, width), lambda step: (step + begin, 0)),
        out_shape=jax.ShapeDtypeStruct((length, width), BF),
        scratch_shapes=[
            pltpu.VMEM((width, 3 * width), BF),
            pltpu.SemaphoreType.DMA((3 * PAIRS * count,)),
        ],
        compiler_params=params(56),
        cost_estimate=cost(3.3e9, 14e6),
        name="input_side",
        input_output_aliases={} if into is None else {2 + count + PAIRS: 0},
    )(mine, *pieces, *grads, grad_first, *kept)


def swap(value, axis, size, mask):
    return lax.ppermute(value, axis, [(index, index ^ mask) for index in range(size)])


def masks_of(size):
    return [1 << bit for bit in range(size.bit_length() - 1)]


def gather_direct(piece, axis, size):
    return [piece] + [swap(piece, axis, size, mask) for mask in range(1, size)]


def halving(keep, send, axis, size):
    mine = lax.axis_index(axis)
    rows = 2 * keep.shape[0] // size
    got = yield send, axis, size, 1
    value = (keep.astype(F32) + got.astype(F32)).astype(BF).reshape(size // 2, rows, -1)
    for bit, mask in list(enumerate(masks_of(size)))[1:]:
        value = value.reshape(value.shape[0] // 2, 2, rows, -1).swapaxes(0, 1)
        side = (mine >> bit) & 1
        send = lax.dynamic_index_in_dim(value, 1 - side, 0, keepdims=False)
        got = yield send, axis, size, mask
        keep = lax.dynamic_index_in_dim(value, side, 0, keepdims=False)
        value = (keep.astype(F32) + got.astype(F32)).astype(value.dtype)
    return value.reshape(rows, -1)


def doubling(value, axis, size):
    for mask in masks_of(size):
        got = yield value, axis, size, mask
        value = (value.astype(F32) + got.astype(F32)).astype(value.dtype)
    return value


def side_steps(keep, send, fsdp, dp):
    value = yield from halving(keep, send, "fsdp", fsdp)
    return (yield from doubling(value, "dp", dp))


def small_steps(value, fsdp, dp):
    value = yield from doubling(value, "fsdp", fsdp)
    return (yield from doubling(value, "dp", dp))


class Chain:
    def __init__(self, steps):
        self.steps, self.result, self.got = steps, None, None
        self.request = next(steps)

    def send(self, value):
        _, axis, size, mask = self.request
        self.got = swap(value, axis, size, mask)

    def land(self, value):
        try:
            self.request = self.steps.send(value)
        except StopIteration as end:
            self.request, self.result = None, end.value

    def finish(self):
        while self.request is not None:
            if self.got is None:
                self.send(self.request[0])
            value, self.got = self.got, None
            self.land(value)
        return self.result


def start_steps(anchor, chains):
    live = [chain for chain in chains if chain.request is not None]
    anchor, *values = lax.optimization_barrier((anchor, *(chain.request[0] for chain in live)))
    for chain, value in zip(live, values):
        chain.send(value)
    return anchor


def end_steps(anchor, chains):
    live = [chain for chain in chains if chain.got is not None]
    anchor, *values = lax.optimization_barrier((anchor, *(chain.got for chain in live)))
    for chain, value in zip(live, values):
        chain.got = None
        chain.land(value)
    return anchor


def spread_kernel(parts, out):
    total = jnp.sum(parts[...].astype(F32), axis=0).astype(BF)
    for index in range(out.shape[0]):
        out[index] = total


def spread_sums(parts):
    return pl.pallas_call(
        spread_kernel,
        out_shape=jax.ShapeDtypeStruct(parts.shape, BF),
        cost_estimate=cost(1e6, 1e6),
        name="spread",
    )(parts)


def moments(gradient, first_old, second_old):
    first_new = BETA * first_old + (1.0 - BETA) * gradient
    second_new = BETA * second_old + (1.0 - BETA) * gradient * gradient
    return first_new, second_new


def update_of(first_new, second_new):
    debias = 1.0 - BETA**STEP
    return first_new / debias / (jnp.sqrt(second_new / debias) + ADAM_EPS)


def square_row(values):
    total = jnp.sum(values * values, axis=0, keepdims=True)
    return lane_sums(total)


def moments_kernel(count, paired, gradient, *refs):
    olds, outs, squares = refs[: 3 * count], refs[3 * count : 6 * count], refs[6 * count]
    at = 0

    @pl.when(pl.program_id(0) == 0)
    def _():
        squares[...] = jnp.zeros(squares.shape, F32)

    for index in range(count):
        weight, first_old, second_old = (ref[...] for ref in olds[3 * index : 3 * index + 3])
        columns = weight.shape[1]
        if paired:
            places = [
                3 * PAIR * (PAIRS - 1 - pair) + PAIR * kind
                for kind in range(3)
                for pair in range(PAIRS)
            ]
            grad = jnp.concatenate([gradient[:, at : at + PAIR] for at in places], axis=1)
        else:
            grad = gradient[:, at : at + columns]
        grad = grad.astype(F32)
        at += columns
        first_new, second_new = moments(grad, first_old, second_old)
        update = update_of(first_new, second_new) + MATRIX_DECAY * weight
        for place, value in enumerate((first_new, second_new, update)):
            outs[3 * index + place][...] = value
        squares[index : index + 1, :] += square_row(weight)
        squares[4 + index : 5 + index, :] += square_row(update)


def row_blocks(arrays):
    rows = arrays[0].shape[0]
    steps = rows // 32 if rows % 32 == 0 else 1
    return steps, [
        pl.BlockSpec((rows // steps, array.shape[1]), lambda step: (step, 0)) for array in arrays
    ]


def new_moments(gradient, olds, paired):
    count = len(olds) // 3
    outs = [jax.ShapeDtypeStruct(old.shape, F32) for old in olds]
    steps, in_specs = row_blocks((gradient, *olds))
    results = pl.pallas_call(
        partial(moments_kernel, count, paired),
        grid=(steps,),
        in_specs=in_specs,
        out_specs=row_blocks(outs)[1] + [whole(8, 128)],
        out_shape=outs + [jax.ShapeDtypeStruct((8, 128), F32)],
        compiler_params=params(32),
        cost_estimate=cost(5e6, 5e6),
        name="moments",
    )(gradient, *olds)
    return results[:-1], results[-1]


def apply_kernel(count, squares, *refs):
    inputs, outs, norms = refs[: 2 * count], refs[2 * count : 4 * count], refs[4 * count]
    total = jnp.sum(jnp.sum(squares[...], axis=0), axis=1, keepdims=True)
    size = jnp.sqrt(total)
    ratio = size[0:4] / size[4:8]
    lane = iota((1, 4), 1)
    rows = [jnp.zeros((1, 4), F32)] * 3
    for index in range(count):
        weight, update = inputs[2 * index][...], inputs[2 * index + 1][...]
        trust = ratio[index : index + 1]
        weight = weight - MATRIX_RATE * trust * update
        outs[2 * index][...] = weight
        outs[2 * index + 1][...] = weight.astype(BF)
        for place, value in enumerate((size[index : index + 1], size[4 + index : 5 + index], trust)):
            rows[place] = jnp.where(lane == index, value, rows[place])
    for place in range(3):
        norms[place : place + 1, :] = rows[place]


def apply_updates(squares, arrays):
    count = len(arrays) // 2
    outs = []
    for weight in arrays[::2]:
        outs += [jax.ShapeDtypeStruct(weight.shape, F32), jax.ShapeDtypeStruct(weight.shape, BF)]
    steps, in_specs = row_blocks(arrays)
    results = pl.pallas_call(
        partial(apply_kernel, count),
        grid=(steps,),
        in_specs=[whole(*squares.shape)] + in_specs,
        out_specs=row_blocks(outs)[1] + [whole(3, 4)],
        out_shape=outs + [jax.ShapeDtypeStruct((3, 4), F32)],
        compiler_params=params(32),
        cost_estimate=cost(5e6, 8e6),
        name="apply",
    )(squares, *arrays)
    return results[:-1], results[-1]


def shards(
    fsdp,
    dp,
    tokens,
    cotangent,
    known_genes,
    cell_kind,
    gene_counts,
    study_index,
    qkv_weight,
    qkv_first,
    qkv_second,
    proj_weight,
    proj_first,
    proj_second,
    up_weight,
    up_first,
    up_second,
    down_weight,
    down_first,
    down_second,
    norm_params,
    norm_first,
    norm_second,
):
    _, length, width = tokens.shape
    mine = lax.axis_index("fsdp").astype(jnp.int32)
    mine_ref = mine.reshape(1)

    tokens_t, packed, slot, meta = prep(
        cell_kind, gene_counts.reshape(-1), known_genes, tokens[0]
    )
    norm_columns = jnp.pad(norm_params.T, ((0, 0), (0, 124)))
    rest = jnp.concatenate([proj_weight, up_weight, down_weight, norm_columns], axis=1).astype(BF)
    own = qkv_weight.astype(BF)
    core, *far_masks = masks_of(fsdp)
    far = {0: own}
    for mask in reversed(far_masks):
        far.update({known ^ mask: swap(far[known], "fsdp", fsdp, mask) for known in far})
    names = sorted(far)[1:]
    slot, *values = lax.optimization_barrier((slot, *(far[name] for name in names)))
    far.update(zip(names, values))
    pieces = dict(far)
    pieces.update({known ^ core: swap(far[known], "fsdp", fsdp, core) for known in far})
    rest, far_piece = lax.optimization_barrier((rest, pieces[names[-1]]))
    pieces[names[-1]] = far_piece
    rest_pieces = gather_direct(rest, "fsdp", fsdp)
    qkv_pieces = [pieces[index] for index in range(fsdp)]
    q_t, k_t, v_t, kc, kct, vct, context, log_total = forward(
        mine_ref, meta, qkv_pieces, tokens_t, packed, slot
    )
    *rest_pieces, context = lax.optimization_barrier((*rest_pieces, context))
    out, grad_context, grad_first, inner, keep, send, small = dense(
        mine_ref, cell_kind, study_index.reshape(-1), rest_pieces, tokens_t, context, cotangent[0]
    )
    side_chain = Chain(side_steps(keep, send, fsdp, dp))
    small_chain = Chain(small_steps(small, fsdp, dp))
    meta = start_steps(meta, [side_chain])
    meta = end_steps(meta, [side_chain])
    chains = [side_chain, small_chain]
    half_chains = []
    grads = []
    before = ()
    for pair in reversed(range(PAIRS)):
        meta = start_steps(meta, chains)
        grad_t, *before = backward(
            pair, mine_ref, fsdp, before, meta, q_t, k_t, v_t, kc, kct, vct, grad_context, log_total,
            inner, slot, tokens_t,
        )
        before[0] = end_steps(before[0], chains)
        grads.append(grad_t)
        if pair % 2 == 0:
            half_chains.append(Chain(halving(*before, "fsdp", fsdp)))
            chains.append(half_chains[-1])
            before = ()
    late = half_chains[-1:]
    side_share = side_chain.finish()
    side_share = start_steps(side_share, late)
    side_old = (proj_weight, proj_first, proj_second, up_weight, up_first, up_second)
    side_old += (down_weight, down_first, down_second)
    side_new, side_squares = new_moments(side_share, side_old, False)
    side_squares = end_steps(side_squares, late)
    mine_ref, side_squares = lax.optimization_barrier((mine_ref, side_squares))
    mine_ref = start_steps(mine_ref, late + [small_chain])
    input_grad = input_side(mine_ref, qkv_pieces, grads[::-1], grad_first)
    input_grad = end_steps(input_grad, late + [small_chain])
    qkv_share = jnp.concatenate([chain.finish() for chain in half_chains], axis=1)
    qkv_share, mine_ref = lax.optimization_barrier((qkv_share, mine_ref))
    rows = qkv_share.shape[0]
    parts = lax.all_to_all(qkv_share, "dp", 0, 0, tiled=True)
    input_grad = input_side(mine_ref, qkv_pieces, grads[::-1], grad_first, input_grad)
    parts, input_grad = lax.optimization_barrier((parts, input_grad))
    parts = spread_sums(parts.reshape(dp, rows // dp, -1)).reshape(rows, -1)
    qkv_share = lax.all_to_all(parts, "dp", 0, 0, tiled=True)
    small = small_chain.finish()
    study_mean = small[8:16] / small[:8]
    study_var = small[16:24] / small[:8] - study_mean * study_mean
    norm_share = lax.dynamic_slice_in_dim(small[24:28], mine * (width // fsdp), width // fsdp, 1)
    norm_first, norm_second = moments(norm_share, norm_first, norm_second)
    norm_params = norm_params - VECTOR_RATE * update_of(norm_first, norm_second)

    (qkv_first, qkv_second, qkv_update), qkv_squares = new_moments(
        qkv_share, (qkv_weight, qkv_first, qkv_second), True
    )
    squares = jnp.concatenate(
        [qkv_squares[0:1], side_squares[0:3], qkv_squares[4:5], side_squares[4:7]], axis=0
    )
    squares = jnp.stack(gather_direct(squares, "fsdp", fsdp))
    arrays = (qkv_weight, qkv_update, proj_weight, side_new[2])
    arrays += (up_weight, side_new[5], down_weight, side_new[8])
    applied, matrix_norms = apply_updates(squares, arrays)
    firsts = (qkv_first, side_new[0], side_new[3], side_new[6])
    seconds = (qkv_second, side_new[1], side_new[4], side_new[7])
    results = []
    for index in range(4):
        results += [firsts[index], seconds[index], applied[2 * index], applied[2 * index + 1]]
    return (
        out.reshape(tokens.shape),
        input_grad.reshape(tokens.shape),
        study_mean,
        study_var,
        *results,
        norm_first,
        norm_second,
        norm_params,
        norm_params.astype(BF),
        matrix_norms,
    )


def solution(mesh):
    whole_groups = P(("dp", "fsdp"))
    rows = P("fsdp", None)
    columns = P(None, "fsdp")
    return jax.shard_map(
        partial(shards, mesh.shape["fsdp"], mesh.shape["dp"]),
        mesh=mesh,
        in_specs=(whole_groups,) * 6 + (rows,) * 12 + (columns,) * 3,
        out_specs=(whole_groups,) * 2 + (P(), P()) + (rows,) * 16 + (columns,) * 4 + (P(),),
        check_vma=False,
    )
```

```python
from functools import partial

import jax
import jax.numpy as jnp
from jax import lax
from jax.experimental import pallas as pl
from jax.experimental.pallas import tpu as pltpu
from jax.sharding import PartitionSpec as P

HEADS = 8
HDIM = 64
SHORT_LENGTH = 512
STUDY_COUNT = 8
STEP = 5
PAIR = 2 * HDIM
PAIRS = HEADS // 2
KEY_BLOCK = 256
FORWARD_WALK = 512, (128, 256)
BACKWARD_WALK = 256, (128,)


BETA = 0.5
ADAM_EPS = 1e-06
NORM_EPS = 1e-05
MATRIX_RATE = 0.5
VECTOR_RATE = 0.3
MATRIX_DECAY = 0.01
MASKED = -1000000000.0
SAFE_SCORE = 40.0

BF = jnp.bfloat16
F32 = jnp.float32
NN = (((1,), (0,)), ((), ()))
NT = (((1,), (1,)), ((), ()))
TN = (((0,), (0,)), ((), ()))
SMEM = pl.BlockSpec(memory_space=pltpu.SMEM)
ANY = pl.BlockSpec(memory_space=pl.ANY)


def mm(left, right, dims):
    return lax.dot_general(left, right, dims, preferred_element_type=F32)


def whole(*shape):
    return pl.BlockSpec(shape, lambda *_: (0,) * len(shape))


def params(mebibytes):
    return pltpu.CompilerParams(vmem_limit_bytes=mebibytes * 2**20)


def cost(flops, nbytes, trans=0):
    return pl.CostEstimate(flops=int(flops), bytes_accessed=int(nbytes), transcendentals=int(trans))


def iota(shape, dim):
    return lax.broadcasted_iota(jnp.int32, shape, dim)


def prep_kernel(kind, counts, known, tokens, tokens_t, packed, slot, meta):
    length = tokens.shape[0]
    cells = length // SHORT_LENGTH
    is_long = kind[0] == 1
    shape = (8, SHORT_LENGTH)
    row = iota(shape, 0)
    col = iota(shape, 1)
    given = jnp.zeros(shape, jnp.int32)
    for cell in range(cells):
        given = jnp.where(row == cell, known[0:1, pl.ds(cell * SHORT_LENGTH, SHORT_LENGTH)], given)
    limit = jnp.zeros(shape, jnp.int32)
    for cell in range(cells):
        limit = jnp.where(row == cell, counts[cell], limit)
    limit = jnp.where(is_long, counts[0] - SHORT_LENGTH * row, limit)
    first = (col == 0) & (jnp.logical_not(is_long) | (row == 0))
    usable = (col < limit) & ((given == 1) | first) & (row < cells)
    usable_f = jnp.where(usable, 1.0, 0.0)
    square = (SHORT_LENGTH, SHORT_LENGTH)
    before = jnp.where(iota(square, 0) < iota(square, 1), 1.0, 0.0).astype(BF)
    rank = mm(usable_f.astype(BF), before, NN).astype(jnp.int32)
    totals = [jnp.sum(usable_f[cell : cell + 1, :]).astype(jnp.int32) for cell in range(cells)]
    base = jnp.zeros(shape, jnp.int32)
    running = jnp.int32(0)
    for cell in range(cells):
        start = jnp.where(is_long, running, SHORT_LENGTH * cell)
        base = jnp.where(row == cell, start, base)
        running = running + totals[cell]
    place = jnp.where(usable, rank + base, -1)
    for cell in range(cells):
        slot[0:1, pl.ds(cell * SHORT_LENGTH, SHORT_LENGTH)] = place[cell : cell + 1, :]
    meta[0] = kind[0]
    for cell in range(cells):
        meta[1 + cell] = jnp.where(is_long, running if cell == 0 else 0, totals[cell])

    for block in range(length // KEY_BLOCK):
        rows = pl.ds(block * KEY_BLOCK, KEY_BLOCK)
        tokens_t[:, rows] = tokens[rows, :].T
        cell = block * KEY_BLOCK // SHORT_LENGTH
        inside = block * KEY_BLOCK - cell * SHORT_LENGTH
        needed = jnp.where(is_long, block * KEY_BLOCK < running, inside < totals[cell])

        @pl.when(needed)
        def _(block=block, rows=rows):
            hot = one_hot(slot, block * KEY_BLOCK, KEY_BLOCK)
            packed[rows, :] = mm(hot, tokens[...], NN).astype(BF)


def one_hot(slot, begin, rows):
    shape = (rows, slot.shape[1])
    hit = (iota(shape, 0) + begin) == slot[0:1, :]
    return jnp.where(hit, 1.0, 0.0).astype(BF)


def prep(kind, counts, known, tokens):
    length, width = tokens.shape
    return pl.pallas_call(
        prep_kernel,
        in_specs=[SMEM, SMEM, whole(1, length), whole(length, width)],
        out_specs=[
            whole(width, length),
            whole(length, width),
            whole(1, length),
            SMEM,
        ],
        out_shape=[
            jax.ShapeDtypeStruct((width, length), BF),
            jax.ShapeDtypeStruct((length, width), BF),
            jax.ShapeDtypeStruct((1, length), jnp.int32),
            jax.ShapeDtypeStruct((8,), jnp.int32),
        ],
        compiler_params=params(56),
        cost_estimate=cost(3e9, 12e6),
        name="prep",
    )(kind, counts, known, tokens)


def fetch_rows(pieces, mine, target, sem, kinds=1):
    rows = pieces[0].shape[0]
    copies = []
    for index, piece in enumerate(pieces):
        owner = jnp.bitwise_xor(mine, index)
        place = pl.ds(pl.multiple_of(owner * rows, rows), rows)
        if kinds == 1:
            copies.append((piece, target.at[place, :]))
            continue
        for pair in range(PAIRS):
            for kind in range(kinds):
                come = piece.at[:, pl.ds(PAIR * (PAIRS * kind + pair), PAIR)]
                copies.append((come, target.at[place, pl.ds(PAIR * (kinds * pair + kind), PAIR)]))
    copies = [pltpu.make_async_copy(*ends, sem.at[index]) for index, ends in enumerate(copies)]
    for copy in copies:
        copy.start()
    for copy in copies:
        copy.wait()


def head_lanes(shape, head):
    lane = iota(shape, 1)
    return (lane >= HDIM * head) & (lane < HDIM * (head + 1))


def spare(head):
    return HDIM * (1 - head)


def key_lanes(block, head, begin, count):
    lane = iota(block.shape, 1) - spare(head)
    row = iota(block.shape, 0) + begin
    bias = jnp.where(row < count, 0.0, MASKED)
    extra = jnp.where(lane == 0, bias, jnp.where((lane > 0) & (lane < 4), 1.0, 0.0))
    return jnp.where(head_lanes(block.shape, head), block.astype(F32), extra).astype(BF)


def split_rows(shift):
    high = shift.astype(BF).astype(F32)
    rest = shift - high
    mid = rest.astype(BF).astype(F32)
    low = rest - mid
    shape = (16, shift.shape[1])
    row = iota(shape, 0)
    out = jnp.where(row == 0, 1.0, 0.0)
    out = jnp.where(row == 1, -high, out)
    out = jnp.where(row == 2, -mid, out)
    return jnp.where(row == 3, -low, out).astype(BF)


def query_side(target, head, rows, shift):
    other = spare(head)
    target[head, HDIM * head : HDIM * (head + 1), :] = rows
    target[head, other : other + 16, :] = split_rows(shift)
    target[head, other + 16 : other + HDIM, :] = jnp.zeros((HDIM - 16, rows.shape[1]), BF)


def walk(meta, length, body, size, tails):
    @pl.when(meta[0] == 1)
    def _():
        cell_walk(meta[1], 0, 0, length, body, size, tails)

    @pl.when(meta[0] != 1)
    def _():
        @pl.loop(0, length // SHORT_LENGTH)
        def _(cell):
            begin = pl.multiple_of(cell * SHORT_LENGTH, SHORT_LENGTH)
            cell_walk(meta[1 + cell], begin, begin, SHORT_LENGTH, body, min(size, SHORT_LENGTH), tails)


def cell_walk(count, slot_begin, query_begin, queries, body, size, tails):
    tails = [tail for tail in tails if tail < size]
    rest = lax.rem(count, size)
    full = count // size + jnp.where(rest > (tails or [0])[-1], 1, 0)
    end = slot_begin + count

    @pl.loop(0, full)
    def _(index):
        begin = pl.multiple_of(slot_begin + index * size, size)
        body(begin, size, query_begin, queries, end)

    for low, tail in zip([0] + tails, tails):

        @pl.when((rest > low) & (rest <= tail))
        def _(tail=tail):
            begin = pl.multiple_of(slot_begin + full * size, size)
            body(begin, tail, query_begin, queries, end)


def forward_kernel(count, mine, meta, *refs):
    pieces = refs[:count]
    tokens_t, packed, slot = refs[count : count + 3]
    q_out, k_out, v_out, kc_out, kct_out, vct_out, context, log_total = refs[count + 3 : count + 11]
    weights, kept_all, turned_all, vct, side, total, shift, sem = refs[count + 11 :]
    step = pl.program_id(0)
    width, length = tokens_t.shape

    @pl.when(step == 0)
    def _():
        fetch_rows(pieces, mine[0], weights, sem)

        def project(begin, rows, *_):
            place = pl.ds(begin, rows)
            both = mm(packed[place, :], weights[:, width:], NN)
            kept_all[place, :] = both[:, :width].astype(BF)
            turned_all[:, place] = both.T.astype(BF)

        walk(meta, length, project, *FORWARD_WALK)

    def here(kind):
        return pl.ds(pl.multiple_of(kind * width + step * PAIR, PAIR), PAIR)

    part = jnp.concatenate([weights[:, here(kind)] for kind in range(3)], axis=1)
    joined = mm(part, tokens_t[...], TN)
    q_out[...] = (joined[:PAIR] * HDIM**-0.5).astype(BF)
    k_out[...] = joined[PAIR : 2 * PAIR].astype(BF)
    v_out[...] = joined[2 * PAIR :].astype(BF)
    kc_out[...] = kept_all[:, here(0)]
    kct_out[...] = turned_all[here(0), :]
    vct_out[...] = turned_all[here(1), :]
    ones = jnp.where(iota((16, length), 0) == 0, 1.0, 0.0).astype(BF)
    for head in range(2):
        vct[head, :HDIM, :] = vct_out[HDIM * head : HDIM * (head + 1), :]
        vct[head, HDIM:, :] = ones

    masked = slot[...] < 0
    own = []
    for head in range(2):
        rows = slice(HDIM * head, HDIM * (head + 1))
        queries = q_out[rows, :].astype(F32)
        keys = k_out[rows, :].astype(F32)
        own.append(jnp.where(masked, jnp.sum(queries * keys, axis=0, keepdims=True), MASKED))
        top_q = jnp.max(jnp.sum(queries * queries, axis=0, keepdims=True))
        top_k = jnp.max(jnp.sum(keys * keys, axis=0, keepdims=True))
        unsafe = jnp.logical_not(top_q * top_k < SAFE_SCORE * SAFE_SCORE)
        shift[head : head + 1, :] = jnp.zeros((1, length), F32)
        query_side(side, head, q_out[rows, :], jnp.zeros((1, length), F32))

        @pl.when(unsafe)
        def _(head=head, rows=rows):
            shift[head : head + 1, :] = own[head]

            def raise_top(begin, rows, first, queries, end):
                keys = key_lanes(kc_out[pl.ds(begin, rows), :], head, begin, end)
                place = pl.ds(first, queries)
                scores = mm(keys, side[head, :, place], NN)
                top = jnp.max(scores, axis=0, keepdims=True)
                shift[head : head + 1, place] = jnp.maximum(shift[head : head + 1, place], top)

            walk(meta, length, raise_top, 128, ())
            query_side(side, head, q_out[rows, :], shift[head : head + 1, :])

    total[...] = jnp.zeros(total.shape, F32)

    def attend(begin, rows, first, queries, end):
        slots = pl.ds(begin, rows)
        place = pl.ds(first, queries)
        for head in range(2):
            keys = key_lanes(kc_out[slots, :], head, begin, end)
            raised = jnp.exp(mm(keys, side[head, :, place], NN)).astype(BF)
            total[head, :, place] += mm(vct[head, :, slots], raised, NN)

    walk(meta, length, attend, *FORWARD_WALK)

    for head in range(2):
        rows = slice(HDIM * head, HDIM * (head + 1))
        alone = jnp.exp(own[head] - shift[head : head + 1, :])
        row_total = total[head, HDIM : HDIM + 1, :] + alone
        gathered = total[head, :HDIM, :] + v_out[rows, :].astype(F32) * alone
        context[rows, :] = (gathered * (1.0 / row_total)).astype(BF)
        log_total[pl.ds(step * 2 + head, 1), :] = shift[head : head + 1, :] + jnp.log(row_total)


def forward(mine, meta, pieces, tokens_t, packed, slot):
    width, length = tokens_t.shape
    pair_rows = pl.BlockSpec((PAIR, length), lambda step: (step, 0))
    pair_lanes = pl.BlockSpec((length, PAIR), lambda step: (0, step))
    transposed = jax.ShapeDtypeStruct((width, length), BF)
    natural = jax.ShapeDtypeStruct((length, width), BF)
    count = len(pieces)
    return pl.pallas_call(
        partial(forward_kernel, count),
        grid=(PAIRS,),
        in_specs=[SMEM, SMEM]
        + [ANY] * count
        + [whole(width, length), whole(length, width), whole(1, length)],
        out_specs=[pair_rows] * 3 + [pair_lanes] + [pair_rows] * 3 + [whole(HEADS, length)],
        out_shape=[transposed] * 3
        + [natural]
        + [transposed] * 3
        + [jax.ShapeDtypeStruct((HEADS, length), F32)],
        scratch_shapes=[
            pltpu.VMEM((width, 3 * width), BF),
            pltpu.VMEM((length, width), BF),
            pltpu.VMEM((2 * width, length), BF),
            pltpu.VMEM((2, HDIM + 16, length), BF),
            pltpu.VMEM((2, PAIR, length), BF),
            pltpu.VMEM((2, HDIM + 16, length), F32),
            pltpu.VMEM((8, length), F32),
            pltpu.SemaphoreType.DMA((count,)),
        ],
        compiler_params=params(56),
        cost_estimate=cost(15e9, 25e6, 20e6),
        name="attend_forward",
    )(mine, meta, *pieces, tokens_t, packed, slot)


def backward_kernel(owners, pair_ref, mine, meta, *refs):
    pair = pair_ref[0]
    q_t, kc, kct, vct, grad_context, log_total, inner, slot, k_far, v_far, tokens_far = refs[:11]
    before = refs[11:-14]
    grad_far, keep, send = refs[-14:-11]
    turned_side, q_side, g_side, grad_q, grad_kv, ready, k_t, v_t, tokens_t, grad_t, sem = refs[-11:]
    length = q_t.shape[1]
    rows = pl.ds(pl.multiple_of(PAIR * pair, PAIR), PAIR)
    come = [
        pltpu.make_async_copy(k_far.at[rows, :], k_t, sem.at[0]),
        pltpu.make_async_copy(v_far.at[rows, :], v_t, sem.at[1]),
        pltpu.make_async_copy(tokens_far, tokens_t, sem.at[2]),
    ]
    for index, (part, target) in enumerate(zip(before, (keep, send))):
        target = target.at[:, pl.ds(0, part.shape[1])]
        come.append(pltpu.make_async_copy(part, target, sem.at[4 + index]))
    for copy in come:
        copy.start()

    for head in range(2):
        lanes = slice(HDIM * head, HDIM * (head + 1))
        index = 2 * pair + head
        query_side(turned_side, head, q_t[lanes, :], log_total[pl.ds(index, 1), :])
        q_side[head] = turned_side[head].T
        query_side(turned_side, head, grad_context[lanes, :], inner[pl.ds(index, 1), :])
        g_side[head] = turned_side[head].T
    grad_q[...] = jnp.zeros(grad_q.shape, F32)
    grad_kv[...] = jnp.zeros(grad_kv.shape, F32)
    ready[...] = jnp.zeros(ready.shape, BF)

    def pull(begin, count, first, queries, end):
        slots = pl.ds(begin, count)
        place = pl.ds(first, queries)
        keys = kc[slots, :]
        for head in range(2):
            lanes = slice(HDIM * head, HDIM * (head + 1))
            key_rows = key_side(kct[lanes, slots], head, begin, end)
            value_rows = key_side(vct[lanes, slots], head, begin, None)
            probs = jnp.exp(mm(q_side[head, place, :], key_rows, NN))
            pulled = mm(g_side[head, place, :], value_rows, NN)
            grad_scores = (probs * pulled).astype(BF)
            own_keys = jnp.where(head_lanes(keys.shape, head), keys.astype(F32), 0.0).astype(BF)
            grad_q[place, :] += mm(grad_scores, own_keys, NN)
            ready[lanes, slots] = mm(q_t[lanes, place], grad_scores, NN).astype(BF)
            ready[PAIR + HDIM * head : PAIR + HDIM * (head + 1), slots] = mm(
                grad_context[lanes, place], probs.astype(BF), NN
            ).astype(BF)

    walk(meta, length, pull, *BACKWARD_WALK)

    def scatter(begin, count, first, queries, end):
        slots = pl.ds(begin, count)
        place = pl.ds(first, queries)
        hit = (iota((count, queries), 0) + begin) == slot[0:1, place]
        spread = jnp.where(hit, 1.0, 0.0).astype(BF)
        grad_kv[:, place] += mm(ready[:, slots], spread, NN)

    walk(meta, length, scatter, 512, (256,))

    for copy in come:
        copy.wait()
    masked = slot[...] < 0
    turned = grad_q[...].T
    for head in range(2):
        lanes = slice(HDIM * head, HDIM * (head + 1))
        index = 2 * pair + head
        queries = q_t[lanes, :].astype(F32)
        keys = k_t[lanes, :].astype(F32)
        values = v_t[lanes, :].astype(F32)
        grads = grad_context[lanes, :].astype(F32)
        own = jnp.sum(queries * keys, axis=0, keepdims=True)
        own = jnp.where(masked, own - log_total[pl.ds(index, 1), :], MASKED)
        alone = jnp.exp(own)
        pulled = jnp.sum(grads * values, axis=0, keepdims=True) - inner[pl.ds(index, 1), :]
        pulled = (alone * pulled).astype(BF).astype(F32)
        alone = alone.astype(BF).astype(F32)
        part = (turned[lanes, :] + keys * pulled) * HDIM**-0.5
        grad_t[HDIM * head : HDIM * (head + 1), :] = part.astype(BF)
        part = grad_kv[lanes, :] + queries * pulled
        grad_t[PAIR + HDIM * head : PAIR + HDIM * (head + 1), :] = part.astype(BF)
        part = grad_kv[PAIR + HDIM * head : PAIR + HDIM * (head + 1), :] + grads * alone
        grad_t[2 * PAIR + HDIM * head : 2 * PAIR + HDIM * (head + 1), :] = part.astype(BF)
    leave = pltpu.make_async_copy(grad_t, grad_far, sem.at[3])
    leave.start()
    take_apart([mm(tokens_t[...], grad_t[...], NT)], mine[0], keep, send, owners)
    leave.wait()


def key_side(rows, head, begin, end):
    shape = (16, rows.shape[1])
    row = iota(shape, 0)
    extra = jnp.where((row > 0) & (row < 4), 1.0, 0.0)
    if end is not None:
        bias = jnp.where(iota(shape, 1) + begin < end, 0.0, MASKED)
        extra = jnp.where(row == 0, bias, extra)
    blank = jnp.zeros((HDIM - 16, rows.shape[1]), BF)
    extra = [extra.astype(BF), blank]
    return jnp.concatenate([rows] + extra if head == 0 else extra + [rows], axis=0)


def backward(
    pair, mine, owners, before, meta, q_t, k_t, v_t, kc, kct, vct, grad_context, log_total, inner,
    slot, tokens_t,
):
    width, length = tokens_t.shape
    pair_rows = pl.BlockSpec((PAIR, length), lambda step, place: (place[0], 0))
    pair_lanes = pl.BlockSpec((length, PAIR), lambda step, place: (0, place[0]))
    columns = 3 * PAIR + (before[0].shape[1] if before else 0)
    half = jax.ShapeDtypeStruct((width // 2, columns), BF)
    return pl.pallas_call(
        partial(backward_kernel, owners),
        grid_spec=pltpu.PrefetchScalarGridSpec(
            num_scalar_prefetch=1,
            grid=(1,),
            in_specs=[SMEM, SMEM, pair_rows, pair_lanes]
            + [pair_rows] * 3
            + [whole(HEADS, length)] * 2
            + [whole(1, length)]
            + [ANY] * (3 + len(before)),
            out_specs=[ANY] + [whole(*half.shape)] * 2,
            scratch_shapes=[
                pltpu.VMEM((2, PAIR, length), BF),
                pltpu.VMEM((2, length, PAIR), BF),
                pltpu.VMEM((2, length, PAIR), BF),
                pltpu.VMEM((length, PAIR), F32),
                pltpu.VMEM((2 * PAIR, length), F32),
                pltpu.VMEM((2 * PAIR, length), BF),
                pltpu.VMEM((PAIR, length), BF),
                pltpu.VMEM((PAIR, length), BF),
                pltpu.VMEM((width, length), BF),
                pltpu.VMEM((3 * PAIR, length), BF),
                pltpu.SemaphoreType.DMA((6,)),
            ],
        ),
        out_shape=[jax.ShapeDtypeStruct((3 * PAIR, length), BF), half, half],
        compiler_params=params(56),
        cost_estimate=cost(12e9, 10e6, 6e6),
        name="attend_backward",
    )(
        jnp.full((1,), pair, jnp.int32), mine, meta, q_t, kc, kct, vct, grad_context, log_total,
        inner, slot, k_t, v_t, tokens_t, *before,
    )


def feature_mean(values):
    return jnp.sum(values, axis=0, keepdims=True) * (1.0 / values.shape[0])


def normalise(values):
    centred = values - feature_mean(values)
    scale = lax.rsqrt(feature_mean(centred * centred) + NORM_EPS)
    return centred * scale, scale


def pull_norm(grad, scaled, scale, gain):
    lifted = grad * gain
    return scale * (lifted - feature_mean(lifted) - scaled * feature_mean(lifted * scaled))


def lane_sums(values):
    width = 128
    out = values[:, :width]
    for begin in range(width, values.shape[1], width):
        out = out + values[:, begin : begin + width]
    return out


def dense_kernel(count, mine, kind, study, *refs):
    pieces = refs[:count]
    tokens_t, context, cot_far = refs[count : count + 3]
    out, grad_context, grad_first, inner, keep, send, small = refs[count + 3 : count + 10]
    weights, total, norm_total, firsts, sem = refs[count + 10 :]
    step = pl.program_id(0)
    width = tokens_t.shape[0]

    @pl.when(step == 0)
    def _():
        fetch_rows(pieces, mine[0], weights, sem)
        total[...] = jnp.zeros(total.shape, F32)
        norm_total[...] = jnp.zeros(norm_total.shape, F32)

    proj = weights[:, :width]
    up = weights[:, width : 2 * width]
    down = weights[:, 2 * width : 3 * width]
    rows = weights[:, 3 * width :].astype(F32)
    gain1, bias1, gain2, bias2 = (rows[:, index : index + 1] for index in range(4))

    def part(place):
        context_low = context[:, place]
        first_sum = tokens_t[:, place].astype(F32) + mm(proj, context_low, TN)
        yield
        scaled1, scale1 = normalise(first_sum)
        middle = scaled1 * gain1 + bias1
        middle_low = middle.astype(BF)
        hidden = mm(up, middle_low, TN)
        yield
        cdf = 0.5 * (1.0 + lax.erf(hidden * 2.0**-0.5))
        slope = cdf + hidden * jnp.exp(hidden * hidden * -0.5) * 0.3989422804014327
        active = (hidden * cdf).astype(BF)
        second_sum = middle + mm(down, active, TN)
        yield
        scaled2, scale2 = normalise(second_sum)
        result = (scaled2 * gain2 + bias2).astype(BF).T
        out[place, :] = result
        if place.start % SHORT_LENGTH == 0:
            cell = 2 * step + place.start // SHORT_LENGTH
            firsts[pl.ds(cell, 1), :] = result[:8].astype(F32)[0:1]
        cot = cot_far[place, :].T.astype(F32)
        norm_total[2] += lane_sums(cot * scaled2)
        norm_total[3] += lane_sums(cot)
        grad_second = pull_norm(cot, scaled2, scale2, gain2)
        grad_low = grad_second.astype(BF)
        pulled = mm(down, grad_low, NN)
        total[2] += mm(active, grad_low, NT)
        yield
        grad_hidden = (pulled * slope).astype(BF)
        grad_middle = grad_second + mm(up, grad_hidden, NN)
        total[1] += mm(middle_low, grad_hidden, NT)
        yield
        norm_total[0] += lane_sums(grad_middle * scaled1)
        norm_total[1] += lane_sums(grad_middle)
        grad_h1 = pull_norm(grad_middle, scaled1, scale1, gain1)
        proj_low = grad_h1.astype(BF)
        grad_first[:, place] = proj_low
        pulled = mm(proj, proj_low, NN)
        total[0] += mm(context_low, proj_low, NT)
        yield
        pulled = pulled.astype(BF)
        grad_context[:, place] = pulled
        both = pulled.astype(F32) * context_low.astype(F32)
        for head in range(HEADS):
            part = both[HDIM * head : HDIM * (head + 1), :]
            inner[head : head + 1, place] = jnp.sum(part, axis=0, keepdims=True)

    columns = tokens_t.shape[1] // 4
    parts = [part(slice(columns * index, columns * (index + 1))) for index in range(4)]
    turn = 0
    while parts:
        parts = [stage for index, stage in enumerate(parts) if next(stage, stage) is None]
        turn += 1

    @pl.when(step == pl.num_programs(0) - 1)
    def _():
        take_apart([total.at[index] for index in range(3)], mine[0], keep, send, count)
        lane = iota((width, 128), 1)
        packed = jnp.zeros((width, 128), F32)
        for index in range(4):
            column = jnp.sum(norm_total[index], axis=1, keepdims=True)
            packed = jnp.where(lane == index, column, packed)
        row = iota((STUDY_COUNT, width), 0)
        sums = [jnp.zeros((STUDY_COUNT, width), F32)] * 3
        for cell in range(firsts.shape[0]):
            hit = (row == study[cell]) & ((kind[0] == 0) | (cell == 0))
            first = firsts[cell : cell + 1, :]
            for index, term in enumerate((1.0, first, first * first)):
                sums[index] = sums[index] + jnp.where(hit, term, 0.0)
        for index in range(3):
            small[STUDY_COUNT * index : STUDY_COUNT * (index + 1), :] = sums[index]
        small[3 * STUDY_COUNT :, :] = packed.T[:8]


def take_apart(totals, mine, keep, send, owners):
    first = lax.rem(mine, 2) == 0
    at = keep.shape[1] - sum(total.shape[1] for total in totals)
    for total in totals:
        rows, columns = total.shape[0] // owners, total.shape[1]
        for half in range(owners // 2):
            even = total[2 * half * rows : (2 * half + 1) * rows, :].astype(BF)
            odd = total[(2 * half + 1) * rows : (2 * half + 2) * rows, :].astype(BF)
            here = slice(half * rows, (half + 1) * rows)
            keep[here, at : at + columns] = jnp.where(first, even, odd)
            send[here, at : at + columns] = jnp.where(first, odd, even)
        at += columns


def dense(mine, kind, study, pieces, tokens_t, context, cot):
    width, length = tokens_t.shape
    block = 2 * SHORT_LENGTH
    count = len(pieces)
    columns = pl.BlockSpec((width, block), lambda step: (0, step))
    rows = pl.BlockSpec((block, width), lambda step: (step, 0))
    return pl.pallas_call(
        partial(dense_kernel, count),
        grid=(length // block,),
        in_specs=[SMEM] * 3 + [ANY] * count + [columns, columns, rows],
        out_specs=[
            rows,
            columns,
            columns,
            pl.BlockSpec((HEADS, block), lambda step: (0, step)),
            whole(width // 2, 3 * width),
            whole(width // 2, 3 * width),
            whole(4 * STUDY_COUNT, width),
        ],
        out_shape=[
            jax.ShapeDtypeStruct((length, width), BF),
            jax.ShapeDtypeStruct((width, length), BF),
            jax.ShapeDtypeStruct((width, length), BF),
            jax.ShapeDtypeStruct((HEADS, length), F32),
            jax.ShapeDtypeStruct((width // 2, 3 * width), BF),
            jax.ShapeDtypeStruct((width // 2, 3 * width), BF),
            jax.ShapeDtypeStruct((4 * STUDY_COUNT, width), F32),
        ],
        scratch_shapes=[
            pltpu.VMEM((width, 3 * width + 128), BF),
            pltpu.VMEM((3, width, width), F32),
            pltpu.VMEM((4, width, 128), F32),
            pltpu.VMEM((length // SHORT_LENGTH, width), F32),
            pltpu.SemaphoreType.DMA((count,)),
        ],
        compiler_params=params(48),
        cost_estimate=cost(10e9, 20e6, 4e6),
        name="dense",
    )(mine, kind, study, *pieces, tokens_t, context, cot)


def input_kernel(count, mine, *refs):
    pieces = refs[:count]
    grads = refs[count : count + PAIRS]
    grad_first = refs[count + PAIRS]
    out, weights, sem = refs[-3:]

    @pl.when(pl.program_id(0) == 0)
    def _():
        fetch_rows(pieces, mine[0], weights, sem, 3)

    total = grad_first[...].T.astype(F32)
    for pair in range(PAIRS):
        part = weights[:, 3 * PAIR * pair : 3 * PAIR * (pair + 1)]
        total = total + mm(grads[pair][...], part, (((0,), (1,)), ((), ())))
    out[...] = total.astype(BF)


def input_side(mine, pieces, grads, grad_first, into=None):
    width, length = grad_first.shape
    block = 512
    count = len(pieces)
    steps = length // block // 2
    begin = 0 if into is None else steps
    kept = [] if into is None else [into]
    return pl.pallas_call(
        partial(input_kernel, count),
        grid=(steps,),
        in_specs=[SMEM]
        + [ANY] * count
        + [pl.BlockSpec((3 * PAIR, block), lambda step: (0, step + begin))] * PAIRS
        + [pl.BlockSpec((width, block), lambda step: (0, step + begin))]
        + [ANY] * len(kept),
        out_specs=pl.BlockSpec((block, width), lambda step: (step + begin, 0)),
        out_shape=jax.ShapeDtypeStruct((length, width), BF),
        scratch_shapes=[
            pltpu.VMEM((width, 3 * width), BF),
            pltpu.SemaphoreType.DMA((3 * PAIRS * count,)),
        ],
        compiler_params=params(56),
        cost_estimate=cost(3.3e9, 14e6),
        name="input_side",
        input_output_aliases={} if into is None else {2 + count + PAIRS: 0},
    )(mine, *pieces, *grads, grad_first, *kept)


def swap(value, axis, size, mask):
    return lax.ppermute(value, axis, [(index, index ^ mask) for index in range(size)])


def masks_of(size):
    return [1 << bit for bit in range(size.bit_length() - 1)]


def gather_direct(piece, axis, size):
    return [piece] + [swap(piece, axis, size, mask) for mask in range(1, size)]


def halving(keep, send, axis, size):
    mine = lax.axis_index(axis)
    rows = 2 * keep.shape[0] // size
    got = yield send, axis, size, 1
    value = (keep.astype(F32) + got.astype(F32)).astype(BF).reshape(size // 2, rows, -1)
    for bit, mask in list(enumerate(masks_of(size)))[1:]:
        value = value.reshape(value.shape[0] // 2, 2, rows, -1).swapaxes(0, 1)
        side = (mine >> bit) & 1
        send = lax.dynamic_index_in_dim(value, 1 - side, 0, keepdims=False)
        got = yield send, axis, size, mask
        keep = lax.dynamic_index_in_dim(value, side, 0, keepdims=False)
        value = (keep.astype(F32) + got.astype(F32)).astype(value.dtype)
    return value.reshape(rows, -1)


def doubling(value, axis, size):
    for mask in masks_of(size):
        got = yield value, axis, size, mask
        value = (value.astype(F32) + got.astype(F32)).astype(value.dtype)
    return value


def side_steps(keep, send, fsdp, dp):
    value = yield from halving(keep, send, "fsdp", fsdp)
    return (yield from doubling(value, "dp", dp))


def small_steps(value, fsdp, dp):
    value = yield from doubling(value, "fsdp", fsdp)
    return (yield from doubling(value, "dp", dp))


class Chain:
    def __init__(self, steps):
        self.steps, self.result, self.got = steps, None, None
        self.request = next(steps)

    def send(self, value):
        _, axis, size, mask = self.request
        self.got = swap(value, axis, size, mask)

    def land(self, value):
        try:
            self.request = self.steps.send(value)
        except StopIteration as end:
            self.request, self.result = None, end.value

    def finish(self):
        while self.request is not None:
            if self.got is None:
                self.send(self.request[0])
            value, self.got = self.got, None
            self.land(value)
        return self.result


def start_steps(anchor, chains):
    live = [chain for chain in chains if chain.request is not None]
    anchor, *values = lax.optimization_barrier((anchor, *(chain.request[0] for chain in live)))
    for chain, value in zip(live, values):
        chain.send(value)
    return anchor


def end_steps(anchor, chains):
    live = [chain for chain in chains if chain.got is not None]
    anchor, values = lax.optimization_barrier((anchor, [chain.got for chain in live]))
    for chain, value in zip(live, values):
        chain.got = None
        chain.land(value)
    return anchor


def spread_kernel(parts, out):
    total = jnp.sum(parts[...].astype(F32), axis=0).astype(BF)
    for index in range(out.shape[0]):
        out[index] = total


def spread_sums(parts):
    return pl.pallas_call(
        spread_kernel,
        out_shape=jax.ShapeDtypeStruct(parts.shape, BF),
        cost_estimate=cost(1e6, 1e6),
        name="spread",
    )(parts)


def moments(gradient, first_old, second_old):
    first_new = BETA * first_old + (1.0 - BETA) * gradient
    second_new = BETA * second_old + (1.0 - BETA) * gradient * gradient
    return first_new, second_new


def update_of(first_new, second_new):
    debias = 1.0 - BETA**STEP
    return first_new / debias / (jnp.sqrt(second_new / debias) + ADAM_EPS)


def square_row(values):
    total = jnp.sum(values * values, axis=0, keepdims=True)
    return lane_sums(total)


def moments_kernel(count, paired, gradient, *refs):
    olds, outs, squares = refs[: 3 * count], refs[3 * count : 6 * count], refs[6 * count]
    at = 0

    @pl.when(pl.program_id(0) == 0)
    def _():
        squares[...] = jnp.zeros(squares.shape, F32)

    for index in range(count):
        weight, first_old, second_old = (ref[...] for ref in olds[3 * index : 3 * index + 3])
        columns = weight.shape[1]
        if paired:
            places = [
                3 * PAIR * (PAIRS - 1 - pair) + PAIR * kind
                for kind in range(3)
                for pair in range(PAIRS)
            ]
            grad = jnp.concatenate([gradient[:, at : at + PAIR] for at in places], axis=1)
        else:
            grad = gradient[:, at : at + columns]
        grad = grad.astype(F32)
        at += columns
        first_new, second_new = moments(grad, first_old, second_old)
        update = update_of(first_new, second_new) + MATRIX_DECAY * weight
        for place, value in enumerate((first_new, second_new, update)):
            outs[3 * index + place][...] = value
        squares[index : index + 1, :] += square_row(weight)
        squares[4 + index : 5 + index, :] += square_row(update)


def row_blocks(arrays):
    rows = arrays[0].shape[0]
    steps = rows // 32 if rows % 32 == 0 else 1
    return steps, [
        pl.BlockSpec((rows // steps, array.shape[1]), lambda step: (step, 0)) for array in arrays
    ]


def new_moments(gradient, olds, paired):
    count = len(olds) // 3
    outs = [jax.ShapeDtypeStruct(old.shape, F32) for old in olds]
    steps, in_specs = row_blocks((gradient, *olds))
    results = pl.pallas_call(
        partial(moments_kernel, count, paired),
        grid=(steps,),
        in_specs=in_specs,
        out_specs=row_blocks(outs)[1] + [whole(8, 128)],
        out_shape=outs + [jax.ShapeDtypeStruct((8, 128), F32)],
        compiler_params=params(32),
        cost_estimate=cost(5e6, 5e6),
        name="moments",
    )(gradient, *olds)
    return results[:-1], results[-1]


def apply_kernel(count, squares, *refs):
    inputs, outs, norms = refs[: 2 * count], refs[2 * count : 4 * count], refs[4 * count]
    total = jnp.sum(jnp.sum(squares[...], axis=0), axis=1, keepdims=True)
    size = jnp.sqrt(total)
    ratio = size[0:4] / size[4:8]
    lane = iota((1, 4), 1)
    rows = [jnp.zeros((1, 4), F32)] * 3
    for index in range(count):
        weight, update = inputs[2 * index][...], inputs[2 * index + 1][...]
        trust = ratio[index : index + 1]
        weight = weight - MATRIX_RATE * trust * update
        outs[2 * index][...] = weight
        outs[2 * index + 1][...] = weight.astype(BF)
        for place, value in enumerate((size[index : index + 1], size[4 + index : 5 + index], trust)):
            rows[place] = jnp.where(lane == index, value, rows[place])
    for place in range(3):
        norms[place : place + 1, :] = rows[place]


def apply_updates(squares, arrays):
    count = len(arrays) // 2
    outs = []
    for weight in arrays[::2]:
        outs += [jax.ShapeDtypeStruct(weight.shape, F32), jax.ShapeDtypeStruct(weight.shape, BF)]
    steps, in_specs = row_blocks(arrays)
    results = pl.pallas_call(
        partial(apply_kernel, count),
        grid=(steps,),
        in_specs=[whole(*squares.shape)] + in_specs,
        out_specs=row_blocks(outs)[1] + [whole(3, 4)],
        out_shape=outs + [jax.ShapeDtypeStruct((3, 4), F32)],
        compiler_params=params(32),
        cost_estimate=cost(5e6, 8e6),
        name="apply",
    )(squares, *arrays)
    return results[:-1], results[-1]


def shards(
    fsdp,
    dp,
    tokens,
    cotangent,
    known_genes,
    cell_kind,
    gene_counts,
    study_index,
    qkv_weight,
    qkv_first,
    qkv_second,
    proj_weight,
    proj_first,
    proj_second,
    up_weight,
    up_first,
    up_second,
    down_weight,
    down_first,
    down_second,
    norm_params,
    norm_first,
    norm_second,
):
    _, length, width = tokens.shape
    mine = lax.axis_index("fsdp").astype(jnp.int32)
    mine_ref = mine.reshape(1)

    tokens_t, packed, slot, meta = prep(
        cell_kind, gene_counts.reshape(-1), known_genes, tokens[0]
    )
    norm_columns = jnp.pad(norm_params.T, ((0, 0), (0, 124)))
    rest = jnp.concatenate([proj_weight, up_weight, down_weight, norm_columns], axis=1).astype(BF)
    own = qkv_weight.astype(BF)
    core, *far_masks = masks_of(fsdp)
    far = {0: own}
    for mask in reversed(far_masks):
        far.update({known ^ mask: swap(far[known], "fsdp", fsdp, mask) for known in far})
    names = sorted(far)[1:]
    slot, *values = lax.optimization_barrier((slot, *(far[name] for name in names)))
    far.update(zip(names, values))
    pieces = dict(far)
    pieces.update({known ^ core: swap(far[known], "fsdp", fsdp, core) for known in far})
    rest, far_piece = lax.optimization_barrier((rest, pieces[names[-1]]))
    pieces[names[-1]] = far_piece
    rest_pieces = gather_direct(rest, "fsdp", fsdp)
    qkv_pieces = [pieces[index] for index in range(fsdp)]
    q_t, k_t, v_t, kc, kct, vct, context, log_total = forward(
        mine_ref, meta, qkv_pieces, tokens_t, packed, slot
    )
    *rest_pieces, context = lax.optimization_barrier((*rest_pieces, context))
    out, grad_context, grad_first, inner, keep, send, small = dense(
        mine_ref, cell_kind, study_index.reshape(-1), rest_pieces, tokens_t, context, cotangent[0]
    )
    side_chain = Chain(side_steps(keep, send, fsdp, dp))
    small_chain = Chain(small_steps(small, fsdp, dp))
    meta = start_steps(meta, [side_chain])
    meta = end_steps(meta, [side_chain])
    chains = [side_chain, small_chain]
    half_chains = []
    grads = []
    before = ()
    for pair in reversed(range(PAIRS)):
        meta = start_steps(meta, chains)
        grad_t, *before = backward(
            pair, mine_ref, fsdp, before, meta, q_t, k_t, v_t, kc, kct, vct, grad_context, log_total,
            inner, slot, tokens_t,
        )
        before = list(end_steps(tuple(before), chains))
        grads.append(grad_t)
        if pair % 2 == 0:
            half_chains.append(Chain(halving(*before, "fsdp", fsdp)))
            chains.append(half_chains[-1])
            before = ()
    late = half_chains[-1:]
    side_share = side_chain.finish()
    mine_ref = start_steps(mine_ref, late)
    mine_ref = end_steps(mine_ref, late)
    mine_ref = start_steps(mine_ref, late + [small_chain])
    input_grad = input_side(mine_ref, qkv_pieces, grads[::-1], grad_first)
    input_grad = end_steps(input_grad, late + [small_chain])
    qkv_share = jnp.concatenate([chain.finish() for chain in half_chains], axis=1)
    qkv_share, mine_ref = lax.optimization_barrier((qkv_share, mine_ref))
    rows = qkv_share.shape[0]
    parts = lax.all_to_all(qkv_share, "dp", 0, 0, tiled=True)
    input_grad = input_side(mine_ref, qkv_pieces, grads[::-1], grad_first, input_grad)
    parts, input_grad = lax.optimization_barrier((parts, input_grad))
    parts = spread_sums(parts.reshape(dp, rows // dp, -1)).reshape(rows, -1)
    qkv_share = lax.all_to_all(parts, "dp", 0, 0, tiled=True)
    side_share, _ = lax.optimization_barrier((side_share, parts))
    side_old = (proj_weight, proj_first, proj_second, up_weight, up_first, up_second)
    side_old += (down_weight, down_first, down_second)
    side_new, side_squares = new_moments(side_share, side_old, False)
    qkv_share, side_squares = lax.optimization_barrier((qkv_share, side_squares))
    small = small_chain.finish()
    study_mean = small[8:16] / small[:8]
    study_var = small[16:24] / small[:8] - study_mean * study_mean
    norm_share = lax.dynamic_slice_in_dim(small[24:28], mine * (width // fsdp), width // fsdp, 1)
    norm_first, norm_second = moments(norm_share, norm_first, norm_second)
    norm_params = norm_params - VECTOR_RATE * update_of(norm_first, norm_second)

    (qkv_first, qkv_second, qkv_update), qkv_squares = new_moments(
        qkv_share, (qkv_weight, qkv_first, qkv_second), True
    )
    squares = jnp.concatenate(
        [qkv_squares[0:1], side_squares[0:3], qkv_squares[4:5], side_squares[4:7]], axis=0
    )
    squares = jnp.stack(gather_direct(squares, "fsdp", fsdp))
    arrays = (qkv_weight, qkv_update, proj_weight, side_new[2])
    arrays += (up_weight, side_new[5], down_weight, side_new[8])
    applied, matrix_norms = apply_updates(squares, arrays)
    firsts = (qkv_first, side_new[0], side_new[3], side_new[6])
    seconds = (qkv_second, side_new[1], side_new[4], side_new[7])
    results = []
    for index in range(4):
        results += [firsts[index], seconds[index], applied[2 * index], applied[2 * index + 1]]
    return (
        out.reshape(tokens.shape),
        input_grad.reshape(tokens.shape),
        study_mean,
        study_var,
        *results,
        norm_first,
        norm_second,
        norm_params,
        norm_params.astype(BF),
        matrix_norms,
    )


def solution(mesh):
    whole_groups = P(("dp", "fsdp"))
    rows = P("fsdp", None)
    columns = P(None, "fsdp")
    return jax.shard_map(
        partial(shards, mesh.shape["fsdp"], mesh.shape["dp"]),
        mesh=mesh,
        in_specs=(whole_groups,) * 6 + (rows,) * 12 + (columns,) * 3,
        out_specs=(whole_groups,) * 2 + (P(), P()) + (rows,) * 16 + (columns,) * 4 + (P(),),
        check_vma=False,
    )
```

```python
from functools import partial

import jax
import jax.numpy as jnp
from jax import lax
from jax.experimental import pallas as pl
from jax.experimental.pallas import tpu as pltpu
from jax.sharding import PartitionSpec as P

HEADS = 8
HDIM = 64
SHORT_LENGTH = 512
STUDY_COUNT = 8
STEP = 5
PAIR = 2 * HDIM
PAIRS = HEADS // 2
KEY_BLOCK = 256
FORWARD_WALK = 512, (128, 256)
BACKWARD_WALK = 256, (128,)


BETA = 0.5
ADAM_EPS = 1e-06
NORM_EPS = 1e-05
MATRIX_RATE = 0.5
VECTOR_RATE = 0.3
MATRIX_DECAY = 0.01
MASKED = -1000000000.0
SAFE_SCORE = 40.0

BF = jnp.bfloat16
F32 = jnp.float32
NN = (((1,), (0,)), ((), ()))
NT = (((1,), (1,)), ((), ()))
TN = (((0,), (0,)), ((), ()))
SMEM = pl.BlockSpec(memory_space=pltpu.SMEM)
ANY = pl.BlockSpec(memory_space=pl.ANY)


def mm(left, right, dims):
    return lax.dot_general(left, right, dims, preferred_element_type=F32)


def whole(*shape):
    return pl.BlockSpec(shape, lambda *_: (0,) * len(shape))


def params(mebibytes):
    return pltpu.CompilerParams(vmem_limit_bytes=mebibytes * 2**20)


def cost(flops, nbytes, trans=0):
    return pl.CostEstimate(flops=int(flops), bytes_accessed=int(nbytes), transcendentals=int(trans))


def iota(shape, dim):
    return lax.broadcasted_iota(jnp.int32, shape, dim)


def prep_kernel(kind, counts, known, tokens, tokens_t, packed, slot, meta):
    length = tokens.shape[0]
    cells = length // SHORT_LENGTH
    is_long = kind[0] == 1
    shape = (8, SHORT_LENGTH)
    row = iota(shape, 0)
    col = iota(shape, 1)
    given = jnp.zeros(shape, jnp.int32)
    for cell in range(cells):
        given = jnp.where(row == cell, known[0:1, pl.ds(cell * SHORT_LENGTH, SHORT_LENGTH)], given)
    limit = jnp.zeros(shape, jnp.int32)
    for cell in range(cells):
        limit = jnp.where(row == cell, counts[cell], limit)
    limit = jnp.where(is_long, counts[0] - SHORT_LENGTH * row, limit)
    first = (col == 0) & (jnp.logical_not(is_long) | (row == 0))
    usable = (col < limit) & ((given == 1) | first) & (row < cells)
    usable_f = jnp.where(usable, 1.0, 0.0)
    square = (SHORT_LENGTH, SHORT_LENGTH)
    before = jnp.where(iota(square, 0) < iota(square, 1), 1.0, 0.0).astype(BF)
    rank = mm(usable_f.astype(BF), before, NN).astype(jnp.int32)
    totals = [jnp.sum(usable_f[cell : cell + 1, :]).astype(jnp.int32) for cell in range(cells)]
    base = jnp.zeros(shape, jnp.int32)
    running = jnp.int32(0)
    for cell in range(cells):
        start = jnp.where(is_long, running, SHORT_LENGTH * cell)
        base = jnp.where(row == cell, start, base)
        running = running + totals[cell]
    place = jnp.where(usable, rank + base, -1)
    for cell in range(cells):
        slot[0:1, pl.ds(cell * SHORT_LENGTH, SHORT_LENGTH)] = place[cell : cell + 1, :]
    meta[0] = kind[0]
    for cell in range(cells):
        meta[1 + cell] = jnp.where(is_long, running if cell == 0 else 0, totals[cell])

    for block in range(length // KEY_BLOCK):
        rows = pl.ds(block * KEY_BLOCK, KEY_BLOCK)
        tokens_t[:, rows] = tokens[rows, :].T
        cell = block * KEY_BLOCK // SHORT_LENGTH
        inside = block * KEY_BLOCK - cell * SHORT_LENGTH
        needed = jnp.where(is_long, block * KEY_BLOCK < running, inside < totals[cell])

        @pl.when(needed)
        def _(block=block, rows=rows):
            hot = one_hot(slot, block * KEY_BLOCK, KEY_BLOCK)
            packed[rows, :] = mm(hot, tokens[...], NN).astype(BF)


def one_hot(slot, begin, rows):
    shape = (rows, slot.shape[1])
    hit = (iota(shape, 0) + begin) == slot[0:1, :]
    return jnp.where(hit, 1.0, 0.0).astype(BF)


def prep(kind, counts, known, tokens):
    length, width = tokens.shape
    return pl.pallas_call(
        prep_kernel,
        in_specs=[SMEM, SMEM, whole(1, length), whole(length, width)],
        out_specs=[
            whole(width, length),
            whole(length, width),
            whole(1, length),
            SMEM,
        ],
        out_shape=[
            jax.ShapeDtypeStruct((width, length), BF),
            jax.ShapeDtypeStruct((length, width), BF),
            jax.ShapeDtypeStruct((1, length), jnp.int32),
            jax.ShapeDtypeStruct((8,), jnp.int32),
        ],
        compiler_params=params(56),
        cost_estimate=cost(3e9, 12e6),
        name="prep",
    )(kind, counts, known, tokens)


def fetch_rows(pieces, mine, target, sem, kinds=1):
    rows = pieces[0].shape[0]
    copies = []
    for index, piece in enumerate(pieces):
        owner = jnp.bitwise_xor(mine, index)
        place = pl.ds(pl.multiple_of(owner * rows, rows), rows)
        if kinds == 1:
            copies.append((piece, target.at[place, :]))
            continue
        for pair in range(PAIRS):
            for kind in range(kinds):
                come = piece.at[:, pl.ds(PAIR * (PAIRS * kind + pair), PAIR)]
                copies.append((come, target.at[place, pl.ds(PAIR * (kinds * pair + kind), PAIR)]))
    copies = [pltpu.make_async_copy(*ends, sem.at[index]) for index, ends in enumerate(copies)]
    for copy in copies:
        copy.start()
    for copy in copies:
        copy.wait()


def head_lanes(shape, head):
    lane = iota(shape, 1)
    return (lane >= HDIM * head) & (lane < HDIM * (head + 1))


def spare(head):
    return HDIM * (1 - head)


def key_lanes(block, head, begin, count):
    lane = iota(block.shape, 1) - spare(head)
    row = iota(block.shape, 0) + begin
    bias = jnp.where(row < count, 0.0, MASKED)
    extra = jnp.where(lane == 0, bias, jnp.where((lane > 0) & (lane < 4), 1.0, 0.0))
    return jnp.where(head_lanes(block.shape, head), block.astype(F32), extra).astype(BF)


def split_rows(shift):
    high = shift.astype(BF).astype(F32)
    rest = shift - high
    mid = rest.astype(BF).astype(F32)
    low = rest - mid
    shape = (16, shift.shape[1])
    row = iota(shape, 0)
    out = jnp.where(row == 0, 1.0, 0.0)
    out = jnp.where(row == 1, -high, out)
    out = jnp.where(row == 2, -mid, out)
    return jnp.where(row == 3, -low, out).astype(BF)


def query_side(target, head, rows, shift):
    other = spare(head)
    target[head, HDIM * head : HDIM * (head + 1), :] = rows
    target[head, other : other + 16, :] = split_rows(shift)
    target[head, other + 16 : other + HDIM, :] = jnp.zeros((HDIM - 16, rows.shape[1]), BF)


def walk(meta, length, body, size, tails):
    @pl.when(meta[0] == 1)
    def _():
        cell_walk(meta[1], 0, 0, length, body, size, tails)

    @pl.when(meta[0] != 1)
    def _():
        @pl.loop(0, length // SHORT_LENGTH)
        def _(cell):
            begin = pl.multiple_of(cell * SHORT_LENGTH, SHORT_LENGTH)
            cell_walk(meta[1 + cell], begin, begin, SHORT_LENGTH, body, min(size, SHORT_LENGTH), tails)


def cell_walk(count, slot_begin, query_begin, queries, body, size, tails):
    tails = [tail for tail in tails if tail < size]
    rest = lax.rem(count, size)
    full = count // size + jnp.where(rest > (tails or [0])[-1], 1, 0)
    end = slot_begin + count

    @pl.loop(0, full)
    def _(index):
        begin = pl.multiple_of(slot_begin + index * size, size)
        body(begin, size, query_begin, queries, end)

    for low, tail in zip([0] + tails, tails):

        @pl.when((rest > low) & (rest <= tail))
        def _(tail=tail):
            begin = pl.multiple_of(slot_begin + full * size, size)
            body(begin, tail, query_begin, queries, end)


def forward_kernel(count, mine, meta, *refs):
    pieces = refs[:count]
    tokens_t, packed, slot = refs[count : count + 3]
    q_out, k_out, v_out, kc_out, kct_out, vct_out, context, log_total = refs[count + 3 : count + 11]
    weights, kept_all, turned_all, vct, side, total, shift, sem = refs[count + 11 :]
    step = pl.program_id(0)
    width, length = tokens_t.shape

    @pl.when(step == 0)
    def _():
        fetch_rows(pieces, mine[0], weights, sem)

        def project(begin, rows, *_):
            place = pl.ds(begin, rows)
            both = mm(packed[place, :], weights[:, width:], NN)
            kept_all[place, :] = both[:, :width].astype(BF)
            turned_all[:, place] = both.T.astype(BF)

        walk(meta, length, project, *FORWARD_WALK)

    def here(kind):
        return pl.ds(pl.multiple_of(kind * width + step * PAIR, PAIR), PAIR)

    part = jnp.concatenate([weights[:, here(kind)] for kind in range(3)], axis=1)
    joined = mm(part, tokens_t[...], TN)
    q_out[...] = (joined[:PAIR] * HDIM**-0.5).astype(BF)
    k_out[...] = joined[PAIR : 2 * PAIR].astype(BF)
    v_out[...] = joined[2 * PAIR :].astype(BF)
    kc_out[...] = kept_all[:, here(0)]
    kct_out[...] = turned_all[here(0), :]
    vct_out[...] = turned_all[here(1), :]
    ones = jnp.where(iota((16, length), 0) == 0, 1.0, 0.0).astype(BF)
    for head in range(2):
        vct[head, :HDIM, :] = vct_out[HDIM * head : HDIM * (head + 1), :]
        vct[head, HDIM:, :] = ones

    masked = slot[...] < 0
    own = []
    for head in range(2):
        rows = slice(HDIM * head, HDIM * (head + 1))
        queries = q_out[rows, :].astype(F32)
        keys = k_out[rows, :].astype(F32)
        own.append(jnp.where(masked, jnp.sum(queries * keys, axis=0, keepdims=True), MASKED))
        top_q = jnp.max(jnp.sum(queries * queries, axis=0, keepdims=True))
        top_k = jnp.max(jnp.sum(keys * keys, axis=0, keepdims=True))
        unsafe = jnp.logical_not(top_q * top_k < SAFE_SCORE * SAFE_SCORE)
        shift[head : head + 1, :] = jnp.zeros((1, length), F32)
        query_side(side, head, q_out[rows, :], jnp.zeros((1, length), F32))

        @pl.when(unsafe)
        def _(head=head, rows=rows):
            shift[head : head + 1, :] = own[head]

            def raise_top(begin, rows, first, queries, end):
                keys = key_lanes(kc_out[pl.ds(begin, rows), :], head, begin, end)
                place = pl.ds(first, queries)
                scores = mm(keys, side[head, :, place], NN)
                top = jnp.max(scores, axis=0, keepdims=True)
                shift[head : head + 1, place] = jnp.maximum(shift[head : head + 1, place], top)

            walk(meta, length, raise_top, 128, ())
            query_side(side, head, q_out[rows, :], shift[head : head + 1, :])

    total[...] = jnp.zeros(total.shape, F32)

    def attend(begin, rows, first, queries, end):
        slots = pl.ds(begin, rows)
        place = pl.ds(first, queries)
        for head in range(2):
            keys = key_lanes(kc_out[slots, :], head, begin, end)
            raised = jnp.exp(mm(keys, side[head, :, place], NN)).astype(BF)
            total[head, :, place] += mm(vct[head, :, slots], raised, NN)

    walk(meta, length, attend, *FORWARD_WALK)

    for head in range(2):
        rows = slice(HDIM * head, HDIM * (head + 1))
        alone = jnp.exp(own[head] - shift[head : head + 1, :])
        row_total = total[head, HDIM : HDIM + 1, :] + alone
        gathered = total[head, :HDIM, :] + v_out[rows, :].astype(F32) * alone
        context[rows, :] = (gathered * (1.0 / row_total)).astype(BF)
        log_total[pl.ds(step * 2 + head, 1), :] = shift[head : head + 1, :] + jnp.log(row_total)


def forward(mine, meta, pieces, tokens_t, packed, slot):
    width, length = tokens_t.shape
    pair_rows = pl.BlockSpec((PAIR, length), lambda step: (step, 0))
    pair_lanes = pl.BlockSpec((length, PAIR), lambda step: (0, step))
    transposed = jax.ShapeDtypeStruct((width, length), BF)
    natural = jax.ShapeDtypeStruct((length, width), BF)
    count = len(pieces)
    return pl.pallas_call(
        partial(forward_kernel, count),
        grid=(PAIRS,),
        in_specs=[SMEM, SMEM]
        + [ANY] * count
        + [whole(width, length), whole(length, width), whole(1, length)],
        out_specs=[pair_rows] * 3 + [pair_lanes] + [pair_rows] * 3 + [whole(HEADS, length)],
        out_shape=[transposed] * 3
        + [natural]
        + [transposed] * 3
        + [jax.ShapeDtypeStruct((HEADS, length), F32)],
        scratch_shapes=[
            pltpu.VMEM((width, 3 * width), BF),
            pltpu.VMEM((length, width), BF),
            pltpu.VMEM((2 * width, length), BF),
            pltpu.VMEM((2, HDIM + 16, length), BF),
            pltpu.VMEM((2, PAIR, length), BF),
            pltpu.VMEM((2, HDIM + 16, length), F32),
            pltpu.VMEM((8, length), F32),
            pltpu.SemaphoreType.DMA((count,)),
        ],
        compiler_params=params(56),
        cost_estimate=cost(15e9, 25e6, 20e6),
        name="attend_forward",
    )(mine, meta, *pieces, tokens_t, packed, slot)


def backward_kernel(owners, pair_ref, mine, meta, *refs):
    pair = pair_ref[0]
    q_t, kc, kct, vct, grad_context, log_total, inner, slot, k_far, v_far, tokens_far = refs[:11]
    before = refs[11:-14][:2] if len(refs) == 28 else ()
    grad_far, keep, send = refs[-14:-11]
    turned_side, q_side, g_side, grad_q, grad_kv, ready, k_t, v_t, tokens_t, grad_t, sem = refs[-11:]
    length = q_t.shape[1]
    rows = pl.ds(pl.multiple_of(PAIR * pair, PAIR), PAIR)
    come = [
        pltpu.make_async_copy(k_far.at[rows, :], k_t, sem.at[0]),
        pltpu.make_async_copy(v_far.at[rows, :], v_t, sem.at[1]),
        pltpu.make_async_copy(tokens_far, tokens_t, sem.at[2]),
    ]
    for index, (part, target) in enumerate(zip(before, (keep, send))):
        target = target.at[:, pl.ds(0, part.shape[1])]
        come.append(pltpu.make_async_copy(part, target, sem.at[4 + index]))
    for copy in come:
        copy.start()

    for head in range(2):
        lanes = slice(HDIM * head, HDIM * (head + 1))
        index = 2 * pair + head
        query_side(turned_side, head, q_t[lanes, :], log_total[pl.ds(index, 1), :])
        q_side[head] = turned_side[head].T
        query_side(turned_side, head, grad_context[lanes, :], inner[pl.ds(index, 1), :])
        g_side[head] = turned_side[head].T
    grad_q[...] = jnp.zeros(grad_q.shape, F32)
    grad_kv[...] = jnp.zeros(grad_kv.shape, F32)
    ready[...] = jnp.zeros(ready.shape, BF)

    def pull(begin, count, first, queries, end):
        slots = pl.ds(begin, count)
        place = pl.ds(first, queries)
        keys = kc[slots, :]
        for head in range(2):
            lanes = slice(HDIM * head, HDIM * (head + 1))
            key_rows = key_side(kct[lanes, slots], head, begin, end)
            value_rows = key_side(vct[lanes, slots], head, begin, None)
            probs = jnp.exp(mm(q_side[head, place, :], key_rows, NN))
            pulled = mm(g_side[head, place, :], value_rows, NN)
            grad_scores = (probs * pulled).astype(BF)
            own_keys = jnp.where(head_lanes(keys.shape, head), keys.astype(F32), 0.0).astype(BF)
            grad_q[place, :] += mm(grad_scores, own_keys, NN)
            ready[lanes, slots] = mm(q_t[lanes, place], grad_scores, NN).astype(BF)
            ready[PAIR + HDIM * head : PAIR + HDIM * (head + 1), slots] = mm(
                grad_context[lanes, place], probs.astype(BF), NN
            ).astype(BF)

    walk(meta, length, pull, *BACKWARD_WALK)

    def scatter(begin, count, first, queries, end):
        slots = pl.ds(begin, count)
        place = pl.ds(first, queries)
        hit = (iota((count, queries), 0) + begin) == slot[0:1, place]
        spread = jnp.where(hit, 1.0, 0.0).astype(BF)
        grad_kv[:, place] += mm(ready[:, slots], spread, NN)

    walk(meta, length, scatter, 512, (256,))

    for copy in come:
        copy.wait()
    masked = slot[...] < 0
    turned = grad_q[...].T
    for head in range(2):
        lanes = slice(HDIM * head, HDIM * (head + 1))
        index = 2 * pair + head
        queries = q_t[lanes, :].astype(F32)
        keys = k_t[lanes, :].astype(F32)
        values = v_t[lanes, :].astype(F32)
        grads = grad_context[lanes, :].astype(F32)
        own = jnp.sum(queries * keys, axis=0, keepdims=True)
        own = jnp.where(masked, own - log_total[pl.ds(index, 1), :], MASKED)
        alone = jnp.exp(own)
        pulled = jnp.sum(grads * values, axis=0, keepdims=True) - inner[pl.ds(index, 1), :]
        pulled = (alone * pulled).astype(BF).astype(F32)
        alone = alone.astype(BF).astype(F32)
        part = (turned[lanes, :] + keys * pulled) * HDIM**-0.5
        grad_t[HDIM * head : HDIM * (head + 1), :] = part.astype(BF)
        part = grad_kv[lanes, :] + queries * pulled
        grad_t[PAIR + HDIM * head : PAIR + HDIM * (head + 1), :] = part.astype(BF)
        part = grad_kv[PAIR + HDIM * head : PAIR + HDIM * (head + 1), :] + grads * alone
        grad_t[2 * PAIR + HDIM * head : 2 * PAIR + HDIM * (head + 1), :] = part.astype(BF)
    mine_rows = pl.ds(pl.multiple_of(3 * PAIR * pair, 3 * PAIR), 3 * PAIR)
    leave = pltpu.make_async_copy(grad_t, grad_far.at[mine_rows, :], sem.at[3])
    leave.start()
    take_apart([mm(tokens_t[...], grad_t[...], NT)], mine[0], keep, send, owners)
    leave.wait()


def key_side(rows, head, begin, end):
    shape = (16, rows.shape[1])
    row = iota(shape, 0)
    extra = jnp.where((row > 0) & (row < 4), 1.0, 0.0)
    if end is not None:
        bias = jnp.where(iota(shape, 1) + begin < end, 0.0, MASKED)
        extra = jnp.where(row == 0, bias, extra)
    blank = jnp.zeros((HDIM - 16, rows.shape[1]), BF)
    extra = [extra.astype(BF), blank]
    return jnp.concatenate([rows] + extra if head == 0 else extra + [rows], axis=0)


def backward(
    pair, mine, owners, before, into, meta, q_t, k_t, v_t, kc, kct, vct, grad_context, log_total, inner,
    slot, tokens_t,
):
    more = [*before] + [part for part in (into,) if part is not None]
    width, length = tokens_t.shape
    pair_rows = pl.BlockSpec((PAIR, length), lambda step, place: (place[0], 0))
    pair_lanes = pl.BlockSpec((length, PAIR), lambda step, place: (0, place[0]))
    columns = 3 * PAIR + (before[0].shape[1] if before else 0)
    half = jax.ShapeDtypeStruct((width // 2, columns), BF)
    return pl.pallas_call(
        partial(backward_kernel, owners),
        grid_spec=pltpu.PrefetchScalarGridSpec(
            num_scalar_prefetch=1,
            grid=(1,),
            in_specs=[SMEM, SMEM, pair_rows, pair_lanes]
            + [pair_rows] * 3
            + [whole(HEADS, length)] * 2
            + [whole(1, length)]
            + [ANY] * (3 + len(more)),
            out_specs=[ANY] + [whole(*half.shape)] * 2,
            scratch_shapes=[
                pltpu.VMEM((2, PAIR, length), BF),
                pltpu.VMEM((2, length, PAIR), BF),
                pltpu.VMEM((2, length, PAIR), BF),
                pltpu.VMEM((length, PAIR), F32),
                pltpu.VMEM((2 * PAIR, length), F32),
                pltpu.VMEM((2 * PAIR, length), BF),
                pltpu.VMEM((PAIR, length), BF),
                pltpu.VMEM((PAIR, length), BF),
                pltpu.VMEM((width, length), BF),
                pltpu.VMEM((3 * PAIR, length), BF),
                pltpu.SemaphoreType.DMA((6,)),
            ],
        ),
        out_shape=[jax.ShapeDtypeStruct((3 * width, length), BF), half, half],
        input_output_aliases={} if into is None else {13 + len(more): 0},
        compiler_params=params(48),
        cost_estimate=cost(12e9, 10e6, 6e6),
        name="attend_backward",
    )(
        jnp.full((1,), pair, jnp.int32), mine, meta, q_t, kc, kct, vct, grad_context, log_total,
        inner, slot, k_t, v_t, tokens_t, *more,
    )


def feature_mean(values):
    return jnp.sum(values, axis=0, keepdims=True) * (1.0 / values.shape[0])


def normalise(values):
    centred = values - feature_mean(values)
    scale = lax.rsqrt(feature_mean(centred * centred) + NORM_EPS)
    return centred * scale, scale


def pull_norm(grad, scaled, scale, gain):
    lifted = grad * gain
    return scale * (lifted - feature_mean(lifted) - scaled * feature_mean(lifted * scaled))


def lane_sums(values):
    width = 128
    out = values[:, :width]
    for begin in range(width, values.shape[1], width):
        out = out + values[:, begin : begin + width]
    return out


def dense_kernel(count, mine, kind, study, *refs):
    pieces = refs[:count]
    tokens_t, context, cot_far = refs[count : count + 3]
    out, grad_context, grad_first, inner, keep, send, small = refs[count + 3 : count + 10]
    weights, total, norm_total, firsts, sem = refs[count + 10 :]
    step = pl.program_id(0)
    width = tokens_t.shape[0]

    @pl.when(step == 0)
    def _():
        fetch_rows(pieces, mine[0], weights, sem)
        total[...] = jnp.zeros(total.shape, F32)
        norm_total[...] = jnp.zeros(norm_total.shape, F32)

    proj = weights[:, :width]
    up = weights[:, width : 2 * width]
    down = weights[:, 2 * width : 3 * width]
    rows = weights[:, 3 * width :].astype(F32)
    gain1, bias1, gain2, bias2 = (rows[:, index : index + 1] for index in range(4))

    def part(place):
        context_low = context[:, place]
        first_sum = tokens_t[:, place].astype(F32) + mm(proj, context_low, TN)
        yield
        scaled1, scale1 = normalise(first_sum)
        middle = scaled1 * gain1 + bias1
        middle_low = middle.astype(BF)
        hidden = mm(up, middle_low, TN)
        yield
        cdf = 0.5 * (1.0 + lax.erf(hidden * 2.0**-0.5))
        slope = cdf + hidden * jnp.exp(hidden * hidden * -0.5) * 0.3989422804014327
        active = (hidden * cdf).astype(BF)
        second_sum = middle + mm(down, active, TN)
        yield
        scaled2, scale2 = normalise(second_sum)
        result = (scaled2 * gain2 + bias2).astype(BF).T
        out[place, :] = result
        if place.start % SHORT_LENGTH == 0:
            cell = 2 * step + place.start // SHORT_LENGTH
            firsts[pl.ds(cell, 1), :] = result[:8].astype(F32)[0:1]
        cot = cot_far[place, :].T.astype(F32)
        norm_total[2] += lane_sums(cot * scaled2)
        norm_total[3] += lane_sums(cot)
        grad_second = pull_norm(cot, scaled2, scale2, gain2)
        grad_low = grad_second.astype(BF)
        pulled = mm(down, grad_low, NN)
        total[2] += mm(active, grad_low, NT)
        yield
        grad_hidden = (pulled * slope).astype(BF)
        grad_middle = grad_second + mm(up, grad_hidden, NN)
        total[1] += mm(middle_low, grad_hidden, NT)
        yield
        norm_total[0] += lane_sums(grad_middle * scaled1)
        norm_total[1] += lane_sums(grad_middle)
        grad_h1 = pull_norm(grad_middle, scaled1, scale1, gain1)
        proj_low = grad_h1.astype(BF)
        grad_first[:, place] = proj_low
        pulled = mm(proj, proj_low, NN)
        total[0] += mm(context_low, proj_low, NT)
        yield
        pulled = pulled.astype(BF)
        grad_context[:, place] = pulled
        both = pulled.astype(F32) * context_low.astype(F32)
        for head in range(HEADS):
            part = both[HDIM * head : HDIM * (head + 1), :]
            inner[head : head + 1, place] = jnp.sum(part, axis=0, keepdims=True)

    columns = tokens_t.shape[1] // 4
    parts = [part(slice(columns * index, columns * (index + 1))) for index in range(4)]
    turn = 0
    while parts:
        parts = [stage for index, stage in enumerate(parts) if next(stage, stage) is None]
        turn += 1

    @pl.when(step == pl.num_programs(0) - 1)
    def _():
        take_apart([total.at[index] for index in range(3)], mine[0], keep, send, count)
        lane = iota((width, 128), 1)
        packed = jnp.zeros((width, 128), F32)
        for index in range(4):
            column = jnp.sum(norm_total[index], axis=1, keepdims=True)
            packed = jnp.where(lane == index, column, packed)
        row = iota((STUDY_COUNT, width), 0)
        sums = [jnp.zeros((STUDY_COUNT, width), F32)] * 3
        for cell in range(firsts.shape[0]):
            hit = (row == study[cell]) & ((kind[0] == 0) | (cell == 0))
            first = firsts[cell : cell + 1, :]
            for index, term in enumerate((1.0, first, first * first)):
                sums[index] = sums[index] + jnp.where(hit, term, 0.0)
        for index in range(3):
            small[STUDY_COUNT * index : STUDY_COUNT * (index + 1), :] = sums[index]
        small[3 * STUDY_COUNT :, :] = packed.T[:8]


def take_apart(totals, mine, keep, send, owners):
    first = lax.rem(mine, 2) == 0
    at = keep.shape[1] - sum(total.shape[1] for total in totals)
    for total in totals:
        rows, columns = total.shape[0] // owners, total.shape[1]
        for half in range(owners // 2):
            even = total[2 * half * rows : (2 * half + 1) * rows, :].astype(BF)
            odd = total[(2 * half + 1) * rows : (2 * half + 2) * rows, :].astype(BF)
            here = slice(half * rows, (half + 1) * rows)
            keep[here, at : at + columns] = jnp.where(first, even, odd)
            send[here, at : at + columns] = jnp.where(first, odd, even)
        at += columns


def dense(mine, kind, study, pieces, tokens_t, context, cot):
    width, length = tokens_t.shape
    block = 2 * SHORT_LENGTH
    count = len(pieces)
    columns = pl.BlockSpec((width, block), lambda step: (0, step))
    rows = pl.BlockSpec((block, width), lambda step: (step, 0))
    return pl.pallas_call(
        partial(dense_kernel, count),
        grid=(length // block,),
        in_specs=[SMEM] * 3 + [ANY] * count + [columns, columns, rows],
        out_specs=[
            rows,
            columns,
            columns,
            pl.BlockSpec((HEADS, block), lambda step: (0, step)),
            whole(width // 2, 3 * width),
            whole(width // 2, 3 * width),
            whole(4 * STUDY_COUNT, width),
        ],
        out_shape=[
            jax.ShapeDtypeStruct((length, width), BF),
            jax.ShapeDtypeStruct((width, length), BF),
            jax.ShapeDtypeStruct((width, length), BF),
            jax.ShapeDtypeStruct((HEADS, length), F32),
            jax.ShapeDtypeStruct((width // 2, 3 * width), BF),
            jax.ShapeDtypeStruct((width // 2, 3 * width), BF),
            jax.ShapeDtypeStruct((4 * STUDY_COUNT, width), F32),
        ],
        scratch_shapes=[
            pltpu.VMEM((width, 3 * width + 128), BF),
            pltpu.VMEM((3, width, width), F32),
            pltpu.VMEM((4, width, 128), F32),
            pltpu.VMEM((length // SHORT_LENGTH, width), F32),
            pltpu.SemaphoreType.DMA((count,)),
        ],
        compiler_params=params(48),
        cost_estimate=cost(10e9, 20e6, 4e6),
        name="dense",
    )(mine, kind, study, *pieces, tokens_t, context, cot)


def input_kernel(count, mine, *refs):
    pieces = refs[:count]
    grads, grad_first = refs[count : count + 2]
    out, weights, sem = refs[-3:]

    @pl.when(pl.program_id(0) == 0)
    def _():
        fetch_rows(pieces, mine[0], weights, sem, 3)

    total = grad_first[...].T.astype(F32)
    total = total + mm(grads[...], weights[...], (((0,), (1,)), ((), ())))
    out[...] = total.astype(BF)


def input_side(mine, pieces, grads, grad_first, into=None):
    width, length = grad_first.shape
    block = 512
    count = len(pieces)
    steps = length // block // 2
    begin = 0 if into is None else steps
    kept = [] if into is None else [into]
    return pl.pallas_call(
        partial(input_kernel, count),
        grid=(steps,),
        in_specs=[SMEM]
        + [ANY] * count
        + [pl.BlockSpec((3 * width, block), lambda step: (0, step + begin))]
        + [pl.BlockSpec((width, block), lambda step: (0, step + begin))]
        + [ANY] * len(kept),
        out_specs=pl.BlockSpec((block, width), lambda step: (step + begin, 0)),
        out_shape=jax.ShapeDtypeStruct((length, width), BF),
        scratch_shapes=[
            pltpu.VMEM((width, 3 * width), BF),
            pltpu.SemaphoreType.DMA((3 * PAIRS * count,)),
        ],
        compiler_params=params(40),
        cost_estimate=cost(3.3e9, 14e6),
        name="input_side",
        input_output_aliases={} if into is None else {3 + count: 0},
    )(mine, *pieces, grads, grad_first, *kept)


def swap(value, axis, size, mask):
    return lax.ppermute(value, axis, [(index, index ^ mask) for index in range(size)])


def masks_of(size):
    return [1 << bit for bit in range(size.bit_length() - 1)]


def gather_direct(piece, axis, size):
    return [piece] + [swap(piece, axis, size, mask) for mask in range(1, size)]


def halving(keep, send, axis, size):
    mine = lax.axis_index(axis)
    rows = 2 * keep.shape[0] // size
    got = yield send, axis, size, 1
    value = (keep.astype(F32) + got.astype(F32)).astype(BF).reshape(size // 2, rows, -1)
    for bit, mask in list(enumerate(masks_of(size)))[1:]:
        value = value.reshape(value.shape[0] // 2, 2, rows, -1).swapaxes(0, 1)
        side = (mine >> bit) & 1
        send = lax.dynamic_index_in_dim(value, 1 - side, 0, keepdims=False)
        got = yield send, axis, size, mask
        keep = lax.dynamic_index_in_dim(value, side, 0, keepdims=False)
        value = (keep.astype(F32) + got.astype(F32)).astype(value.dtype)
    return value.reshape(rows, -1)


def doubling(value, axis, size):
    for mask in masks_of(size):
        got = yield value, axis, size, mask
        value = (value.astype(F32) + got.astype(F32)).astype(value.dtype)
    return value


def side_steps(keep, send, fsdp, dp):
    value = yield from halving(keep, send, "fsdp", fsdp)
    return (yield from doubling(value, "dp", dp))


def small_steps(value, fsdp, dp):
    value = yield from doubling(value, "fsdp", fsdp)
    return (yield from doubling(value, "dp", dp))


class Chain:
    def __init__(self, steps):
        self.steps, self.result, self.got = steps, None, None
        self.request = next(steps)

    def send(self, value):
        _, axis, size, mask = self.request
        self.got = swap(value, axis, size, mask)

    def land(self, value):
        try:
            self.request = self.steps.send(value)
        except StopIteration as end:
            self.request, self.result = None, end.value

    def finish(self):
        while self.request is not None:
            if self.got is None:
                self.send(self.request[0])
            value, self.got = self.got, None
            self.land(value)
        return self.result


def start_steps(anchor, chains):
    live = [chain for chain in chains if chain.request is not None]
    anchor, *values = lax.optimization_barrier((anchor, *(chain.request[0] for chain in live)))
    for chain, value in zip(live, values):
        chain.send(value)
    return anchor


def end_steps(anchor, chains):
    live = [chain for chain in chains if chain.got is not None]
    anchor, values = lax.optimization_barrier((anchor, [chain.got for chain in live]))
    for chain, value in zip(live, values):
        chain.got = None
        chain.land(value)
    return anchor


def spread_kernel(parts, out):
    total = jnp.sum(parts[...].astype(F32), axis=0).astype(BF)
    for index in range(out.shape[0]):
        out[index] = total


def spread_sums(parts):
    return pl.pallas_call(
        spread_kernel,
        out_shape=jax.ShapeDtypeStruct(parts.shape, BF),
        cost_estimate=cost(1e6, 1e6),
        name="spread",
    )(parts)


def moments(gradient, first_old, second_old):
    first_new = BETA * first_old + (1.0 - BETA) * gradient
    second_new = BETA * second_old + (1.0 - BETA) * gradient * gradient
    return first_new, second_new


def update_of(first_new, second_new):
    debias = 1.0 - BETA**STEP
    return first_new / debias / (jnp.sqrt(second_new / debias) + ADAM_EPS)


def square_row(values):
    total = jnp.sum(values * values, axis=0, keepdims=True)
    return lane_sums(total)


def moments_kernel(count, paired, gradient, *refs):
    olds, outs, squares = refs[: 3 * count], refs[3 * count : 6 * count], refs[6 * count]
    at = 0

    @pl.when(pl.program_id(0) == 0)
    def _():
        squares[...] = jnp.zeros(squares.shape, F32)

    for index in range(count):
        weight, first_old, second_old = (ref[...] for ref in olds[3 * index : 3 * index + 3])
        columns = weight.shape[1]
        if paired:
            places = [
                3 * PAIR * (PAIRS - 1 - pair) + PAIR * kind
                for kind in range(3)
                for pair in range(PAIRS)
            ]
            grad = jnp.concatenate([gradient[:, at : at + PAIR] for at in places], axis=1)
        else:
            grad = gradient[:, at : at + columns]
        grad = grad.astype(F32)
        at += columns
        first_new, second_new = moments(grad, first_old, second_old)
        update = update_of(first_new, second_new) + MATRIX_DECAY * weight
        for place, value in enumerate((first_new, second_new, update)):
            outs[3 * index + place][...] = value
        squares[index : index + 1, :] += square_row(weight)
        squares[4 + index : 5 + index, :] += square_row(update)


def row_blocks(arrays):
    rows = arrays[0].shape[0]
    steps = rows // 32 if rows % 32 == 0 else 1
    return steps, [
        pl.BlockSpec((rows // steps, array.shape[1]), lambda step: (step, 0)) for array in arrays
    ]


def new_moments(gradient, olds, paired):
    count = len(olds) // 3
    outs = [jax.ShapeDtypeStruct(old.shape, F32) for old in olds]
    steps, in_specs = row_blocks((gradient, *olds))
    results = pl.pallas_call(
        partial(moments_kernel, count, paired),
        grid=(steps,),
        in_specs=in_specs,
        out_specs=row_blocks(outs)[1] + [whole(8, 128)],
        out_shape=outs + [jax.ShapeDtypeStruct((8, 128), F32)],
        compiler_params=params(32 if paired else 60),
        cost_estimate=cost(5e6, 5e6),
        name="moments",
    )(gradient, *olds)
    return results[:-1], results[-1]


def apply_kernel(count, squares, *refs):
    inputs, outs, norms = refs[: 2 * count], refs[2 * count : 4 * count], refs[4 * count]
    total = jnp.sum(jnp.sum(squares[...], axis=0), axis=1, keepdims=True)
    size = jnp.sqrt(total)
    ratio = size[0:4] / size[4:8]
    lane = iota((1, 4), 1)
    rows = [jnp.zeros((1, 4), F32)] * 3
    for index in range(count):
        weight, update = inputs[2 * index][...], inputs[2 * index + 1][...]
        trust = ratio[index : index + 1]
        weight = weight - MATRIX_RATE * trust * update
        outs[2 * index][...] = weight
        outs[2 * index + 1][...] = weight.astype(BF)
        for place, value in enumerate((size[index : index + 1], size[4 + index : 5 + index], trust)):
            rows[place] = jnp.where(lane == index, value, rows[place])
    for place in range(3):
        norms[place : place + 1, :] = rows[place]


def apply_updates(squares, arrays):
    count = len(arrays) // 2
    outs = []
    for weight in arrays[::2]:
        outs += [jax.ShapeDtypeStruct(weight.shape, F32), jax.ShapeDtypeStruct(weight.shape, BF)]
    steps, in_specs = row_blocks(arrays)
    results = pl.pallas_call(
        partial(apply_kernel, count),
        grid=(steps,),
        in_specs=[whole(*squares.shape)] + in_specs,
        out_specs=row_blocks(outs)[1] + [whole(3, 4)],
        out_shape=outs + [jax.ShapeDtypeStruct((3, 4), F32)],
        compiler_params=params(32),
        cost_estimate=cost(5e6, 8e6),
        name="apply",
    )(squares, *arrays)
    return results[:-1], results[-1]


def shards(
    fsdp,
    dp,
    tokens,
    cotangent,
    known_genes,
    cell_kind,
    gene_counts,
    study_index,
    qkv_weight,
    qkv_first,
    qkv_second,
    proj_weight,
    proj_first,
    proj_second,
    up_weight,
    up_first,
    up_second,
    down_weight,
    down_first,
    down_second,
    norm_params,
    norm_first,
    norm_second,
):
    _, length, width = tokens.shape
    mine = lax.axis_index("fsdp").astype(jnp.int32)
    mine_ref = mine.reshape(1)

    tokens_t, packed, slot, meta = prep(
        cell_kind, gene_counts.reshape(-1), known_genes, tokens[0]
    )
    norm_columns = jnp.pad(norm_params.T, ((0, 0), (0, 124)))
    rest = jnp.concatenate([proj_weight, up_weight, down_weight, norm_columns], axis=1).astype(BF)
    own = qkv_weight.astype(BF)
    core, *far_masks = masks_of(fsdp)
    far = {0: own}
    for mask in reversed(far_masks):
        far.update({known ^ mask: swap(far[known], "fsdp", fsdp, mask) for known in far})
    names = sorted(far)[1:]
    slot, *values = lax.optimization_barrier((slot, *(far[name] for name in names)))
    far.update(zip(names, values))
    pieces = dict(far)
    pieces.update({known ^ core: swap(far[known], "fsdp", fsdp, core) for known in far})
    rest, far_piece = lax.optimization_barrier((rest, pieces[names[-1]]))
    pieces[names[-1]] = far_piece
    rest_pieces = gather_direct(rest, "fsdp", fsdp)
    qkv_pieces = [pieces[index] for index in range(fsdp)]
    q_t, k_t, v_t, kc, kct, vct, context, log_total = forward(
        mine_ref, meta, qkv_pieces, tokens_t, packed, slot
    )
    *rest_pieces, context = lax.optimization_barrier((*rest_pieces, context))
    out, grad_context, grad_first, inner, keep, send, small = dense(
        mine_ref, cell_kind, study_index.reshape(-1), rest_pieces, tokens_t, context, cotangent[0]
    )
    side_chain = Chain(side_steps(keep, send, fsdp, dp))
    small_chain = Chain(small_steps(small, fsdp, dp))
    meta = start_steps(meta, [side_chain])
    meta = end_steps(meta, [side_chain])
    chains = [side_chain, small_chain]
    half_chains = []
    grads = None
    before = ()
    for pair in reversed(range(PAIRS)):
        meta = start_steps(meta, chains)
        grads, *before = backward(
            pair, mine_ref, fsdp, before, grads, meta, q_t, k_t, v_t, kc, kct, vct, grad_context, log_total,
            inner, slot, tokens_t,
        )
        before = list(end_steps(tuple(before), chains))
        if pair % 2 == 0:
            half_chains.append(Chain(halving(*before, "fsdp", fsdp)))
            chains.append(half_chains[-1])
            before = ()
    late = half_chains[-1:]
    side_share = side_chain.finish()
    mine_ref = start_steps(mine_ref, late)
    mine_ref = end_steps(mine_ref, late)
    mine_ref = start_steps(mine_ref, late + [small_chain])
    input_grad = input_side(mine_ref, qkv_pieces, grads, grad_first)
    input_grad = end_steps(input_grad, late + [small_chain])
    qkv_share = jnp.concatenate([chain.finish() for chain in half_chains], axis=1)
    qkv_share, mine_ref = lax.optimization_barrier((qkv_share, mine_ref))
    rows = qkv_share.shape[0]
    parts = lax.all_to_all(qkv_share, "dp", 0, 0, tiled=True)
    input_grad = input_side(mine_ref, qkv_pieces, grads, grad_first, input_grad)
    parts, input_grad = lax.optimization_barrier((parts, input_grad))
    parts = spread_sums(parts.reshape(dp, rows // dp, -1)).reshape(rows, -1)
    qkv_share = lax.all_to_all(parts, "dp", 0, 0, tiled=True)
    side_share, _ = lax.optimization_barrier((side_share, parts))
    side_old = (proj_weight, proj_first, proj_second, up_weight, up_first, up_second)
    side_old += (down_weight, down_first, down_second)
    side_new, side_squares = new_moments(side_share, side_old, False)
    qkv_share, side_squares = lax.optimization_barrier((qkv_share, side_squares))
    small = small_chain.finish()
    study_mean = small[8:16] / small[:8]
    study_var = small[16:24] / small[:8] - study_mean * study_mean
    norm_share = lax.dynamic_slice_in_dim(small[24:28], mine * (width // fsdp), width // fsdp, 1)
    norm_first, norm_second = moments(norm_share, norm_first, norm_second)
    norm_params = norm_params - VECTOR_RATE * update_of(norm_first, norm_second)

    (qkv_first, qkv_second, qkv_update), qkv_squares = new_moments(
        qkv_share, (qkv_weight, qkv_first, qkv_second), True
    )
    squares = jnp.concatenate(
        [qkv_squares[0:1], side_squares[0:3], qkv_squares[4:5], side_squares[4:7]], axis=0
    )
    squares = jnp.stack(gather_direct(squares, "fsdp", fsdp))
    arrays = (qkv_weight, qkv_update, proj_weight, side_new[2])
    arrays += (up_weight, side_new[5], down_weight, side_new[8])
    applied, matrix_norms = apply_updates(squares, arrays)
    firsts = (qkv_first, side_new[0], side_new[3], side_new[6])
    seconds = (qkv_second, side_new[1], side_new[4], side_new[7])
    results = []
    for index in range(4):
        results += [firsts[index], seconds[index], applied[2 * index], applied[2 * index + 1]]
    return (
        out.reshape(tokens.shape),
        input_grad.reshape(tokens.shape),
        study_mean,
        study_var,
        *results,
        norm_first,
        norm_second,
        norm_params,
        norm_params.astype(BF),
        matrix_norms,
    )


def solution(mesh):
    whole_groups = P(("dp", "fsdp"))
    rows = P("fsdp", None)
    columns = P(None, "fsdp")
    return jax.shard_map(
        partial(shards, mesh.shape["fsdp"], mesh.shape["dp"]),
        mesh=mesh,
        in_specs=(whole_groups,) * 6 + (rows,) * 12 + (columns,) * 3,
        out_specs=(whole_groups,) * 2 + (P(), P()) + (rows,) * 16 + (columns,) * 4 + (P(),),
        check_vma=False,
    )
```

```python
from functools import partial

import jax
import jax.numpy as jnp
from jax import lax
from jax.experimental import pallas as pl
from jax.experimental.pallas import tpu as pltpu
from jax.sharding import PartitionSpec as P

HEADS = 8
HDIM = 64
SHORT_LENGTH = 512
STUDY_COUNT = 8
STEP = 5
PAIR = 2 * HDIM
PAIRS = HEADS // 2
KEY_BLOCK = 256
FORWARD_WALK = 512, (128, 256)
BACKWARD_WALK = 256, (128,)


BETA = 0.5
ADAM_EPS = 1e-06
NORM_EPS = 1e-05
MATRIX_RATE = 0.5
VECTOR_RATE = 0.3
MATRIX_DECAY = 0.01
MASKED = -1000000000.0
SAFE_SCORE = 40.0

BF = jnp.bfloat16
F32 = jnp.float32
NN = (((1,), (0,)), ((), ()))
NT = (((1,), (1,)), ((), ()))
TN = (((0,), (0,)), ((), ()))
SMEM = pl.BlockSpec(memory_space=pltpu.SMEM)
ANY = pl.BlockSpec(memory_space=pl.ANY)


def mm(left, right, dims):
    return lax.dot_general(left, right, dims, preferred_element_type=F32)


def whole(*shape):
    return pl.BlockSpec(shape, lambda *_: (0,) * len(shape))


def params(mebibytes):
    return pltpu.CompilerParams(vmem_limit_bytes=mebibytes * 2**20)


def cost(flops, nbytes, trans=0):
    return pl.CostEstimate(flops=int(flops), bytes_accessed=int(nbytes), transcendentals=int(trans))


def iota(shape, dim):
    return lax.broadcasted_iota(jnp.int32, shape, dim)


def prep_kernel(kind, counts, known, tokens, tokens_t, packed, slot, meta):
    length = tokens.shape[0]
    cells = length // SHORT_LENGTH
    is_long = kind[0] == 1
    shape = (8, SHORT_LENGTH)
    row = iota(shape, 0)
    col = iota(shape, 1)
    given = jnp.zeros(shape, jnp.int32)
    for cell in range(cells):
        given = jnp.where(row == cell, known[0:1, pl.ds(cell * SHORT_LENGTH, SHORT_LENGTH)], given)
    limit = jnp.zeros(shape, jnp.int32)
    for cell in range(cells):
        limit = jnp.where(row == cell, counts[cell], limit)
    limit = jnp.where(is_long, counts[0] - SHORT_LENGTH * row, limit)
    first = (col == 0) & (jnp.logical_not(is_long) | (row == 0))
    usable = (col < limit) & ((given == 1) | first) & (row < cells)
    usable_f = jnp.where(usable, 1.0, 0.0)
    square = (SHORT_LENGTH, SHORT_LENGTH)
    before = jnp.where(iota(square, 0) < iota(square, 1), 1.0, 0.0).astype(BF)
    rank = mm(usable_f.astype(BF), before, NN).astype(jnp.int32)
    totals = [jnp.sum(usable_f[cell : cell + 1, :]).astype(jnp.int32) for cell in range(cells)]
    base = jnp.zeros(shape, jnp.int32)
    running = jnp.int32(0)
    for cell in range(cells):
        start = jnp.where(is_long, running, SHORT_LENGTH * cell)
        base = jnp.where(row == cell, start, base)
        running = running + totals[cell]
    place = jnp.where(usable, rank + base, -1)
    for cell in range(cells):
        slot[0:1, pl.ds(cell * SHORT_LENGTH, SHORT_LENGTH)] = place[cell : cell + 1, :]
    meta[0] = kind[0]
    for cell in range(cells):
        meta[1 + cell] = jnp.where(is_long, running if cell == 0 else 0, totals[cell])

    for block in range(length // KEY_BLOCK):
        rows = pl.ds(block * KEY_BLOCK, KEY_BLOCK)
        tokens_t[:, rows] = tokens[rows, :].T
        cell = block * KEY_BLOCK // SHORT_LENGTH
        inside = block * KEY_BLOCK - cell * SHORT_LENGTH
        needed = jnp.where(is_long, block * KEY_BLOCK < running, inside < totals[cell])

        @pl.when(needed)
        def _(block=block, rows=rows):
            hot = one_hot(slot, block * KEY_BLOCK, KEY_BLOCK)
            packed[rows, :] = mm(hot, tokens[...], NN).astype(BF)


def one_hot(slot, begin, rows):
    shape = (rows, slot.shape[1])
    hit = (iota(shape, 0) + begin) == slot[0:1, :]
    return jnp.where(hit, 1.0, 0.0).astype(BF)


def prep(kind, counts, known, tokens):
    length, width = tokens.shape
    return pl.pallas_call(
        prep_kernel,
        in_specs=[SMEM, SMEM, whole(1, length), whole(length, width)],
        out_specs=[
            whole(width, length),
            whole(length, width),
            whole(1, length),
            SMEM,
        ],
        out_shape=[
            jax.ShapeDtypeStruct((width, length), BF),
            jax.ShapeDtypeStruct((length, width), BF),
            jax.ShapeDtypeStruct((1, length), jnp.int32),
            jax.ShapeDtypeStruct((8,), jnp.int32),
        ],
        compiler_params=params(56),
        cost_estimate=cost(3e9, 12e6),
        name="prep",
    )(kind, counts, known, tokens)


def fetch_rows(pieces, mine, target, sem, kinds=1):
    rows = pieces[0].shape[0]
    copies = []
    for index, piece in enumerate(pieces):
        owner = jnp.bitwise_xor(mine, index)
        place = pl.ds(pl.multiple_of(owner * rows, rows), rows)
        if kinds == 1:
            copies.append((piece, target.at[place, :]))
            continue
        for pair in range(PAIRS):
            for kind in range(kinds):
                come = piece.at[:, pl.ds(PAIR * (PAIRS * kind + pair), PAIR)]
                copies.append((come, target.at[place, pl.ds(PAIR * (kinds * pair + kind), PAIR)]))
    copies = [pltpu.make_async_copy(*ends, sem.at[index]) for index, ends in enumerate(copies)]
    for copy in copies:
        copy.start()
    for copy in copies:
        copy.wait()


def head_lanes(shape, head):
    lane = iota(shape, 1)
    return (lane >= HDIM * head) & (lane < HDIM * (head + 1))


def spare(head):
    return HDIM * (1 - head)


def key_lanes(block, head, begin, count):
    lane = iota(block.shape, 1) - spare(head)
    row = iota(block.shape, 0) + begin
    bias = jnp.where(row < count, 0.0, MASKED)
    extra = jnp.where(lane == 0, bias, jnp.where((lane > 0) & (lane < 4), 1.0, 0.0))
    return jnp.where(head_lanes(block.shape, head), block.astype(F32), extra).astype(BF)


def split_rows(shift):
    high = shift.astype(BF).astype(F32)
    rest = shift - high
    mid = rest.astype(BF).astype(F32)
    low = rest - mid
    shape = (16, shift.shape[1])
    row = iota(shape, 0)
    out = jnp.where(row == 0, 1.0, 0.0)
    out = jnp.where(row == 1, -high, out)
    out = jnp.where(row == 2, -mid, out)
    return jnp.where(row == 3, -low, out).astype(BF)


def query_side(target, head, rows, shift):
    other = spare(head)
    target[head, HDIM * head : HDIM * (head + 1), :] = rows
    target[head, other : other + 16, :] = split_rows(shift)
    target[head, other + 16 : other + HDIM, :] = jnp.zeros((HDIM - 16, rows.shape[1]), BF)


def walk(meta, length, body, size, tails, joined=0):
    @pl.when(meta[0] == 1)
    def _():
        cell_walk(meta[1], 0, 0, length, body, size, tails, joined)

    @pl.when(meta[0] != 1)
    def _():
        @pl.loop(0, length // SHORT_LENGTH)
        def _(cell):
            begin = pl.multiple_of(cell * SHORT_LENGTH, SHORT_LENGTH)
            cell_walk(meta[1 + cell], begin, begin, SHORT_LENGTH, body, min(size, SHORT_LENGTH), tails)


def cell_walk(count, slot_begin, query_begin, queries, body, size, tails, joined=0):
    tails = [tail for tail in tails if tail < size]
    rest = lax.rem(count, size)
    full = count // size + jnp.where(rest > (tails or [0])[-1], 1, 0)
    end = slot_begin + count
    together = (rest > 0) & (rest <= joined) & (full > 0)
    blocks = full - jnp.where(together, 1, 0)

    @pl.loop(0, blocks)
    def _(index):
        begin = pl.multiple_of(slot_begin + index * size, size)
        body(begin, size, query_begin, queries, end)

    last = pl.multiple_of(slot_begin + blocks * size, size)
    for low, tail in zip([0] + tails, tails):

        @pl.when((rest > low) & (rest <= tail) & jnp.logical_not(together))
        def _(tail=tail):
            body(last, tail, query_begin, queries, end)

    if joined:

        @pl.when(together)
        def _():
            body(last, size + joined, query_begin, queries, end)


def forward_kernel(count, mine, meta, *refs):
    pieces = refs[:count]
    tokens_t, packed, slot = refs[count : count + 3]
    q_out, k_out, v_out, kc_out, kct_out, vct_out, context, log_total = refs[count + 3 : count + 11]
    weights, kept_all, turned_all, vct, side, total, shift, sem = refs[count + 11 :]
    step = pl.program_id(0)
    width, length = tokens_t.shape

    @pl.when(step == 0)
    def _():
        fetch_rows(pieces, mine[0], weights, sem)

        def project(begin, rows, *_):
            place = pl.ds(begin, rows)
            both = mm(packed[place, :], weights[:, width:], NN)
            kept_all[place, :] = both[:, :width].astype(BF)
            turned_all[:, place] = both.T.astype(BF)

        walk(meta, length, project, *FORWARD_WALK)

    def here(kind):
        return pl.ds(pl.multiple_of(kind * width + step * PAIR, PAIR), PAIR)

    part = jnp.concatenate([weights[:, here(kind)] for kind in range(3)], axis=1)
    joined = mm(part, tokens_t[...], TN)
    q_out[...] = (joined[:PAIR] * HDIM**-0.5).astype(BF)
    k_out[...] = joined[PAIR : 2 * PAIR].astype(BF)
    v_out[...] = joined[2 * PAIR :].astype(BF)
    kc_out[...] = kept_all[:, here(0)]
    kct_out[...] = turned_all[here(0), :]
    vct_out[...] = turned_all[here(1), :]
    ones = jnp.where(iota((16, length), 0) == 0, 1.0, 0.0).astype(BF)
    for head in range(2):
        vct[head, :HDIM, :] = vct_out[HDIM * head : HDIM * (head + 1), :]
        vct[head, HDIM:, :] = ones

    masked = slot[...] < 0
    own = []
    for head in range(2):
        rows = slice(HDIM * head, HDIM * (head + 1))
        queries = q_out[rows, :].astype(F32)
        keys = k_out[rows, :].astype(F32)
        own.append(jnp.where(masked, jnp.sum(queries * keys, axis=0, keepdims=True), MASKED))
        top_q = jnp.max(jnp.sum(queries * queries, axis=0, keepdims=True))
        top_k = jnp.max(jnp.sum(keys * keys, axis=0, keepdims=True))
        unsafe = jnp.logical_not(top_q * top_k < SAFE_SCORE * SAFE_SCORE)
        shift[head : head + 1, :] = jnp.zeros((1, length), F32)
        query_side(side, head, q_out[rows, :], jnp.zeros((1, length), F32))

        @pl.when(unsafe)
        def _(head=head, rows=rows):
            shift[head : head + 1, :] = own[head]

            def raise_top(begin, rows, first, queries, end):
                keys = key_lanes(kc_out[pl.ds(begin, rows), :], head, begin, end)
                place = pl.ds(first, queries)
                scores = mm(keys, side[head, :, place], NN)
                top = jnp.max(scores, axis=0, keepdims=True)
                shift[head : head + 1, place] = jnp.maximum(shift[head : head + 1, place], top)

            walk(meta, length, raise_top, 128, ())
            query_side(side, head, q_out[rows, :], shift[head : head + 1, :])

    total[...] = jnp.zeros(total.shape, F32)

    def attend(begin, rows, first, queries, end):
        slots = pl.ds(begin, rows)
        place = pl.ds(first, queries)
        for head in range(2):
            keys = key_lanes(kc_out[slots, :], head, begin, end)
            raised = jnp.exp(mm(keys, side[head, :, place], NN)).astype(BF)
            total[head, :, place] += mm(vct[head, :, slots], raised, NN)

    walk(meta, length, attend, *FORWARD_WALK, 128)

    for head in range(2):
        rows = slice(HDIM * head, HDIM * (head + 1))
        alone = jnp.exp(own[head] - shift[head : head + 1, :])
        row_total = total[head, HDIM : HDIM + 1, :] + alone
        gathered = total[head, :HDIM, :] + v_out[rows, :].astype(F32) * alone
        context[rows, :] = (gathered * (1.0 / row_total)).astype(BF)
        log_total[pl.ds(step * 2 + head, 1), :] = shift[head : head + 1, :] + jnp.log(row_total)


def forward(mine, meta, pieces, tokens_t, packed, slot):
    width, length = tokens_t.shape
    pair_rows = pl.BlockSpec((PAIR, length), lambda step: (step, 0))
    pair_lanes = pl.BlockSpec((length, PAIR), lambda step: (0, step))
    transposed = jax.ShapeDtypeStruct((width, length), BF)
    natural = jax.ShapeDtypeStruct((length, width), BF)
    count = len(pieces)
    return pl.pallas_call(
        partial(forward_kernel, count),
        grid=(PAIRS,),
        in_specs=[SMEM, SMEM]
        + [ANY] * count
        + [whole(width, length), whole(length, width), whole(1, length)],
        out_specs=[pair_rows] * 3 + [pair_lanes] + [pair_rows] * 3 + [whole(HEADS, length)],
        out_shape=[transposed] * 3
        + [natural]
        + [transposed] * 3
        + [jax.ShapeDtypeStruct((HEADS, length), F32)],
        scratch_shapes=[
            pltpu.VMEM((width, 3 * width), BF),
            pltpu.VMEM((length, width), BF),
            pltpu.VMEM((2 * width, length), BF),
            pltpu.VMEM((2, HDIM + 16, length), BF),
            pltpu.VMEM((2, PAIR, length), BF),
            pltpu.VMEM((2, HDIM + 16, length), F32),
            pltpu.VMEM((8, length), F32),
            pltpu.SemaphoreType.DMA((count,)),
        ],
        compiler_params=params(56),
        cost_estimate=cost(15e9, 25e6, 20e6),
        name="attend_forward",
    )(mine, meta, *pieces, tokens_t, packed, slot)


def backward_kernel(owners, pair_ref, mine, meta, *refs):
    pair = pair_ref[0]
    q_t, kc, kct, vct, grad_context, log_total, inner, slot, k_far, v_far, tokens_far = refs[:11]
    before = refs[11:-14][:2] if len(refs) == 28 else ()
    grad_far, keep, send = refs[-14:-11]
    turned_side, q_side, g_side, grad_q, grad_kv, ready, k_t, v_t, tokens_t, grad_t, sem = refs[-11:]
    length = q_t.shape[1]
    rows = pl.ds(pl.multiple_of(PAIR * pair, PAIR), PAIR)
    come = [
        pltpu.make_async_copy(k_far.at[rows, :], k_t, sem.at[0]),
        pltpu.make_async_copy(v_far.at[rows, :], v_t, sem.at[1]),
        pltpu.make_async_copy(tokens_far, tokens_t, sem.at[2]),
    ]
    for index, (part, target) in enumerate(zip(before, (keep, send))):
        target = target.at[:, pl.ds(0, part.shape[1])]
        come.append(pltpu.make_async_copy(part, target, sem.at[4 + index]))
    for copy in come:
        copy.start()

    for head in range(2):
        lanes = slice(HDIM * head, HDIM * (head + 1))
        index = 2 * pair + head
        query_side(turned_side, head, q_t[lanes, :], log_total[pl.ds(index, 1), :])
        q_side[head] = turned_side[head].T
        query_side(turned_side, head, grad_context[lanes, :], inner[pl.ds(index, 1), :])
        g_side[head] = turned_side[head].T
    grad_q[...] = jnp.zeros(grad_q.shape, F32)
    grad_kv[...] = jnp.zeros(grad_kv.shape, F32)
    ready[...] = jnp.zeros(ready.shape, BF)

    def pull(begin, count, first, queries, end):
        slots = pl.ds(begin, count)
        place = pl.ds(first, queries)
        keys = kc[slots, :]
        for head in range(2):
            lanes = slice(HDIM * head, HDIM * (head + 1))
            key_rows = key_side(kct[lanes, slots], head, begin, end)
            value_rows = key_side(vct[lanes, slots], head, begin, None)
            probs = jnp.exp(mm(q_side[head, place, :], key_rows, NN))
            pulled = mm(g_side[head, place, :], value_rows, NN)
            grad_scores = (probs * pulled).astype(BF)
            own_keys = jnp.where(head_lanes(keys.shape, head), keys.astype(F32), 0.0).astype(BF)
            grad_q[place, :] += mm(grad_scores, own_keys, NN)
            ready[lanes, slots] = mm(q_t[lanes, place], grad_scores, NN).astype(BF)
            ready[PAIR + HDIM * head : PAIR + HDIM * (head + 1), slots] = mm(
                grad_context[lanes, place], probs.astype(BF), NN
            ).astype(BF)

    walk(meta, length, pull, *BACKWARD_WALK)

    def scatter(begin, count, first, queries, end):
        slots = pl.ds(begin, count)
        place = pl.ds(first, queries)
        hit = (iota((count, queries), 0) + begin) == slot[0:1, place]
        spread = jnp.where(hit, 1.0, 0.0).astype(BF)
        grad_kv[:, place] += mm(ready[:, slots], spread, NN)

    walk(meta, length, scatter, 512, (256,))

    for copy in come:
        copy.wait()
    masked = slot[...] < 0
    turned = grad_q[...].T
    for head in range(2):
        lanes = slice(HDIM * head, HDIM * (head + 1))
        index = 2 * pair + head
        queries = q_t[lanes, :].astype(F32)
        keys = k_t[lanes, :].astype(F32)
        values = v_t[lanes, :].astype(F32)
        grads = grad_context[lanes, :].astype(F32)
        own = jnp.sum(queries * keys, axis=0, keepdims=True)
        own = jnp.where(masked, own - log_total[pl.ds(index, 1), :], MASKED)
        alone = jnp.exp(own)
        pulled = jnp.sum(grads * values, axis=0, keepdims=True) - inner[pl.ds(index, 1), :]
        pulled = (alone * pulled).astype(BF).astype(F32)
        alone = alone.astype(BF).astype(F32)
        part = (turned[lanes, :] + keys * pulled) * HDIM**-0.5
        grad_t[HDIM * head : HDIM * (head + 1), :] = part.astype(BF)
        part = grad_kv[lanes, :] + queries * pulled
        grad_t[PAIR + HDIM * head : PAIR + HDIM * (head + 1), :] = part.astype(BF)
        part = grad_kv[PAIR + HDIM * head : PAIR + HDIM * (head + 1), :] + grads * alone
        grad_t[2 * PAIR + HDIM * head : 2 * PAIR + HDIM * (head + 1), :] = part.astype(BF)
    mine_rows = pl.ds(pl.multiple_of(3 * PAIR * pair, 3 * PAIR), 3 * PAIR)
    leave = pltpu.make_async_copy(grad_t, grad_far.at[mine_rows, :], sem.at[3])
    leave.start()
    take_apart([mm(tokens_t[...], grad_t[...], NT)], mine[0], keep, send, owners)
    leave.wait()


def key_side(rows, head, begin, end):
    shape = (16, rows.shape[1])
    row = iota(shape, 0)
    extra = jnp.where((row > 0) & (row < 4), 1.0, 0.0)
    if end is not None:
        bias = jnp.where(iota(shape, 1) + begin < end, 0.0, MASKED)
        extra = jnp.where(row == 0, bias, extra)
    blank = jnp.zeros((HDIM - 16, rows.shape[1]), BF)
    extra = [extra.astype(BF), blank]
    return jnp.concatenate([rows] + extra if head == 0 else extra + [rows], axis=0)


def backward(
    pair, mine, owners, before, into, meta, q_t, k_t, v_t, kc, kct, vct, grad_context, log_total, inner,
    slot, tokens_t,
):
    more = [*before] + [part for part in (into,) if part is not None]
    width, length = tokens_t.shape
    pair_rows = pl.BlockSpec((PAIR, length), lambda step, place: (place[0], 0))
    pair_lanes = pl.BlockSpec((length, PAIR), lambda step, place: (0, place[0]))
    columns = 3 * PAIR + (before[0].shape[1] if before else 0)
    half = jax.ShapeDtypeStruct((width // 2, columns), BF)
    return pl.pallas_call(
        partial(backward_kernel, owners),
        grid_spec=pltpu.PrefetchScalarGridSpec(
            num_scalar_prefetch=1,
            grid=(1,),
            in_specs=[SMEM, SMEM, pair_rows, pair_lanes]
            + [pair_rows] * 3
            + [whole(HEADS, length)] * 2
            + [whole(1, length)]
            + [ANY] * (3 + len(more)),
            out_specs=[ANY] + [whole(*half.shape)] * 2,
            scratch_shapes=[
                pltpu.VMEM((2, PAIR, length), BF),
                pltpu.VMEM((2, length, PAIR), BF),
                pltpu.VMEM((2, length, PAIR), BF),
                pltpu.VMEM((length, PAIR), F32),
                pltpu.VMEM((2 * PAIR, length), F32),
                pltpu.VMEM((2 * PAIR, length), BF),
                pltpu.VMEM((PAIR, length), BF),
                pltpu.VMEM((PAIR, length), BF),
                pltpu.VMEM((width, length), BF),
                pltpu.VMEM((3 * PAIR, length), BF),
                pltpu.SemaphoreType.DMA((6,)),
            ],
        ),
        out_shape=[jax.ShapeDtypeStruct((3 * width, length), BF), half, half],
        input_output_aliases={} if into is None else {13 + len(more): 0},
        compiler_params=params(48),
        cost_estimate=cost(12e9, 10e6, 6e6),
        name="attend_backward",
    )(
        jnp.full((1,), pair, jnp.int32), mine, meta, q_t, kc, kct, vct, grad_context, log_total,
        inner, slot, k_t, v_t, tokens_t, *more,
    )


def feature_mean(values):
    return jnp.sum(values, axis=0, keepdims=True) * (1.0 / values.shape[0])


def normalise(values):
    centred = values - feature_mean(values)
    scale = lax.rsqrt(feature_mean(centred * centred) + NORM_EPS)
    return centred * scale, scale


def pull_norm(grad, scaled, scale, gain):
    lifted = grad * gain
    return scale * (lifted - feature_mean(lifted) - scaled * feature_mean(lifted * scaled))


def lane_sums(values):
    width = 128
    out = values[:, :width]
    for begin in range(width, values.shape[1], width):
        out = out + values[:, begin : begin + width]
    return out


def dense_kernel(count, mine, kind, study, *refs):
    pieces = refs[:count]
    tokens_t, context, cot_far = refs[count : count + 3]
    out, grad_context, grad_first, inner, keep, send, small = refs[count + 3 : count + 10]
    weights, total, norm_total, firsts, sem = refs[count + 10 :]
    step = pl.program_id(0)
    width = tokens_t.shape[0]

    @pl.when(step == 0)
    def _():
        fetch_rows(pieces, mine[0], weights, sem)
        total[...] = jnp.zeros(total.shape, F32)
        norm_total[...] = jnp.zeros(norm_total.shape, F32)

    proj = weights[:, :width]
    up = weights[:, width : 2 * width]
    down = weights[:, 2 * width : 3 * width]
    rows = weights[:, 3 * width :].astype(F32)
    gain1, bias1, gain2, bias2 = (rows[:, index : index + 1] for index in range(4))

    def part(place):
        context_low = context[:, place]
        first_sum = tokens_t[:, place].astype(F32) + mm(proj, context_low, TN)
        yield
        scaled1, scale1 = normalise(first_sum)
        middle = scaled1 * gain1 + bias1
        middle_low = middle.astype(BF)
        hidden = mm(up, middle_low, TN)
        yield
        cdf = 0.5 * (1.0 + lax.erf(hidden * 2.0**-0.5))
        slope = cdf + hidden * jnp.exp(hidden * hidden * -0.5) * 0.3989422804014327
        active = (hidden * cdf).astype(BF)
        second_sum = middle + mm(down, active, TN)
        yield
        scaled2, scale2 = normalise(second_sum)
        result = (scaled2 * gain2 + bias2).astype(BF).T
        out[place, :] = result
        if place.start % SHORT_LENGTH == 0:
            cell = 2 * step + place.start // SHORT_LENGTH
            firsts[pl.ds(cell, 1), :] = result[:8].astype(F32)[0:1]
        cot = cot_far[place, :].T.astype(F32)
        norm_total[2] += lane_sums(cot * scaled2)
        norm_total[3] += lane_sums(cot)
        grad_second = pull_norm(cot, scaled2, scale2, gain2)
        grad_low = grad_second.astype(BF)
        pulled = mm(down, grad_low, NN)
        total[2] += mm(active, grad_low, NT)
        yield
        grad_hidden = (pulled * slope).astype(BF)
        grad_middle = grad_second + mm(up, grad_hidden, NN)
        total[1] += mm(middle_low, grad_hidden, NT)
        yield
        norm_total[0] += lane_sums(grad_middle * scaled1)
        norm_total[1] += lane_sums(grad_middle)
        grad_h1 = pull_norm(grad_middle, scaled1, scale1, gain1)
        proj_low = grad_h1.astype(BF)
        grad_first[:, place] = proj_low
        pulled = mm(proj, proj_low, NN)
        total[0] += mm(context_low, proj_low, NT)
        yield
        pulled = pulled.astype(BF)
        grad_context[:, place] = pulled
        both = pulled.astype(F32) * context_low.astype(F32)
        for head in range(HEADS):
            part = both[HDIM * head : HDIM * (head + 1), :]
            inner[head : head + 1, place] = jnp.sum(part, axis=0, keepdims=True)

    columns = tokens_t.shape[1] // 4
    parts = [part(slice(columns * index, columns * (index + 1))) for index in range(4)]
    turn = 0
    while parts:
        parts = [stage for index, stage in enumerate(parts) if next(stage, stage) is None]
        turn += 1

    @pl.when(step == pl.num_programs(0) - 1)
    def _():
        take_apart([total.at[index] for index in range(3)], mine[0], keep, send, count)
        lane = iota((width, 128), 1)
        packed = jnp.zeros((width, 128), F32)
        for index in range(4):
            column = jnp.sum(norm_total[index], axis=1, keepdims=True)
            packed = jnp.where(lane == index, column, packed)
        row = iota((STUDY_COUNT, width), 0)
        sums = [jnp.zeros((STUDY_COUNT, width), F32)] * 3
        for cell in range(firsts.shape[0]):
            hit = (row == study[cell]) & ((kind[0] == 0) | (cell == 0))
            first = firsts[cell : cell + 1, :]
            for index, term in enumerate((1.0, first, first * first)):
                sums[index] = sums[index] + jnp.where(hit, term, 0.0)
        for index in range(3):
            small[STUDY_COUNT * index : STUDY_COUNT * (index + 1), :] = sums[index]
        small[3 * STUDY_COUNT :, :] = packed.T[:8]


def take_apart(totals, mine, keep, send, owners):
    first = lax.rem(mine, 2) == 0
    at = keep.shape[1] - sum(total.shape[1] for total in totals)
    for total in totals:
        rows, columns = total.shape[0] // owners, total.shape[1]
        for half in range(owners // 2):
            even = total[2 * half * rows : (2 * half + 1) * rows, :].astype(BF)
            odd = total[(2 * half + 1) * rows : (2 * half + 2) * rows, :].astype(BF)
            here = slice(half * rows, (half + 1) * rows)
            keep[here, at : at + columns] = jnp.where(first, even, odd)
            send[here, at : at + columns] = jnp.where(first, odd, even)
        at += columns


def dense(mine, kind, study, pieces, tokens_t, context, cot):
    width, length = tokens_t.shape
    block = 2 * SHORT_LENGTH
    count = len(pieces)
    columns = pl.BlockSpec((width, block), lambda step: (0, step))
    rows = pl.BlockSpec((block, width), lambda step: (step, 0))
    return pl.pallas_call(
        partial(dense_kernel, count),
        grid=(length // block,),
        in_specs=[SMEM] * 3 + [ANY] * count + [columns, columns, rows],
        out_specs=[
            rows,
            columns,
            columns,
            pl.BlockSpec((HEADS, block), lambda step: (0, step)),
            whole(width // 2, 3 * width),
            whole(width // 2, 3 * width),
            whole(4 * STUDY_COUNT, width),
        ],
        out_shape=[
            jax.ShapeDtypeStruct((length, width), BF),
            jax.ShapeDtypeStruct((width, length), BF),
            jax.ShapeDtypeStruct((width, length), BF),
            jax.ShapeDtypeStruct((HEADS, length), F32),
            jax.ShapeDtypeStruct((width // 2, 3 * width), BF),
            jax.ShapeDtypeStruct((width // 2, 3 * width), BF),
            jax.ShapeDtypeStruct((4 * STUDY_COUNT, width), F32),
        ],
        scratch_shapes=[
            pltpu.VMEM((width, 3 * width + 128), BF),
            pltpu.VMEM((3, width, width), F32),
            pltpu.VMEM((4, width, 128), F32),
            pltpu.VMEM((length // SHORT_LENGTH, width), F32),
            pltpu.SemaphoreType.DMA((count,)),
        ],
        compiler_params=params(48),
        cost_estimate=cost(10e9, 20e6, 4e6),
        name="dense",
    )(mine, kind, study, *pieces, tokens_t, context, cot)


def input_kernel(count, mine, *refs):
    pieces = refs[:count]
    grads, grad_first = refs[count : count + 2]
    out, weights, sem = refs[-3:]

    @pl.when(pl.program_id(0) == 0)
    def _():
        fetch_rows(pieces, mine[0], weights, sem, 3)

    total = grad_first[...].T.astype(F32)
    total = total + mm(grads[...], weights[...], (((0,), (1,)), ((), ())))
    out[...] = total.astype(BF)


def input_side(mine, pieces, grads, grad_first, into=None):
    width, length = grad_first.shape
    block = 512
    count = len(pieces)
    steps = length // block // 2
    begin = 0 if into is None else steps
    kept = [] if into is None else [into]
    return pl.pallas_call(
        partial(input_kernel, count),
        grid=(steps,),
        in_specs=[SMEM]
        + [ANY] * count
        + [pl.BlockSpec((3 * width, block), lambda step: (0, step + begin))]
        + [pl.BlockSpec((width, block), lambda step: (0, step + begin))]
        + [ANY] * len(kept),
        out_specs=pl.BlockSpec((block, width), lambda step: (step + begin, 0)),
        out_shape=jax.ShapeDtypeStruct((length, width), BF),
        scratch_shapes=[
            pltpu.VMEM((width, 3 * width), BF),
            pltpu.SemaphoreType.DMA((3 * PAIRS * count,)),
        ],
        compiler_params=params(40),
        cost_estimate=cost(3.3e9, 14e6),
        name="input_side",
        input_output_aliases={} if into is None else {3 + count: 0},
    )(mine, *pieces, grads, grad_first, *kept)


def swap(value, axis, size, mask):
    return lax.ppermute(value, axis, [(index, index ^ mask) for index in range(size)])


def masks_of(size):
    return [1 << bit for bit in range(size.bit_length() - 1)]


def gather_direct(piece, axis, size):
    return [piece] + [swap(piece, axis, size, mask) for mask in range(1, size)]


def halving(keep, send, axis, size):
    mine = lax.axis_index(axis)
    rows = 2 * keep.shape[0] // size
    got = yield send, axis, size, 1
    value = (keep.astype(F32) + got.astype(F32)).astype(BF).reshape(size // 2, rows, -1)
    for bit, mask in list(enumerate(masks_of(size)))[1:]:
        value = value.reshape(value.shape[0] // 2, 2, rows, -1).swapaxes(0, 1)
        side = (mine >> bit) & 1
        send = lax.dynamic_index_in_dim(value, 1 - side, 0, keepdims=False)
        got = yield send, axis, size, mask
        keep = lax.dynamic_index_in_dim(value, side, 0, keepdims=False)
        value = (keep.astype(F32) + got.astype(F32)).astype(value.dtype)
    return value.reshape(rows, -1)


def doubling(value, axis, size):
    for mask in masks_of(size):
        got = yield value, axis, size, mask
        value = (value.astype(F32) + got.astype(F32)).astype(value.dtype)
    return value


def side_steps(keep, send, fsdp, dp):
    value = yield from halving(keep, send, "fsdp", fsdp)
    return (yield from doubling(value, "dp", dp))


def small_steps(value, fsdp, dp):
    value = yield from doubling(value, "fsdp", fsdp)
    return (yield from doubling(value, "dp", dp))


class Chain:
    def __init__(self, steps):
        self.steps, self.result, self.got = steps, None, None
        self.request = next(steps)

    def send(self, value):
        _, axis, size, mask = self.request
        self.got = swap(value, axis, size, mask)

    def land(self, value):
        try:
            self.request = self.steps.send(value)
        except StopIteration as end:
            self.request, self.result = None, end.value

    def finish(self):
        while self.request is not None:
            if self.got is None:
                self.send(self.request[0])
            value, self.got = self.got, None
            self.land(value)
        return self.result


def start_steps(anchor, chains):
    live = [chain for chain in chains if chain.request is not None]
    anchor, *values = lax.optimization_barrier((anchor, *(chain.request[0] for chain in live)))
    for chain, value in zip(live, values):
        chain.send(value)
    return anchor


def end_steps(anchor, chains):
    live = [chain for chain in chains if chain.got is not None]
    anchor, values = lax.optimization_barrier((anchor, [chain.got for chain in live]))
    for chain, value in zip(live, values):
        chain.got = None
        chain.land(value)
    return anchor


def spread_kernel(parts, out):
    total = jnp.sum(parts[...].astype(F32), axis=0).astype(BF)
    for index in range(out.shape[0]):
        out[index] = total


def spread_sums(parts):
    return pl.pallas_call(
        spread_kernel,
        out_shape=jax.ShapeDtypeStruct(parts.shape, BF),
        cost_estimate=cost(1e6, 1e6),
        name="spread",
    )(parts)


def moments(gradient, first_old, second_old):
    first_new = BETA * first_old + (1.0 - BETA) * gradient
    second_new = BETA * second_old + (1.0 - BETA) * gradient * gradient
    return first_new, second_new


def update_of(first_new, second_new):
    debias = 1.0 - BETA**STEP
    return first_new / debias / (jnp.sqrt(second_new / debias) + ADAM_EPS)


def square_row(values):
    total = jnp.sum(values * values, axis=0, keepdims=True)
    return lane_sums(total)


def moments_kernel(count, paired, gradient, *refs):
    olds, outs, squares = refs[: 3 * count], refs[3 * count : 6 * count], refs[6 * count]
    at = 0

    @pl.when(pl.program_id(0) == 0)
    def _():
        squares[...] = jnp.zeros(squares.shape, F32)

    for index in range(count):
        weight, first_old, second_old = (ref[...] for ref in olds[3 * index : 3 * index + 3])
        columns = weight.shape[1]
        if paired:
            places = [
                3 * PAIR * (PAIRS - 1 - pair) + PAIR * kind
                for kind in range(3)
                for pair in range(PAIRS)
            ]
            grad = jnp.concatenate([gradient[:, at : at + PAIR] for at in places], axis=1)
        else:
            grad = gradient[:, at : at + columns]
        grad = grad.astype(F32)
        at += columns
        first_new, second_new = moments(grad, first_old, second_old)
        update = update_of(first_new, second_new) + MATRIX_DECAY * weight
        for place, value in enumerate((first_new, second_new, update)):
            outs[3 * index + place][...] = value
        squares[index : index + 1, :] += square_row(weight)
        squares[4 + index : 5 + index, :] += square_row(update)


def row_blocks(arrays):
    rows = arrays[0].shape[0]
    steps = rows // 32 if rows % 32 == 0 else 1
    return steps, [
        pl.BlockSpec((rows // steps, array.shape[1]), lambda step: (step, 0)) for array in arrays
    ]


def new_moments(gradient, olds, paired):
    count = len(olds) // 3
    outs = [jax.ShapeDtypeStruct(old.shape, F32) for old in olds]
    steps, in_specs = row_blocks((gradient, *olds))
    results = pl.pallas_call(
        partial(moments_kernel, count, paired),
        grid=(steps,),
        in_specs=in_specs,
        out_specs=row_blocks(outs)[1] + [whole(8, 128)],
        out_shape=outs + [jax.ShapeDtypeStruct((8, 128), F32)],
        compiler_params=params(32 if paired else 60),
        cost_estimate=cost(5e6, 5e6),
        name="moments",
    )(gradient, *olds)
    return results[:-1], results[-1]


def apply_kernel(count, squares, *refs):
    inputs, outs, norms = refs[: 2 * count], refs[2 * count : 4 * count], refs[4 * count]
    total = jnp.sum(jnp.sum(squares[...], axis=0), axis=1, keepdims=True)
    size = jnp.sqrt(total)
    ratio = size[0:4] / size[4:8]
    lane = iota((1, 4), 1)
    rows = [jnp.zeros((1, 4), F32)] * 3
    for index in range(count):
        weight, update = inputs[2 * index][...], inputs[2 * index + 1][...]
        trust = ratio[index : index + 1]
        weight = weight - MATRIX_RATE * trust * update
        outs[2 * index][...] = weight
        outs[2 * index + 1][...] = weight.astype(BF)
        for place, value in enumerate((size[index : index + 1], size[4 + index : 5 + index], trust)):
            rows[place] = jnp.where(lane == index, value, rows[place])
    for place in range(3):
        norms[place : place + 1, :] = rows[place]


def apply_updates(squares, arrays):
    count = len(arrays) // 2
    outs = []
    for weight in arrays[::2]:
        outs += [jax.ShapeDtypeStruct(weight.shape, F32), jax.ShapeDtypeStruct(weight.shape, BF)]
    steps, in_specs = row_blocks(arrays)
    results = pl.pallas_call(
        partial(apply_kernel, count),
        grid=(steps,),
        in_specs=[whole(*squares.shape)] + in_specs,
        out_specs=row_blocks(outs)[1] + [whole(3, 4)],
        out_shape=outs + [jax.ShapeDtypeStruct((3, 4), F32)],
        compiler_params=params(32),
        cost_estimate=cost(5e6, 8e6),
        name="apply",
    )(squares, *arrays)
    return results[:-1], results[-1]


def shards(
    fsdp,
    dp,
    tokens,
    cotangent,
    known_genes,
    cell_kind,
    gene_counts,
    study_index,
    qkv_weight,
    qkv_first,
    qkv_second,
    proj_weight,
    proj_first,
    proj_second,
    up_weight,
    up_first,
    up_second,
    down_weight,
    down_first,
    down_second,
    norm_params,
    norm_first,
    norm_second,
):
    _, length, width = tokens.shape
    mine = lax.axis_index("fsdp").astype(jnp.int32)
    mine_ref = mine.reshape(1)

    tokens_t, packed, slot, meta = prep(
        cell_kind, gene_counts.reshape(-1), known_genes, tokens[0]
    )
    norm_columns = jnp.pad(norm_params.T, ((0, 0), (0, 124)))
    rest = jnp.concatenate([proj_weight, up_weight, down_weight, norm_columns], axis=1).astype(BF)
    own = qkv_weight.astype(BF)
    core, *far_masks = masks_of(fsdp)
    far = {0: own}
    for mask in reversed(far_masks):
        far.update({known ^ mask: swap(far[known], "fsdp", fsdp, mask) for known in far})
    names = sorted(far)[1:]
    slot, *values = lax.optimization_barrier((slot, *(far[name] for name in names)))
    far.update(zip(names, values))
    pieces = dict(far)
    pieces.update({known ^ core: swap(far[known], "fsdp", fsdp, core) for known in far})
    rest, far_piece = lax.optimization_barrier((rest, pieces[names[-1]]))
    pieces[names[-1]] = far_piece
    rest_pieces = gather_direct(rest, "fsdp", fsdp)
    qkv_pieces = [pieces[index] for index in range(fsdp)]
    q_t, k_t, v_t, kc, kct, vct, context, log_total = forward(
        mine_ref, meta, qkv_pieces, tokens_t, packed, slot
    )
    *rest_pieces, context = lax.optimization_barrier((*rest_pieces, context))
    out, grad_context, grad_first, inner, keep, send, small = dense(
        mine_ref, cell_kind, study_index.reshape(-1), rest_pieces, tokens_t, context, cotangent[0]
    )
    side_chain = Chain(side_steps(keep, send, fsdp, dp))
    small_chain = Chain(small_steps(small, fsdp, dp))
    meta = start_steps(meta, [side_chain])
    meta = end_steps(meta, [side_chain])
    chains = [side_chain, small_chain]
    half_chains = []
    grads = None
    before = ()
    for pair in reversed(range(PAIRS)):
        meta = start_steps(meta, chains)
        grads, *before = backward(
            pair, mine_ref, fsdp, before, grads, meta, q_t, k_t, v_t, kc, kct, vct, grad_context, log_total,
            inner, slot, tokens_t,
        )
        before = list(end_steps(tuple(before), chains))
        if pair % 2 == 0:
            half_chains.append(Chain(halving(*before, "fsdp", fsdp)))
            chains.append(half_chains[-1])
            before = ()
    late = half_chains[-1:]
    side_share = side_chain.finish()
    mine_ref = start_steps(mine_ref, late)
    mine_ref = end_steps(mine_ref, late)
    mine_ref = start_steps(mine_ref, late + [small_chain])
    input_grad = input_side(mine_ref, qkv_pieces, grads, grad_first)
    input_grad = end_steps(input_grad, late + [small_chain])
    qkv_share = jnp.concatenate([chain.finish() for chain in half_chains], axis=1)
    qkv_share, mine_ref = lax.optimization_barrier((qkv_share, mine_ref))
    rows = qkv_share.shape[0]
    parts = lax.all_to_all(qkv_share, "dp", 0, 0, tiled=True)
    input_grad = input_side(mine_ref, qkv_pieces, grads, grad_first, input_grad)
    parts, input_grad = lax.optimization_barrier((parts, input_grad))
    parts = spread_sums(parts.reshape(dp, rows // dp, -1)).reshape(rows, -1)
    qkv_share = lax.all_to_all(parts, "dp", 0, 0, tiled=True)
    side_share, _ = lax.optimization_barrier((side_share, parts))
    side_old = (proj_weight, proj_first, proj_second, up_weight, up_first, up_second)
    side_old += (down_weight, down_first, down_second)
    side_new, side_squares = new_moments(side_share, side_old, False)
    qkv_share, side_squares = lax.optimization_barrier((qkv_share, side_squares))
    small = small_chain.finish()
    study_mean = small[8:16] / small[:8]
    study_var = small[16:24] / small[:8] - study_mean * study_mean
    norm_share = lax.dynamic_slice_in_dim(small[24:28], mine * (width // fsdp), width // fsdp, 1)
    norm_first, norm_second = moments(norm_share, norm_first, norm_second)
    norm_params = norm_params - VECTOR_RATE * update_of(norm_first, norm_second)

    (qkv_first, qkv_second, qkv_update), qkv_squares = new_moments(
        qkv_share, (qkv_weight, qkv_first, qkv_second), True
    )
    squares = jnp.concatenate(
        [qkv_squares[0:1], side_squares[0:3], qkv_squares[4:5], side_squares[4:7]], axis=0
    )
    squares = jnp.stack(gather_direct(squares, "fsdp", fsdp))
    arrays = (qkv_weight, qkv_update, proj_weight, side_new[2])
    arrays += (up_weight, side_new[5], down_weight, side_new[8])
    applied, matrix_norms = apply_updates(squares, arrays)
    firsts = (qkv_first, side_new[0], side_new[3], side_new[6])
    seconds = (qkv_second, side_new[1], side_new[4], side_new[7])
    results = []
    for index in range(4):
        results += [firsts[index], seconds[index], applied[2 * index], applied[2 * index + 1]]
    return (
        out.reshape(tokens.shape),
        input_grad.reshape(tokens.shape),
        study_mean,
        study_var,
        *results,
        norm_first,
        norm_second,
        norm_params,
        norm_params.astype(BF),
        matrix_norms,
    )


def solution(mesh):
    whole_groups = P(("dp", "fsdp"))
    rows = P("fsdp", None)
    columns = P(None, "fsdp")
    return jax.shard_map(
        partial(shards, mesh.shape["fsdp"], mesh.shape["dp"]),
        mesh=mesh,
        in_specs=(whole_groups,) * 6 + (rows,) * 12 + (columns,) * 3,
        out_specs=(whole_groups,) * 2 + (P(), P()) + (rows,) * 16 + (columns,) * 4 + (P(),),
        check_vma=False,
    )
```
